32 devices in a mesh: dp: 8 (over y, x, core), tensor: 4 (over z).
Axes of the slice: x: 2, y: 2, z: 4, core: 2. Of those that a mesh axis runs over, the one named last changes fastest.
Arguments:
- inputs: bfloat16 [16384, 1024], P(('dp', 'tensor')), may hold values from -6 to 6
- qkv_weight: bfloat16 [1024, 3072], P('dp', 'tensor'), may hold values from -0.25 to 0.25
- dense_weight: bfloat16 [1024, 1024], P('dp', 'tensor'), may hold values from -3 to 3
- expand_weight: bfloat16 [1024, 4096], P('dp', 'tensor'), may hold values from -0.1875 to 0.1875
- shrink_weight: bfloat16 [1024, 4096], P('dp', 'tensor'), may hold values from -0.09375 to 0.09375
- norm_gains: bfloat16 [2, 1024], P(None, 'dp'), may hold values from 0.5 to 1.5
- norm_biases: bfloat16 [2, 1024], P(None, 'dp'), may hold values from -3 to 3
- cotangent: bfloat16 [16384, 1024], P(('dp', 'tensor')), may hold values from -6 to 6
- segments: int32 [16384], P('dp'), may hold values from 0 to 4, as said below
Outputs:
- layer_out: bfloat16 [16384, 1024], P(('dp', 'tensor'))
- input_grad: float32 [16384, 1024], P(('dp', 'tensor'))
- qkv_grad: float32 [1024, 3072], P('dp', 'tensor')
- dense_grad: float32 [1024, 1024], P('dp', 'tensor')
- expand_grad: float32 [1024, 4096], P('dp', 'tensor')
- shrink_grad: float32 [1024, 4096], P('dp', 'tensor')
- attention_norm_grad: float32 [2, 1024], P(None, 'dp')
- feedforward_norm_grad: float32 [2, 1024], P(None, 'dp')
The draws below stay inside these ranges and needn't reach their ends.
Inputs may be any that keep to these rules, and one draw needn't show every extreme that they name: `segments`: document numbers within each sequence of 2048 tokens never fall; attention joins tokens of one document.
All inputs are finite; a program needn't handle non-finite values.
Results may differ from the reference program's by a relative error of at most 0.013.
The reference program's roundings to bfloat16 on the way count: a program that leaves them out, or rounds other values in their place, can miss the bound.
Values may be sent and summed in bfloat16 or wider, within the bound.
No kernel may reach another device: no remote copies, remote signals or barrier semaphores. Data moves between devices by JAX's collectives and lax.ppermute only.
A program may use at most 192 MiB of HBM per device.

```python
import jax
import jax.numpy as jnp
from jax import lax

D = 1024
H = 16
HD = 64
ROT = 16
FF = 4096
L = 2048
QB = 512
SEQS = 8
TOKENS = 16384


def draw_segments(key, part):
    key = jax.random.fold_in(key, 7)
    key_start, key_end, key_first, key_last = jax.random.split(key, 4)
    quarter = L // 4
    doc_start = jax.random.randint(key_start, (SEQS, 1), 1, quarter)
    doc_end = jax.random.randint(key_end, (SEQS, 1), L - quarter + 1, L)
    first_cut = jax.random.randint(key_first, (SEQS, 1), 1, doc_start + 1)
    last_cut = jax.random.randint(key_last, (SEQS, 1), doc_end, L)
    places = jnp.arange(L, dtype=jnp.int32)[None, :]
    numbers = (places >= first_cut).astype(jnp.int32) + (places >= doc_start).astype(jnp.int32)
    numbers = numbers + (places >= doc_end).astype(jnp.int32) + (places >= last_cut).astype(jnp.int32)
    return numbers.reshape(SEQS * L)


def levels(key, extent, cuts, low, top_value):
    gain = 1.0
    for axis_at, parts in cuts:
        heights = jax.random.uniform(jax.random.fold_in(jax.random.fold_in(key, 6), axis_at), (parts,), jnp.float32, low / len(cuts), top_value / len(cuts))
        gain = gain * jnp.repeat(jnp.exp(heights), extent[axis_at] // parts).reshape((-1,) + (1,) * (len(extent) - 1 - axis_at))
    return gain


def scatter_about(own_key, shape, width, reach, cuts=(), kind=jnp.bfloat16):
    result = width * jax.random.normal(own_key, shape, jnp.float32)
    if cuts:
        result = result * levels(own_key, shape, cuts, -0.22, 0.18)
    return jnp.clip(result, -reach, reach).astype(kind)


def setup_inputs(seed: int = 0) -> dict:
    splits = jax.random.split(jax.random.key(seed), 10)
    return {
        "inputs": scatter_about(splits[0], (TOKENS, D), 1.0, 6.0, ((0, 32),)),
        "qkv_weight": scatter_about(splits[1], (D, 3 * H * HD), (D // 2) ** -0.5, 0.25, ((0, 8), (1, 4))),
        "dense_weight": scatter_about(splits[2], (D, H * HD), (max(H * HD // 256, 2)) ** -0.5, 3.0, ((0, 8), (1, 4))),
        "expand_weight": scatter_about(splits[3], (D, FF), D ** -0.5, 0.1875, ((0, 8), (1, 4))),
        "shrink_weight": scatter_about(splits[4], (D, FF), FF ** -0.5, 0.09375, ((0, 8), (1, 4))),
        "norm_gains": jnp.clip(1.0 + 0.1 * jax.random.normal(splits[5], (2, D), jnp.float32), 0.5, 1.5).astype(jnp.bfloat16),
        "norm_biases": scatter_about(splits[6], (2, D), 0.5, 3.0, ((1, 8),)),
        "cotangent": scatter_about(splits[7], (TOKENS, D), 1.0, 6.0, ((0, 32),)),
        "segments": draw_segments(jax.random.fold_in(splits[9], 71), 0),
    }


@jax.custom_vjp
def low(v):
    return lax.optimization_barrier(v.astype(jnp.bfloat16)).astype(jnp.float32)

@jax.custom_vjp
def low_back(v):
    return v

def low_keep(v):
    return (low(v), None)

def low_pass(kept, grad):
    return (grad,)

def back_keep(v):
    return (v, None)

def back_low(kept, grad):
    return (low(grad),)
low.defvjp(low_keep, low_pass)
low_back.defvjp(back_keep, back_low)
EPSILON = 1e-05
MASKED = -1e+30

def rotary_tables(segments):
    grouped = segments.reshape(-1, L)
    places = jnp.arange(L, dtype=jnp.int32)
    change = jnp.concatenate([jnp.ones((grouped.shape[0], 1), jnp.bool_), grouped[:, 1:] != grouped[:, :-1]], axis=1)
    starts = lax.cummax(jnp.where(change, places[None, :], 0), axis=1)
    position = (places[None, :] - starts).reshape(-1).astype(jnp.float32)
    frequency = 10000.0 ** (-(jnp.arange(ROT // 2, dtype=jnp.float32) * 2.0 / ROT))
    angles = position[:, None] * frequency[None, :]
    angles = jnp.concatenate([angles, angles], axis=1)
    return (jnp.cos(angles), jnp.sin(angles))

def rotate(values, cosine, sine):
    half_rot = ROT // 2
    head_part = values[..., :ROT]
    turned = jnp.concatenate([-head_part[..., half_rot:], head_part[..., :half_rot]], axis=-1)
    return jnp.concatenate([head_part * cosine[:, None, :] + turned * sine[:, None, :], values[..., ROT:]], axis=-1)

def matmul(left, right):
    return jnp.dot(left, right, preferred_element_type=jnp.float32, precision=lax.Precision.HIGHEST)

def attend_sequence(packed):
    queries, key_rows, value_rows, segment = packed
    columns = jnp.arange(L, dtype=jnp.int32)

    @jax.checkpoint
    def attend_block(block_index):
        row_index = block_index * QB + jnp.arange(QB, dtype=jnp.int32)
        query_block = lax.dynamic_slice_in_dim(queries, block_index * QB, QB, 0)
        segment_block = lax.dynamic_slice_in_dim(segment, block_index * QB, QB, 0)
        scores = low_back(jnp.einsum('qhd,khd->hqk', query_block, key_rows, precision=lax.Precision.HIGHEST))
        allowed = (segment_block[:, None] == segment[None, :]) & (columns[None, :] <= row_index[:, None])
        scores = jnp.where(allowed[None], scores, MASKED)
        row_max = lax.optimization_barrier(jnp.max(scores, axis=-1, keepdims=True))
        exponent = jnp.exp(scores - row_max)
        probabilities = exponent / lax.optimization_barrier(jnp.sum(exponent, axis=-1, keepdims=True))
        return jnp.einsum('hqk,khd->qhd', low(probabilities), value_rows, precision=lax.Precision.HIGHEST)
    return lax.map(attend_block, jnp.arange(L // QB, dtype=jnp.int32)).reshape(L, H, HD)

def forward(inputs, qkv_weight, dense_weight, expand_weight, shrink_weight, norm_gains, norm_biases, cosine, sine, segments):
    average = lax.optimization_barrier(jnp.mean(inputs, axis=-1, keepdims=True))
    centered = inputs - average
    normalized = centered * lax.rsqrt(lax.optimization_barrier(jnp.mean(centered * centered, axis=-1, keepdims=True)) + EPSILON)
    first_norm = low(normalized * norm_gains[0] + norm_biases[0])
    second_norm = low(normalized * norm_gains[1] + norm_biases[1])
    projected = low_back(matmul(first_norm, qkv_weight)).reshape(-1, H, 3, HD)
    queries = low(rotate(projected[:, :, 0], cosine, sine) * HD ** (-0.5))
    key_rows = low(rotate(projected[:, :, 1], cosine, sine))
    value_rows = low(projected[:, :, 2])
    attended = lax.map(attend_sequence, (queries.reshape(-1, L, H, HD), key_rows.reshape(-1, L, H, HD), value_rows.reshape(-1, L, H, HD), segments.reshape(-1, L)))
    attended = low(low_back(attended.reshape(-1, H * HD)))
    attn_branch = matmul(attended, dense_weight.T)
    hidden_pre = low_back(matmul(second_norm, expand_weight))
    activated = low(jax.nn.gelu(hidden_pre, approximate=False))
    return inputs + attn_branch + matmul(activated, shrink_weight.T)

def reference(inputs, qkv_weight, dense_weight, expand_weight, shrink_weight, norm_gains, norm_biases, cotangent, segments):
    cosine, sine = rotary_tables(segments)
    floats = tuple((array_item.astype(jnp.float32) for array_item in (inputs, qkv_weight, dense_weight, expand_weight, shrink_weight, norm_gains, norm_biases)))

    def closed(*params):
        return forward(*params, cosine, sine, segments)
    output, pullback = jax.vjp(closed, *floats)
    grads = pullback(cotangent.astype(jnp.float32))
    gain_grads = grads[5]
    bias_grads = grads[6]
    attention_norm_grad = jnp.stack([gain_grads[0], bias_grads[0]])
    feedforward_norm_grad = jnp.stack([gain_grads[1], bias_grads[1]])
    return (output.astype(jnp.bfloat16), grads[0], grads[1], grads[2], grads[3], grads[4], attention_norm_grad, feedforward_norm_grad)
```

```python
from functools import partial

import jax
import jax.numpy as jnp
from jax import lax
from jax.experimental import pallas as pl
from jax.experimental.pallas import tpu as pltpu
from jax.sharding import Mesh
from jax.sharding import PartitionSpec as P

HD = 64
ROT = 16
L = 2048
LANES = 128
EPSILON = 1e-05
MASKED = -1e30
AXES = ("pair", "core", "half", "m")
PIECES = 4
PIECE = L // PIECES
SEG_LANE = 64
DOCS = 5
LSE_LANE = SEG_LANE + DOCS
DELTA_LANE = 64
MIB = 1024 * 1024
F32 = jnp.float32
BF16 = jnp.bfloat16


def dot_nn(left, right):
    return lax.dot_general(left, right, (((1,), (0,)), ((), ())), preferred_element_type=F32)


def dot_nt(left, right):
    return lax.dot_general(left, right, (((1,), (1,)), ((), ())), preferred_element_type=F32)


def dot_tn(left, right):
    return lax.dot_general(left, right, (((0,), (0,)), ((), ())), preferred_element_type=F32)


def lanes_of(shape):
    return lax.broadcasted_iota(jnp.int32, shape, len(shape) - 1)


def rows_of(shape):
    return lax.broadcasted_iota(jnp.int32, shape, len(shape) - 2)


def normalize(x):
    rows = x.astype(F32)
    centered = rows - jnp.mean(rows, axis=-1, keepdims=True)
    return centered * lax.rsqrt(jnp.mean(centered * centered, axis=-1, keepdims=True) + EPSILON)


def split3(column):
    high = column.astype(BF16).astype(F32)
    rest = column - high
    middle = rest.astype(BF16).astype(F32)
    return high, middle, rest - middle


def with_lanes(base, first, columns):
    lane = lanes_of(base.shape)
    for offset, column in enumerate(columns):
        base = jnp.where(lane == first + offset, column, base)
    return base


def params(limit_mib):
    return pltpu.CompilerParams(vmem_limit_bytes=limit_mib * MIB)


def whole(shape, **kw):
    return pl.BlockSpec(shape, lambda *_: (0,) * len(shape), **kw)


def once(shape):
    return whole(shape, pipeline_mode=pl.Buffered(1))


def cost(flops, nbytes, trans=0):
    return pl.CostEstimate(flops=int(flops), bytes_accessed=int(nbytes), transcendentals=int(trans))


def row_offsets(info_ref, pairs, rows):
    core, pair = info_ref[1], info_ref[2]
    for j in range(pairs):
        base = (pair ^ j) * 2
        yield pl.multiple_of((base + core) * rows, rows), pl.multiple_of((base + 1 - core) * rows, rows)


def assemble_first_kernel(pairs, rows, width, info_ref, *refs):
    a_refs, b_refs = refs[:pairs], refs[pairs : 2 * pairs]
    weight_ref, gb_ref, small = refs[2 * pairs :]
    for j, (off_a, off_b) in enumerate(row_offsets(info_ref, pairs, rows)):
        for off, part in ((off_a, a_refs[j]), (off_b, b_refs[j])):
            weight_ref[pl.ds(off, rows), :] = part[:, :width]
            small[pl.ds(off, rows), :] = part[:, width:].astype(F32)
    gb_ref[...] = small[...].T[:8, :]


def assemble_first(info, a_parts, b_parts, width):
    pairs, rows = len(a_parts), a_parts[0].shape[0]
    feats = pairs * 2 * rows
    return pl.pallas_call(
        partial(assemble_first_kernel, pairs, rows, width),
        out_shape=(jax.ShapeDtypeStruct((feats, width), BF16), jax.ShapeDtypeStruct((8, feats), F32)),
        in_specs=[pl.BlockSpec(memory_space=pltpu.SMEM)] + [pl.BlockSpec(memory_space=pltpu.VMEM)] * (2 * pairs),
        scratch_shapes=[pltpu.VMEM((feats, LANES), F32)],
        compiler_params=params(32),
        cost_estimate=cost(0, 4 * feats * width),
        name="assemble_qkv",
    )(info, *a_parts, *b_parts)


def assemble_second_kernel(pairs, rows, widths, info_ref, *refs):
    a_refs, b_refs, outs = refs[:pairs], refs[pairs : 2 * pairs], refs[2 * pairs :]
    for j, (off_a, off_b) in enumerate(row_offsets(info_ref, pairs, rows)):
        for off, part in ((off_a, a_refs[j]), (off_b, b_refs[j])):
            start = 0
            for out, width in zip(outs, widths):
                out[pl.ds(off, rows), :] = part[:, start : start + width]
                start += width


def assemble_second(info, a_parts, b_parts, widths):
    pairs, rows = len(a_parts), a_parts[0].shape[0]
    feats = pairs * 2 * rows
    return pl.pallas_call(
        partial(assemble_second_kernel, pairs, rows, widths),
        out_shape=tuple(jax.ShapeDtypeStruct((feats, w), BF16) for w in widths),
        in_specs=[pl.BlockSpec(memory_space=pltpu.SMEM)] + [pl.BlockSpec(memory_space=pltpu.VMEM)] * (2 * pairs),
        compiler_params=params(32),
        cost_estimate=cost(0, 4 * feats * sum(widths)),
        name="assemble_ffn",
    )(info, *a_parts, *b_parts)


def turn(values, cosine, sine_up, sine_down):
    return (
        values * cosine
        + pltpu.roll(values, ROT // 2, 1) * sine_up
        + pltpu.roll(values, LANES - ROT // 2, 1) * sine_down
    )


def project_kernel(heads, info_ref, x_ref, w_ref, gb_ref, cos_ref, up_ref, down_ref, qf_ref, kf_ref, *refs):
    xs_ref, q_ref, k_ref, v_ref = refs[-4:]
    x = x_ref[...]
    xs_ref[0] = x
    first = (normalize(x) * gb_ref[0:1, :] + gb_ref[2:3, :]).astype(BF16)
    projected = dot_nn(first, w_ref[...])
    cosine, up, down = cos_ref[...], up_ref[...], down_ref[...]
    lane = lanes_of(cosine.shape)
    low = lane < HD
    value_feature = ((lane >= DELTA_LANE) & (lane < DELTA_LANE + 3)).astype(F32)

    def part(offset):
        tile = projected[:, offset // LANES * LANES : offset // LANES * LANES + LANES]
        return pltpu.roll(tile, HD, 1) if offset % LANES else tile

    for h in range(heads):
        sl = slice(h * LANES, (h + 1) * LANES)
        base = h * 3 * HD
        query = turn(part(base), cosine, up, down) * HD ** (-0.5)
        key = turn(part(base + HD), cosine, up, down)
        q_ref[0, :, sl] = jnp.where(low, query, qf_ref[...]).astype(BF16)
        k_ref[0, :, sl] = jnp.where(low, key, kf_ref[...]).astype(BF16)
        v_ref[0, :, sl] = jnp.where(low, part(base + 2 * HD), value_feature).astype(BF16)


def project(r, info, x, weight, gb, tables, stacks, block=256):
    feats, width = weight.shape
    heads = width // (3 * HD)
    steps = PIECE // block
    shapes = [(PIECES, PIECE, feats)] + [(PIECES, PIECE, heads * LANES)] * 3
    table = pl.BlockSpec((block, LANES), lambda i, info: ((info[0] ^ r) * steps + i, 0))
    n_fixed = 9
    return pl.pallas_call(
        partial(project_kernel, heads),
        grid_spec=pltpu.PrefetchScalarGridSpec(
            num_scalar_prefetch=1,
            grid=(steps,),
            in_specs=[
                pl.BlockSpec((block, feats), lambda i, info: (i, 0)),
                once((feats, width)),
                once((8, feats)),
            ]
            + [table] * 5
            + [pl.BlockSpec(memory_space=pl.ANY)] * len(stacks),
            out_specs=[pl.BlockSpec((1, block, s[2]), lambda i, info: (r, i, 0)) for s in shapes],
        ),
        out_shape=[jax.ShapeDtypeStruct(s, BF16) for s in shapes],
        input_output_aliases={n_fixed + n: n for n in range(len(stacks))},
        compiler_params=params(40),
        cost_estimate=cost(2 * PIECE * feats * width, 2 * (feats * width + 4 * PIECE * feats)),
        name=f"project_piece_{r}",
    )(info, x, weight, gb, *tables, *stacks)


def attend_kernel(heads, block, info_ref, q_ref, k_ref, v_ref, o_ref, qb_ref):
    step = pl.program_id(0)
    per = PIECE // block
    me = info_ref[0]

    def run(count):
        row = step % per * block + rows_of((block, PIECE))
        causal = lanes_of((block, PIECE)) <= row
        lane = lanes_of((block, LANES))
        pieces = [me ^ j for j in range(count)]
        held = None
        for h in range(heads):
            sl = slice(h * LANES, (h + 1) * LANES)
            query = q_ref[:, sl]
            scores = [dot_nt(query, k_ref[p, :, sl]) for p in pieces]
            scores[-1] = jnp.where(causal, scores[-1], MASKED)
            top = jnp.max(scores[0], axis=-1, keepdims=True)
            for s in scores[1:]:
                top = jnp.maximum(top, jnp.max(s, axis=-1, keepdims=True))
            weights = [jnp.exp(s - top) for s in scores]
            total = jnp.sum(weights[0], axis=-1, keepdims=True)
            for w in weights[1:]:
                total = total + jnp.sum(w, axis=-1, keepdims=True)
            scale = 1.0 / total
            out = None
            for w, p in zip(weights, pieces):
                term = dot_nn((w * scale).astype(BF16), v_ref[p, :, sl])
                out = term if out is None else out + term
            if h % 2 == 0:
                held = out
            else:
                o_ref[:, (h // 2) * LANES : (h // 2 + 1) * LANES] = jnp.where(
                    lane < HD, held, pltpu.roll(out, HD, 1)
                )
            log_total = split3(top + jnp.log(total))
            qb_ref[:, sl] = with_lanes(query.astype(F32), LSE_LANE, [-c for c in log_total]).astype(BF16)

    for n in range(PIECES):
        pl.when(step // per == n)(partial(run, n + 1))


def attend(info, queries, keys, values, block=256):
    width = queries.shape[2]
    heads = width // LANES
    per = PIECE // block
    rel = lambda i, info: ((info[0] ^ (i // per)) * per + i % per, 0)
    return pl.pallas_call(
        partial(attend_kernel, heads, block),
        grid_spec=pltpu.PrefetchScalarGridSpec(
            num_scalar_prefetch=1,
            grid=(L // block,),
            in_specs=[
                pl.BlockSpec((block, width), rel),
                once((PIECES, PIECE, width)),
                once((PIECES, PIECE, width)),
            ],
            out_specs=[pl.BlockSpec((block, heads * HD), rel), pl.BlockSpec((block, width), rel)],
        ),
        out_shape=[jax.ShapeDtypeStruct((L, heads * HD), F32), jax.ShapeDtypeStruct((L, width), BF16)],
        compiler_params=params(50),
        cost_estimate=cost(heads * L * L * LANES * 4, 5 * L * width, heads * L * L // 2),
        name="attention_forward",
    )(info, queries.reshape(L, width), keys, values)


def gelu_parts(h):
    bell = jnp.exp(h * h * -0.5)
    t = 1.0 / (1.0 + (0.3275911 * 0.5**0.5) * jnp.abs(h))
    poly = t * (
        0.254829592 + t * (-0.284496736 + t * (1.421413741 + t * (-1.453152027 + t * 1.061405429)))
    )
    tail = 0.5 * poly * bell
    return jnp.where(h < 0, tail, 1.0 - tail), bell * 0.3989422804014327


def norm_columns(sums_ref):
    wide = jnp.concatenate([sums_ref[...], jnp.zeros((LANES - 8, sums_ref.shape[1]), F32)], axis=0)
    return wide.T


def write_parts(info_ref, totals, width, small, a_refs, b_refs):
    rows = a_refs[0].shape[0]
    for j, (off_a, off_b) in enumerate(row_offsets(info_ref, len(a_refs), rows)):
        for off, part in ((off_a, a_refs[j]), (off_b, b_refs[j])):
            start = 0
            for total in totals:
                part[:, start : start + total.shape[1]] = total[pl.ds(off, rows), :].astype(BF16)
                start += total.shape[1]
            part[:, width:] = small[pl.ds(off, rows), :].astype(BF16)


def feed_kernel(pairs, heads, info_ref, x_ref, *refs):
    g_refs = refs[:PIECES]
    o_ref, wd_ref, we_ref, ws_ref, gb_ref = refs[PIECES : PIECES + 5]
    outs = refs[PIECES + 5 :]
    br_refs = outs[:PIECES]
    sg_ref, doa_ref = outs[PIECES : PIECES + 2]
    a_refs = outs[PIECES + 2 : PIECES + 2 + pairs]
    b_refs = outs[PIECES + 2 + pairs : PIECES + 2 + 2 * pairs]
    g_now, b_now, gd, ge, gs, sums, small = outs[PIECES + 2 + 2 * pairs :]
    step, last = pl.program_id(0), pl.num_programs(0) - 1
    block = x_ref.shape[0]
    per = PIECE // block

    @pl.when(step == 0)
    def _():
        for total in (gd, ge, gs, sums):
            total[...] = jnp.zeros_like(total)

    place = pl.multiple_of(step % per * block, block)
    for r in range(PIECES):

        @pl.when(step // per == r)
        def _():
            g_now[...] = g_refs[r][pl.ds(place, block), :]

    g = g_now[...]
    normalized = normalize(x_ref[...])
    second = (normalized * gb_ref[1:2, :] + gb_ref[3:4, :]).astype(BF16)
    hidden = dot_nn(second, we_ref[...])
    cdf, density = gelu_parts(hidden)
    activated = (hidden * cdf).astype(BF16)
    slope = cdf + hidden * density
    out = o_ref[...]
    attended = out.astype(BF16)
    b_now[...] = (dot_nt(attended, wd_ref[...]) + dot_nt(activated, ws_ref[...])).astype(BF16)
    hidden_grad = (dot_nn(g, ws_ref[...]) * slope).astype(BF16)
    second_grad = dot_nt(hidden_grad, we_ref[...])
    sg_ref[...] = second_grad * gb_ref[1:2, :]
    sums[0:1, :] += jnp.sum(second_grad * normalized, axis=0, keepdims=True)
    sums[1:2, :] += jnp.sum(second_grad, axis=0, keepdims=True)
    ge[...] += dot_tn(second, hidden_grad)
    gs[...] += dot_tn(g, activated)
    gd[...] += dot_tn(g, attended)
    attended_grad = dot_nn(g, wd_ref[...]).astype(BF16).astype(F32)
    product = attended_grad * out
    lane = lanes_of((block, LANES))
    for h in range(heads):
        tile = slice(h // 2 * LANES, (h // 2 + 1) * LANES)
        mine = (lane < HD) if h % 2 == 0 else (lane >= HD)
        delta = split3(jnp.sum(jnp.where(mine, product[:, tile], 0.0), axis=-1, keepdims=True))
        grad = attended_grad[:, tile]
        if h % 2:
            grad = pltpu.roll(grad, HD, 1)
        grad = jnp.where(lane < HD, grad, 0.0)
        doa_ref[:, h * LANES : (h + 1) * LANES] = with_lanes(grad, DELTA_LANE, [-c for c in delta]).astype(BF16)
    for r in range(PIECES):

        @pl.when(step // per == r)
        def _():
            br_refs[r][pl.ds(place, block), :] = b_now[...]

    @pl.when(step == last)
    def _():
        small[...] = norm_columns(sums)
        width = sum(t.shape[1] for t in (gd, ge, gs))
        write_parts(info_ref, (gd, ge, gs), width, small, a_refs, b_refs)


def feed(info, xs, g_parts, out, wd, we, ws, gb, pairs, block=256):
    feats, hidden = we.shape
    heads = wd.shape[1] // HD
    rows = feats // (2 * pairs)
    width = wd.shape[1] + 2 * hidden
    piece = (PIECE, feats)
    part = (rows, width + LANES)
    by_step = lambda i: (i, 0)
    return pl.pallas_call(
        partial(feed_kernel, pairs, heads),
        grid=(L // block,),
        in_specs=[pl.BlockSpec(memory_space=pltpu.SMEM), pl.BlockSpec((block, feats), by_step)]
        + [once(piece)] * PIECES
        + [pl.BlockSpec((block, heads * HD), by_step)]
        + [once(wd.shape), once(we.shape), once(ws.shape), once(gb.shape)],
        out_specs=[once(piece)] * PIECES
        + [pl.BlockSpec((block, feats), by_step), pl.BlockSpec((block, heads * LANES), by_step)]
        + [once(part)] * (2 * pairs),
        out_shape=[jax.ShapeDtypeStruct(piece, BF16)] * PIECES
        + [jax.ShapeDtypeStruct((L, feats), F32), jax.ShapeDtypeStruct((L, heads * LANES), BF16)]
        + [jax.ShapeDtypeStruct(part, BF16)] * (2 * pairs),
        scratch_shapes=[
            pltpu.VMEM((block, feats), BF16),
            pltpu.VMEM((block, feats), BF16),
            pltpu.VMEM(wd.shape, F32),
            pltpu.VMEM(we.shape, F32),
            pltpu.VMEM(ws.shape, F32),
            pltpu.VMEM((8, feats), F32),
            pltpu.VMEM((feats, LANES), F32),
        ],
        compiler_params=params(60),
        cost_estimate=cost(12 * L * feats * hidden, 20 * L * feats),
        name="feed_forward_and_back",
    )(info, xs.reshape(L, feats), *g_parts, out, wd, we, ws, gb)


def attend_back_kernel(info_ref, q_ref, do_ref, k_ref, v_ref, cos_ref, up_ref, down_ref, pg_ref, dq, dk, dv):
    me = info_ref[0]
    here = q_ref.shape[1] // LANES
    causal = rows_of((PIECE, PIECE)) <= lanes_of((PIECE, PIECE))
    at = [pl.multiple_of((me ^ j) * PIECE, PIECE) for j in range(PIECES)]
    for h in range(here):
        sl = slice(h * LANES, (h + 1) * LANES)
        for j in range(PIECES):
            key = k_ref[pl.ds(at[j], PIECE), sl]
            value = v_ref[pl.ds(at[j], PIECE), sl]
            key_sum = value_sum = None
            for i in range(j, PIECES):
                query = q_ref[pl.ds(at[i], PIECE), sl]
                grad = do_ref[pl.ds(at[i], PIECE), sl]
                scores = dot_nt(key, query)
                if i == j:
                    scores = jnp.where(causal, scores, MASKED)
                probs = jnp.exp(scores)
                score_grad = (probs * dot_nt(value, grad)).astype(BF16)
                value_term = dot_nn(probs.astype(BF16), grad)
                key_term = dot_nn(score_grad, query)
                value_sum = value_term if value_sum is None else value_sum + value_term
                key_sum = key_term if key_sum is None else key_sum + key_term
                query_term = dot_tn(score_grad, key)
                if j == 0:
                    dq[h, i] = query_term
                else:
                    dq[h, i] += query_term
            dk[h, j] = key_sum
            dv[h, j] = value_sum
    low = lanes_of((PIECE, LANES)) < HD

    def join(left, right):
        return jnp.where(low, left, pltpu.roll(right, HD, 1)).astype(BF16)

    for j in range(PIECES):
        rows = pl.ds(at[j], PIECE)
        cosine = cos_ref[j * PIECE : (j + 1) * PIECE, :]
        up, down = -up_ref[j * PIECE : (j + 1) * PIECE, :], -down_ref[j * PIECE : (j + 1) * PIECE, :]
        for h in range(0, here, 2):
            start = h // 2 * 3 * LANES
            q0, q1 = (turn(dq[h + n, j] * HD ** (-0.5), cosine, up, down) for n in (0, 1))
            k0, k1 = (turn(dk[h + n, j], cosine, up, down) for n in (0, 1))
            v0, v1 = dv[h, j], dv[h + 1, j]
            for n, (left, right) in enumerate(((q0, k0), (v0, q1), (k1, v1))):
                pg_ref[rows, start + n * LANES : start + (n + 1) * LANES] = join(left, right)


def attend_back(info, queries, grads, keys, values, tables, group=2):
    width = queries.shape[1]
    heads = width // LANES
    head_block = pl.BlockSpec((L, group * LANES), lambda s, info: (0, s))
    table = once((L, LANES))
    return pl.pallas_call(
        attend_back_kernel,
        grid_spec=pltpu.PrefetchScalarGridSpec(
            num_scalar_prefetch=1,
            grid=(heads // group,),
            in_specs=[head_block] * 4 + [table] * 3,
            out_specs=pl.BlockSpec((L, group * 3 * HD), lambda s, info: (0, s)),
            scratch_shapes=[pltpu.VMEM((group, PIECES, PIECE, LANES), F32)] * 3,
        ),
        out_shape=jax.ShapeDtypeStruct((L, heads * 3 * HD), BF16),
        compiler_params=params(60),
        cost_estimate=cost(10 * heads * L * L * LANES, 12 * L * width, heads * L * L // 2),
        name="attention_backward",
    )(info, queries, grads, keys.reshape(L, width), values.reshape(L, width), *tables)


def project_back_kernel(pairs, info_ref, pg_ref, x_ref, sg_ref, w_ref, gb_ref, *refs):
    e_refs = refs[:PIECES]
    a_refs, b_refs = refs[PIECES : PIECES + pairs], refs[PIECES + pairs : PIECES + 2 * pairs]
    e_now, gq, sums, small = refs[PIECES + 2 * pairs :]
    step, last = pl.program_id(0), pl.num_programs(0) - 1
    block = x_ref.shape[0]
    per = PIECE // block

    @pl.when(step == 0)
    def _():
        gq[...] = jnp.zeros_like(gq)
        sums[...] = jnp.zeros_like(sums)

    normalized = normalize(x_ref[...])
    first = (normalized * gb_ref[0:1, :] + gb_ref[2:3, :]).astype(BF16)
    grad = pg_ref[...]
    first_grad = dot_nt(grad, w_ref[...])
    gq[...] += dot_tn(first, grad)
    e_now[...] = (first_grad * gb_ref[0:1, :] + sg_ref[...]).astype(BF16)
    sums[0:1, :] += jnp.sum(first_grad * normalized, axis=0, keepdims=True)
    sums[1:2, :] += jnp.sum(first_grad, axis=0, keepdims=True)
    place = pl.multiple_of(step % per * block, block)
    for r in range(PIECES):

        @pl.when(step // per == r)
        def _():
            e_refs[r][pl.ds(place, block), :] = e_now[...]

    @pl.when(step == last)
    def _():
        small[...] = norm_columns(sums)
        write_parts(info_ref, (gq,), gq.shape[1], small, a_refs, b_refs)


def project_back(info, pg, xs, sg, weight, gb, pairs, block=256):
    feats, width = weight.shape
    rows = feats // (2 * pairs)
    piece, part = (PIECE, feats), (rows, width + LANES)
    by_step = lambda i: (i, 0)
    return pl.pallas_call(
        partial(project_back_kernel, pairs),
        grid=(L // block,),
        in_specs=[
            pl.BlockSpec(memory_space=pltpu.SMEM),
            pl.BlockSpec((block, width), by_step),
            pl.BlockSpec((block, feats), by_step),
            pl.BlockSpec((block, feats), by_step),
            once(weight.shape),
            once(gb.shape),
        ],
        out_specs=[once(piece)] * PIECES + [once(part)] * (2 * pairs),
        out_shape=[jax.ShapeDtypeStruct(piece, BF16)] * PIECES
        + [jax.ShapeDtypeStruct(part, BF16)] * (2 * pairs),
        scratch_shapes=[
            pltpu.VMEM((block, feats), BF16),
            pltpu.VMEM(weight.shape, F32),
            pltpu.VMEM((8, feats), F32),
            pltpu.VMEM((feats, LANES), F32),
        ],
        compiler_params=params(50),
        cost_estimate=cost(4 * L * feats * width, 10 * L * feats),
        name="project_back",
    )(info, pg, xs.reshape(L, feats), sg, weight, gb)


def build_tables(segments):
    places = jnp.arange(L, dtype=jnp.int32)
    starts = jnp.zeros_like(segments)
    for value in range(DOCS):
        starts = starts + jnp.where(segments > value, jnp.sum((segments == value).astype(jnp.int32)), 0)
    position = (places - starts).astype(F32)
    lane = jnp.arange(LANES, dtype=jnp.int32)
    inner = lane % HD
    half = ROT // 2
    frequency = 10000.0 ** (-((inner % half).astype(F32) * 2.0 / ROT))
    angles = position[:, None] * frequency[None, :]
    turned = (inner < ROT)[None, :]
    sine = jnp.sin(angles)
    cosine = jnp.where(turned, jnp.cos(angles), 1.0)
    up = jnp.where(turned & (inner >= half)[None, :], sine, 0.0)
    down = jnp.where((inner < half)[None, :], -sine, 0.0)
    feature = lane - SEG_LANE
    is_doc = ((feature >= 0) & (feature < DOCS))[None, :]
    same = segments[:, None] == feature[None, :]
    one = ((lane >= LSE_LANE) & (lane < LSE_LANE + 3))[None, :]
    query_feature = jnp.where(is_doc & ~same, MASKED, 0.0)
    key_feature = jnp.where((is_doc & same) | one, 1.0, 0.0)
    return cosine, up, down, query_feature, key_feature


class Wires:
    def __init__(self, mesh):
        self.pairs = mesh.shape["pair"]
        self.sizes = [mesh.shape[a] for a in AXES]

    def send(self, array, target):
        _, cores, halves, ms = self.sizes

        def index(k, c, h, m):
            return ((k * cores + c) * halves + h) * ms + m

        moves = []
        for k in range(self.pairs):
            for c in range(cores):
                for h in range(halves):
                    for m in range(ms):
                        there = target(k, c, h, m)
                        if there is not None:
                            moves.append((index(k, c, h, m), index(*there)))
        return lax.ppermute(array, AXES, moves)

    def core(self, array):
        return self.send(array, lambda k, c, h, m: (k, 1 - c, h, m))

    def near(self, array):
        return self.send(array, lambda k, c, h, m: (k, c, h, 1 - m))

    def half(self, array):
        return self.send(array, lambda k, c, h, m: (k, c, 1 - h, m))

    def regroup(self, array):
        return self.send(array, lambda k, c, h, m: (k, 1 - c, 1 - h, m) if c != h else None)

    def plane(self, array, bit):
        return self.send(array, lambda k, c, h, m: (k ^ bit, c, h, m))

    def bits(self):
        bits = [1 << b for b in range(self.pairs.bit_length() - 1)]
        return bits, bits[::-1]

    def plane_gather(self, a_block, b_block):
        result = []
        for block, bits in zip((a_block, b_block), self.bits()):
            parts = {0: block}
            for bit in bits:
                for j in list(parts):
                    parts[j | bit] = self.plane(parts[j], bit)
            result.append([parts[j] for j in range(self.pairs)])
        return result

    def plane_scatter(self, a_parts, b_parts):
        result = []
        for parts, bits in zip((a_parts, b_parts), self.bits()):
            parts = dict(enumerate(parts))
            for bit in reversed(bits):
                for j in sorted(j for j in parts if j & bit):
                    arrived = self.plane(parts.pop(j), bit).astype(F32)
                    parts[j ^ bit] = (parts[j ^ bit].astype(F32) + arrived).astype(BF16)
            result.append(parts[0])
        return result


def on_device(mesh, inputs, qkv_weight, dense_weight, expand_weight, shrink_weight, norm_gains, norm_biases, cotangent, segments):
    wires = Wires(mesh)
    pairs = wires.pairs
    pair, core, half, near = (lax.axis_index(a) for a in AXES)
    native = core == half
    me = 2 * core + near
    info = jnp.stack([me, core, pair, half]).astype(jnp.int32)
    rows = qkv_weight.shape[0]

    def gather_weights(block):
        swapped = wires.half(block)
        own = jnp.where(native, block, swapped)
        other = wires.core(jnp.where(native, swapped, block))
        return wires.plane_gather(own, other)

    def gather_tokens(block):
        mine = jnp.where(native, block, wires.regroup(block))
        beside = wires.near(mine)
        return mine, beside, wires.core(mine), wires.core(beside)

    def reduce_tokens(parts):
        kept = parts[0].astype(F32) + wires.core(parts[2]).astype(F32)
        passed = (parts[1].astype(F32) + wires.core(parts[3]).astype(F32)).astype(BF16)
        kept = kept + wires.near(passed).astype(F32)
        return jnp.where(native, kept, wires.regroup(kept.astype(BF16)).astype(F32))

    def reduce_weights(a_parts, b_parts):
        a_sum, b_sum = wires.plane_scatter(a_parts, b_parts)
        other = wires.core(b_sum)
        mine = jnp.where(native, a_sum, other).astype(F32)
        sent = jnp.where(native, other, a_sum)
        arrived = wires.half(sent).astype(F32)
        total = mine + arrived
        small = (a_sum[:, -LANES:].astype(F32) + other[:, -LANES:].astype(F32)).astype(BF16)
        small = small.astype(F32) + wires.half(small).astype(F32)
        small = small + wires.near(small.astype(BF16)).astype(F32)
        return total[:, :-LANES], small[:, :2].T

    small = jnp.concatenate([norm_gains, norm_biases], axis=0).T
    first_block = jnp.concatenate([qkv_weight, jnp.pad(small, ((0, 0), (0, LANES - 4)))], axis=1)
    first_parts = gather_weights(first_block)
    x_parts = gather_tokens(inputs)
    other_segments = wires.core(segments)
    tables = build_tables(jnp.where(native, segments, other_segments))
    second_parts = gather_weights(jnp.concatenate([dense_weight, expand_weight, shrink_weight], axis=1))
    g_parts = gather_tokens(cotangent)

    qkv_full, gb = assemble_first(info, *first_parts, qkv_weight.shape[1])
    stacks = ()
    for r in range(PIECES):
        stacks = project(r, info, x_parts[r], qkv_full, gb, tables, stacks)
    xs, queries, keys, values = stacks
    out, queries_back = attend(info, queries, keys, values)
    widths = (dense_weight.shape[1], expand_weight.shape[1], shrink_weight.shape[1])
    dense_full, expand_full, shrink_full = assemble_second(info, *second_parts, widths)
    results = feed(info, xs, g_parts, out, dense_full, expand_full, shrink_full, gb, pairs)
    branches = results[:PIECES]
    second_e, out_grads = results[PIECES : PIECES + 2]
    feed_grads = results[PIECES + 2 : PIECES + 2 + pairs], results[PIECES + 2 + pairs :]
    rows_f32 = inputs.astype(F32)
    layer_out = (rows_f32 + reduce_tokens(branches)).astype(BF16)
    feed_total, feedforward_norm_grad = reduce_weights(*feed_grads)
    dense_grad = feed_total[:, : widths[0]]
    expand_grad = feed_total[:, widths[0] : widths[0] + widths[1]]
    shrink_grad = feed_total[:, widths[0] + widths[1] :]

    projected_grad = attend_back(info, queries_back, out_grads, keys, values, tables[:3])
    results = project_back(info, projected_grad, xs, second_e, qkv_full, gb, pairs)
    e = reduce_tokens(results[:PIECES])
    qkv_grad, attention_norm_grad = reduce_weights(results[PIECES : PIECES + pairs], results[PIECES + pairs :])

    centered = rows_f32 - jnp.mean(rows_f32, axis=-1, keepdims=True)
    inv_scale = lax.rsqrt(jnp.mean(centered * centered, axis=-1, keepdims=True) + EPSILON)
    normalized = centered * inv_scale
    input_grad = cotangent.astype(F32) + inv_scale * (
        e - jnp.mean(e, axis=-1, keepdims=True) - normalized * jnp.mean(e * normalized, axis=-1, keepdims=True)
    )
    return (
        layer_out,
        input_grad,
        qkv_grad,
        dense_grad,
        expand_grad,
        shrink_grad,
        attention_norm_grad,
        feedforward_norm_grad,
    )


def solution(mesh):
    dp, tensor = mesh.shape["dp"], mesh.shape["tensor"]
    fine = Mesh(mesh.devices.reshape(dp // 2, 2, 2, tensor // 2), AXES)
    data, split = ("pair", "core"), ("half", "m")
    tokens, weight, norm = P(AXES, None), P(data, split), P(None, data)
    return jax.shard_map(
        partial(on_device, fine),
        mesh=fine,
        in_specs=(tokens, weight, weight, weight, weight, norm, norm, tokens, P(data)),
        out_specs=(tokens, tokens, weight, weight, weight, weight, norm, norm),
        check_vma=False,
    )
```

```python
from functools import partial

import jax
import jax.numpy as jnp
from jax import lax
from jax.experimental import pallas as pl
from jax.experimental.pallas import tpu as pltpu
from jax.sharding import Mesh
from jax.sharding import PartitionSpec as P

HD = 64
ROT = 16
L = 2048
LANES = 128
EPSILON = 1e-05
MASKED = -1e30
AXES = ("pair", "core", "half", "m")
PIECES = 4
PIECE = L // PIECES
SEG_LANE = 64
DOCS = 5
LSE_LANE = SEG_LANE + DOCS
DELTA_LANE = 64
MIB = 1024 * 1024
F32 = jnp.float32
BF16 = jnp.bfloat16


def dot_nn(left, right):
    return lax.dot_general(left, right, (((1,), (0,)), ((), ())), preferred_element_type=F32)


def dot_nt(left, right):
    return lax.dot_general(left, right, (((1,), (1,)), ((), ())), preferred_element_type=F32)


def dot_tn(left, right):
    return lax.dot_general(left, right, (((0,), (0,)), ((), ())), preferred_element_type=F32)


def lanes_of(shape):
    return lax.broadcasted_iota(jnp.int32, shape, len(shape) - 1)


def rows_of(shape):
    return lax.broadcasted_iota(jnp.int32, shape, len(shape) - 2)


def normalize(x):
    rows = x.astype(F32)
    centered = rows - jnp.mean(rows, axis=-1, keepdims=True)
    return centered * lax.rsqrt(jnp.mean(centered * centered, axis=-1, keepdims=True) + EPSILON)


def split3(column):
    high = column.astype(BF16).astype(F32)
    rest = column - high
    middle = rest.astype(BF16).astype(F32)
    return high, middle, rest - middle


def with_lanes(base, first, columns):
    lane = lanes_of(base.shape)
    for offset, column in enumerate(columns):
        base = jnp.where(lane == first + offset, column, base)
    return base


def params():
    return pltpu.CompilerParams(vmem_limit_bytes=60 * MIB)


def fenced(kernel, inputs, after):
    return lambda *refs: kernel(*refs[:inputs], *refs[inputs + after :])


ANYWHERE = pl.BlockSpec(memory_space=pl.ANY)


def whole(shape, **kw):
    return pl.BlockSpec(shape, lambda *_: (0,) * len(shape), **kw)


def once(shape):
    return whole(shape, pipeline_mode=pl.Buffered(1))


def cost(flops, nbytes, trans=0):
    return pl.CostEstimate(flops=int(flops), bytes_accessed=int(nbytes), transcendentals=int(trans))


def hops(pairs):
    near = [0] + [1 << b for b in range(pairs.bit_length() - 1)]
    far = sorted((j for j in range(pairs) if j not in near), key=lambda j: (j.bit_count(), j))
    return near, far


def block_places(info_ref, pairs, rows):
    near, far = hops(pairs)
    return pair_places(info_ref, near + far, rows)


def pair_places(info_ref, order, rows):
    core, pair = info_ref[1], info_ref[2]
    for j in order:
        base = (pair ^ j) * 2
        yield pl.multiple_of((base + core) * rows, rows), pl.multiple_of((base + 1 - core) * rows, rows)


def block_refs(refs, pairs):
    near, far = hops(pairs)
    refs = list(refs)
    for _ in near:
        both = refs.pop(0)
        yield both.at[0], both.at[1]
    for _ in far:
        yield refs.pop(0), refs.pop(0)


def block_shapes(pairs, rows, width):
    near, far = hops(pairs)
    return [(2, rows, width)] * len(near) + [(rows, width)] * (2 * len(far))


def assemble_first_kernel(pairs, rows, width, info_ref, *refs):
    weight_ref, gb_ref, small = refs[-3:]
    for offs, both in zip(pair_places(info_ref, range(pairs), rows), refs[:-3]):
        for off, part in zip(offs, (both.at[0], both.at[1])):
            weight_ref[pl.ds(off, rows), :] = part[:, :width]
            small[pl.ds(off, rows), :] = part[:, width:].astype(F32)
    gb_ref[...] = small[...].T[:8, :]


def assemble_first(info, parts, pairs, width):
    rows = parts[0].shape[1]
    feats = pairs * 2 * rows
    return pl.pallas_call(
        partial(assemble_first_kernel, pairs, rows, width),
        out_shape=(jax.ShapeDtypeStruct((feats, width), BF16), jax.ShapeDtypeStruct((8, feats), F32)),
        in_specs=[pl.BlockSpec(memory_space=pltpu.SMEM)] + [pl.BlockSpec(memory_space=pltpu.VMEM)] * len(parts),
        scratch_shapes=[pltpu.VMEM((feats, LANES), F32)],
        compiler_params=params(),
        cost_estimate=cost(0, 4 * feats * width),
        name="assemble_qkv",
    )(info, *parts)


def assemble_second_kernel(pairs, rows, widths, info_ref, *refs):
    outs = refs[-len(widths) :]
    for offs, parts in zip(block_places(info_ref, pairs, rows), block_refs(refs[: -len(widths)], pairs)):
        for off, part in zip(offs, parts):
            start = 0
            for out, width in zip(outs, widths):
                out[pl.ds(off, rows), :] = part[:, start : start + width]
                start += width


def assemble_second(info, parts, pairs, widths):
    rows = parts[0].shape[1]
    feats = pairs * 2 * rows
    return pl.pallas_call(
        partial(assemble_second_kernel, pairs, rows, widths),
        out_shape=tuple(jax.ShapeDtypeStruct((feats, w), BF16) for w in widths),
        in_specs=[pl.BlockSpec(memory_space=pltpu.SMEM)] + [pl.BlockSpec(memory_space=pltpu.VMEM)] * len(parts),
        compiler_params=params(),
        cost_estimate=cost(0, 4 * feats * sum(widths)),
        name="assemble_ffn",
    )(info, *parts)


def turn(values, cosine, sine_up, sine_down):
    return (
        values * cosine
        + pltpu.roll(values, ROT // 2, 1) * sine_up
        + pltpu.roll(values, LANES - ROT // 2, 1) * sine_down
    )


def project_kernel(heads, info_ref, xa_ref, xb_ref, w_ref, gb_ref, turn_ref, feature_ref, *refs):
    n_ref, q_ref, k_ref, v_ref = refs[-4:]
    first_piece = pl.program_id(0) < pl.num_programs(0) // 2
    normalized = normalize(jnp.where(first_piece, xa_ref[...], xb_ref[...]))
    n_ref[0] = normalized
    first = (normalized * gb_ref[0:1, :] + gb_ref[2:3, :]).astype(BF16)
    projected = dot_nn(first, w_ref[...])
    cosine, up, down = (turn_ref[:, n * LANES : (n + 1) * LANES] for n in range(3))
    query_feature, key_feature = (feature_ref[:, n * LANES : (n + 1) * LANES].astype(F32) for n in range(2))
    lane = lanes_of(cosine.shape)
    low = lane < HD
    value_feature = ((lane >= DELTA_LANE) & (lane < DELTA_LANE + 3)).astype(F32)

    def part(offset):
        tile = projected[:, offset // LANES * LANES : offset // LANES * LANES + LANES]
        return pltpu.roll(tile, HD, 1) if offset % LANES else tile

    for h in range(heads):
        sl = slice(h * LANES, (h + 1) * LANES)
        base = h * 3 * HD
        query = turn(part(base), cosine, up, down) * HD ** (-0.5)
        key = turn(part(base + HD), cosine, up, down)
        q_ref[0, :, sl] = jnp.where(low, query, query_feature).astype(BF16)
        k_ref[0, :, sl] = jnp.where(low, key, key_feature).astype(BF16)
        v_ref[0, :, sl] = jnp.where(low, part(base + 2 * HD), value_feature).astype(BF16)


def project(r, info, xa, xb, weight, gb, tables, stacks, after=(), block=256):
    feats, width = weight.shape
    heads = width // (3 * HD)
    steps = PIECE // block
    shapes = [(PIECES, PIECE, feats)] + [(PIECES, PIECE, heads * LANES)] * 3
    kinds = [F32, BF16, BF16, BF16]
    piece = lambda i: r + 2 * (i // steps)
    table = lambda n: pl.BlockSpec((block, n * LANES), lambda i, info: ((info[0] ^ piece(i)) * steps + i % steps, 0))
    inputs = [info, xa, xb, weight, gb, *tables]
    return pl.pallas_call(
        partial(project_kernel, heads),
        grid_spec=pltpu.PrefetchScalarGridSpec(
            num_scalar_prefetch=1,
            grid=(2 * steps,),
            in_specs=[
                pl.BlockSpec((block, feats), lambda i, info: (jnp.minimum(i, steps - 1), 0)),
                pl.BlockSpec((block, feats), lambda i, info: (jnp.maximum(i - steps, 0), 0)),
                once((feats, width)),
                once((8, feats)),
                table(3),
                table(2),
            ]
            + [ANYWHERE] * (len(stacks) + len(after)),
            out_specs=[pl.BlockSpec((1, block, s[2]), lambda i, info: (piece(i), i % steps, 0)) for s in shapes],
        ),
        out_shape=[jax.ShapeDtypeStruct(s, kind) for s, kind in zip(shapes, kinds)],
        input_output_aliases={len(inputs) + n: n for n in range(len(stacks))},
        compiler_params=params(),
        cost_estimate=cost(4 * PIECE * feats * width, 2 * (feats * width + 12 * PIECE * feats)),
        name=f"project_{r}",
    )(*inputs, *stacks, *after)


def attend_kernel(heads, info_ref, q_ref, k_ref, v_ref, o_ref, qb_ref):
    me = info_ref[0]
    causal = lanes_of((PIECE, PIECE)) <= rows_of((PIECE, PIECE))
    low = lanes_of((PIECE, LANES)) < HD
    at = [pl.multiple_of((me ^ p) * PIECE, PIECE) for p in range(PIECES)]
    for i in range(PIECES):
        rows = pl.ds(at[i], PIECE)
        outs = []
        for h in range(heads):
            sl = slice(h * LANES, (h + 1) * LANES)
            query = q_ref[rows, sl]
            scores = [dot_nt(query, k_ref[pl.ds(at[j], PIECE), sl]) for j in range(i + 1)]
            scores[-1] = jnp.where(causal, scores[-1], MASKED)
            top = jnp.max(scores[0], axis=-1, keepdims=True)
            for s in scores[1:]:
                top = jnp.maximum(top, jnp.max(s, axis=-1, keepdims=True))
            out = total = None
            for j, s in enumerate(scores):
                weight = jnp.exp(s - top)
                part = jnp.sum(weight, axis=-1, keepdims=True)
                term = dot_nn(weight.astype(BF16), v_ref[pl.ds(at[j], PIECE), sl])
                total = part if total is None else total + part
                out = term if out is None else out + term
            outs.append(out * (1.0 / total))
            log_total = split3(top + jnp.log(total))
            qb_ref[rows, sl] = with_lanes(query.astype(F32), LSE_LANE, [-c for c in log_total]).astype(BF16)
        for h in range(0, heads, 2):
            o_ref[rows, h * HD : h * HD + LANES] = jnp.where(low, outs[h], pltpu.roll(outs[h + 1], HD, 1))


def attend(info, queries, keys, values, group, heads, after=()):
    full = queries.shape[2]
    width = heads * LANES
    own = pl.BlockSpec((L, width), lambda i, info: (0, group))
    return pl.pallas_call(
        fenced(partial(attend_kernel, heads), 4, len(after)),
        grid_spec=pltpu.PrefetchScalarGridSpec(
            num_scalar_prefetch=1,
            grid=(1,),
            in_specs=[own] * 3 + [ANYWHERE] * len(after),
            out_specs=[whole((L, heads * HD)), whole((L, width))],
        ),
        out_shape=[jax.ShapeDtypeStruct((L, heads * HD), F32), jax.ShapeDtypeStruct((L, width), BF16)],
        compiler_params=params(),
        cost_estimate=cost(heads * L * L * LANES * 4, 5 * L * width, heads * L * L // 2),
        name=f"attention_forward_{group}",
    )(info, *(a.reshape(L, full) for a in (queries, keys, values)), *after)


def gelu_parts(h):
    bell = jnp.exp2(h * h * (-0.5 * 1.4426950408889634))
    t = pl.reciprocal(1.0 + (0.3275911 * 0.5**0.5) * jnp.abs(h))
    poly = t * (
        0.127414796 + t * (-0.142248368 + t * (0.7107068705 + t * (-0.7265760135 + t * 0.5307027145)))
    )
    tail = poly * bell
    return jnp.where(h < 0, tail, 1.0 - tail), bell * 0.3989422804014327


def norm_columns(sums_ref):
    wide = jnp.concatenate([sums_ref[...], jnp.zeros((LANES - 8, sums_ref.shape[1]), F32)], axis=0)
    return wide.T


def write_parts(info_ref, total, small, refs):
    width, rows = total.shape[1], refs[0].shape[1]
    for offs, both in zip(pair_places(info_ref, range(len(refs)), rows), refs):
        for n, off in enumerate(offs):
            both[n, :, :width] = total[pl.ds(off, rows), :].astype(BF16)
            both[n, :, width:] = small[pl.ds(off, rows), :].astype(BF16)


def feed_kernel(groups, parts, n_ref, *refs):
    o_refs, refs = refs[:groups], refs[groups:]
    wd_ref, we_ref, ws_ref, gb_ref, br01_ref, br23_ref, activated_ref, slope_ref, b_now = refs
    step = pl.program_id(0)
    rows = PIECE // parts
    for n in range(parts):
        sl = slice(n * rows, (n + 1) * rows)
        second = (n_ref[sl, :] * gb_ref[1:2, :] + gb_ref[3:4, :]).astype(BF16)
        hidden = dot_nn(second, we_ref[...])
        cdf, density = gelu_parts(hidden)
        activated = (hidden * cdf).astype(BF16)
        activated_ref[sl, :] = activated
        slope_ref[sl, :] = cdf + hidden * density
        attended = jnp.concatenate([o[sl, :] for o in o_refs], axis=1).astype(BF16)
        b_now[sl, :] = (dot_nt(attended, wd_ref[...]) + dot_nt(activated, ws_ref[...])).astype(BF16)

    @pl.when(step < 2)
    def _():
        br01_ref[0] = b_now[...]

    @pl.when(step >= 2)
    def _():
        br23_ref[0] = b_now[...]


def feed(normalized, outs, wd, we, ws, gb, after=(), parts=2):
    feats, hidden = we.shape
    two = (2, PIECE, feats)
    by_step = lambda i: (i, 0)
    inputs = [normalized.reshape(L, feats), *outs, wd, we, ws, gb]
    return pl.pallas_call(
        fenced(partial(feed_kernel, len(outs), parts), len(inputs), len(after)),
        grid=(PIECES,),
        in_specs=[pl.BlockSpec((PIECE, feats), by_step)]
        + [pl.BlockSpec((PIECE, o.shape[1]), by_step) for o in outs]
        + [once(w.shape) for w in (wd, we, ws, gb)]
        + [ANYWHERE] * len(after),
        out_specs=[
            pl.BlockSpec((1, PIECE, feats), lambda i: (jnp.minimum(i, 1), 0, 0)),
            pl.BlockSpec((1, PIECE, feats), lambda i: (jnp.maximum(i - 2, 0), 0, 0)),
            pl.BlockSpec((PIECE, hidden), by_step),
            pl.BlockSpec((PIECE, hidden), by_step),
        ],
        out_shape=[jax.ShapeDtypeStruct(two, BF16)] * 2
        + [jax.ShapeDtypeStruct((L, hidden), BF16), jax.ShapeDtypeStruct((L, hidden), F32)],
        scratch_shapes=[pltpu.VMEM((PIECE, feats), BF16)],
        compiler_params=params(),
        cost_estimate=cost(4 * L * feats * hidden, 16 * L * feats),
        name="feed_forward",
    )(*inputs, *after)


def feed_back_kernel(heads, group, n_ref, activated_ref, slope_ref, *refs):
    groups = heads // group
    g_refs, refs = refs[:PIECES], refs[PIECES:]
    o_refs, refs = refs[:groups], refs[groups:]
    (wd_ref, we_ref, ws_ref, gb_ref, sg_ref), refs = refs[:5], refs[5:]
    doa_refs, refs = refs[:groups], refs[groups:]
    grads_ref, g_now, gd, ge, gs, sums = refs
    step, last = pl.program_id(0), pl.num_programs(0) - 1

    @pl.when(step == 0)
    def _():
        for total in (gd, ge, gs, sums):
            total[...] = jnp.zeros_like(total)

    for r in range(PIECES):

        @pl.when(step == r)
        def _():
            g_now[...] = g_refs[r][...]

    g = g_now[...]
    hidden_grad = (dot_nn(g, ws_ref[...]) * slope_ref[...]).astype(BF16)
    normalized = n_ref[...]
    second = (normalized * gb_ref[1:2, :] + gb_ref[3:4, :]).astype(BF16)
    out = jnp.concatenate([o[...] for o in o_refs], axis=1)
    gs[...] += dot_tn(g, activated_ref[...])
    gd[...] += dot_tn(g, out.astype(BF16))
    ge[...] += dot_tn(second, hidden_grad)
    second_grad = dot_nt(hidden_grad, we_ref[...])
    sg_ref[...] = second_grad * gb_ref[1:2, :]
    sums[0:1, :] += jnp.sum(second_grad * normalized, axis=0, keepdims=True)
    sums[1:2, :] += jnp.sum(second_grad, axis=0, keepdims=True)
    attended_grad = dot_nn(g, wd_ref[...]).astype(BF16).astype(F32)
    product = attended_grad * out
    lane = lanes_of((PIECE, LANES))
    for h in range(heads):
        tile = slice(h // 2 * LANES, (h // 2 + 1) * LANES)
        mine = (lane < HD) if h % 2 == 0 else (lane >= HD)
        delta = split3(jnp.sum(jnp.where(mine, product[:, tile], 0.0), axis=-1, keepdims=True))
        grad = attended_grad[:, tile]
        if h % 2:
            grad = pltpu.roll(grad, HD, 1)
        grad = jnp.where(lane < HD, grad, 0.0)
        start = h % group * LANES
        doa_refs[h // group][:, start : start + LANES] = with_lanes(grad, DELTA_LANE, [-c for c in delta]).astype(BF16)

    @pl.when(step == last)
    def _():
        start = 0
        for total in (gd, ge, gs):
            grads_ref[:, start : start + total.shape[1]] = total[...].astype(BF16)
            start += total.shape[1]
        grads_ref[:, start:] = norm_columns(sums).astype(BF16)


def feed_back(normalized, activated, slope, g_parts, outs, wd, we, ws, gb, after=()):
    feats, hidden = we.shape
    heads = wd.shape[1] // HD
    group = heads // len(outs)
    width = wd.shape[1] + 2 * hidden + LANES
    by_step = lambda i: (i, 0)
    step = lambda w: pl.BlockSpec((PIECE, w), by_step)
    inputs = [normalized.reshape(L, feats), activated, slope, *g_parts, *outs, wd, we, ws, gb]
    return pl.pallas_call(
        fenced(partial(feed_back_kernel, heads, group), len(inputs), len(after)),
        grid=(PIECES,),
        in_specs=[step(feats), step(hidden), step(hidden)]
        + [once((PIECE, feats))] * PIECES
        + [step(group * HD)] * len(outs)
        + [once(w.shape) for w in (wd, we, ws, gb)]
        + [ANYWHERE] * len(after),
        out_specs=[step(feats)] + [step(group * LANES)] * len(outs) + [once((feats, width))],
        out_shape=[jax.ShapeDtypeStruct((L, feats), F32)]
        + [jax.ShapeDtypeStruct((L, group * LANES), BF16)] * len(outs)
        + [jax.ShapeDtypeStruct((feats, width), BF16)],
        scratch_shapes=[
            pltpu.VMEM((PIECE, feats), BF16),
            pltpu.VMEM(wd.shape, F32),
            pltpu.VMEM(we.shape, F32),
            pltpu.VMEM(ws.shape, F32),
            pltpu.VMEM((8, feats), F32),
        ],
        compiler_params=params(),
        cost_estimate=cost(8 * L * feats * hidden, 20 * L * feats),
        name="feed_back",
    )(*inputs, *after)


def block_back(query, grad, key, value, causal):
    scores = dot_nt(key, query)
    if causal is not None:
        scores = jnp.where(causal, scores, MASKED)
    probs = jnp.exp(scores)
    score_grad = (probs * dot_nt(value, grad)).astype(BF16)
    return dot_tn(score_grad, key), dot_nn(score_grad, query), dot_nn(probs.astype(BF16), grad)


def triangle_back(load, base, sums, h, causal):
    q0, g0, k0, v0 = load(base)
    q1, g1, k1, v1 = load(base + 1)
    low = block_back(q0, g0, k0, v0, causal)
    side = block_back(q1, g1, k0, v0, None)
    high = block_back(q1, g1, k1, v1, causal)
    dq, dk, dv = sums
    dq[h, base] += low[0]
    dq[h, base + 1] += side[0] + high[0]
    for d, n in ((dk, 1), (dv, 2)):
        d[h, base] += low[n] + side[n]
        d[h, base + 1] += high[n]


def finish_back(pg_ref, tables_ref, table_row, sums, base, near, heads):
    low = lanes_of((PIECE, LANES)) < HD
    dq, dk, dv = sums
    for n in range(2):
        rows = pl.ds(pl.multiple_of(table_row + n * PIECE, PIECE), PIECE)
        cosine = tables_ref[rows, :LANES]
        up, down = -tables_ref[rows, LANES : 2 * LANES], -tables_ref[rows, 2 * LANES :]
        for h in range(0, heads, 2):
            start = h // 2 * 3 * LANES
            q0, q1 = (turn(dq[h + x, base + n] * HD ** (-0.5), cosine, up, down) for x in (0, 1))
            k0, k1 = (turn(dk[h + x, base + n], cosine, up, down) for x in (0, 1))
            v0, v1 = dv[h, base + n], dv[h + 1, base + n]
            for tile, (left, right) in enumerate(((q0, k0), (v0, q1), (k1, v1))):
                pg_ref[near ^ n, :, start + tile * LANES : start + (tile + 1) * LANES] = jnp.where(
                    low, left, pltpu.roll(right, HD, 1)
                ).astype(BF16)


def attend_back_first_kernel(info_ref, q_ref, do_ref, k_ref, v_ref, tables_ref, pg_ref, *refs):
    rests, sums = refs[:3], refs[3:]
    dq, dk, dv = sums
    me, half = info_ref[0], info_ref[3]
    heads = q_ref.shape[1] // LANES
    causal = rows_of((PIECE, PIECE)) <= lanes_of((PIECE, PIECE))
    swapped, native = 2 * (1 - half), 2 * half
    zero = jnp.zeros((PIECE, LANES), F32)
    for h in range(heads):
        sl = slice(h * LANES, (h + 1) * LANES)

        def load(piece):
            rows = pl.ds(pl.multiple_of((me ^ piece) * PIECE, PIECE), PIECE)
            return q_ref[rows, sl], do_ref[rows, sl], k_ref[rows, sl], v_ref[rows, sl]

        pieces = [load(p) for p in range(PIECES)]
        terms = {
            (i, j): block_back(*pieces[i][:2], *pieces[j][2:], None) for j in (0, 1) for i in (2, 3)
        }
        for p in (0, 1):
            dq[h, p] = zero
            dq[h, p + 2] = terms[p + 2, 0][0] + terms[p + 2, 1][0]
            for d, n in ((dk, 1), (dv, 2)):
                d[h, p] = terms[2, p][n] + terms[3, p][n]
                d[h, p + 2] = zero
        triangle_back(load, swapped, sums, h, causal)
        for rest, d in zip(rests, sums):
            for n in range(2):
                rest[h, n] = d[h, native + n]
    finish_back(pg_ref, tables_ref, swapped * PIECE, sums, swapped, me % 2, heads)


def attend_back_second_kernel(info_ref, q_ref, do_ref, k_ref, v_ref, tables_ref, *refs):
    rests, pg_ref, sums = refs[:3], refs[3], refs[4:]
    near = info_ref[0] % 2
    heads = q_ref.shape[1] // LANES
    causal = rows_of((PIECE, PIECE)) <= lanes_of((PIECE, PIECE))
    for h in range(heads):
        sl = slice(h * LANES, (h + 1) * LANES)

        def load(piece):
            rows = pl.ds(pl.multiple_of((near ^ piece) * PIECE, PIECE), PIECE)
            return q_ref[rows, sl], do_ref[rows, sl], k_ref[rows, sl], v_ref[rows, sl]

        for rest, d in zip(rests, sums):
            for n in range(2):
                d[h, n] = rest[h, n]
        triangle_back(load, 0, sums, h, causal)
    finish_back(pg_ref, tables_ref, 0, sums, 0, near, heads)


def attend_back(info, queries, grads, keys, values, tables, group, rests=(), after=()):
    width, full = queries.shape[1], keys.shape[2]
    heads = width // LANES
    rest = (heads, 2, PIECE, LANES)
    pg = (2, PIECE, heads * 3 * HD)
    first = not rests
    rows = L if first else L // 2
    place = (lambda info: 0) if first else (lambda info: info[1] ^ info[3])
    own = pl.BlockSpec((rows, width), lambda s, info: (place(info), 0))
    shared = pl.BlockSpec((rows, width), lambda s, info: (place(info), group))
    table = pl.BlockSpec((rows, 3 * LANES), lambda s, info: (0 if first else info[3], 0))
    inputs = [info, queries, grads, keys.reshape(L, full), values.reshape(L, full), tables, *rests]
    blocks = 7 if first else 3
    return pl.pallas_call(
        fenced(attend_back_first_kernel if first else attend_back_second_kernel, len(inputs), len(after)),
        grid_spec=pltpu.PrefetchScalarGridSpec(
            num_scalar_prefetch=1,
            grid=(1,),
            in_specs=[own, own, shared, shared, table] + [whole(rest)] * len(rests) + [ANYWHERE] * len(after),
            out_specs=[whole(pg)] + [whole(rest)] * (3 if first else 0),
            scratch_shapes=[pltpu.VMEM((heads, PIECES if first else 2, PIECE, LANES), F32)] * 3,
        ),
        out_shape=[jax.ShapeDtypeStruct(pg, BF16)] + [jax.ShapeDtypeStruct(rest, F32)] * (3 if first else 0),
        compiler_params=params(),
        cost_estimate=cost(blocks * heads * PIECE * PIECE * LANES * 10, 12 * L * width, blocks * heads * PIECE * PIECE),
        name=f"attention_backward_{group}" + ("a" if first else "b"),
    )(*inputs, *after)


def project_back_kernel(pairs, groups, final, info_ref, *refs):
    pg_refs, refs = refs[:groups], refs[groups:]
    (n_ref, sg_ref, w_ref, gb_ref), refs = refs[:4], refs[4:]
    if final:
        (gq_in, sums_in, e_ref), refs = refs[:3], refs[3:]
        *part_refs, gq, sums, small = refs
    else:
        e_ref, gq, sums = refs
    step, last = pl.program_id(0), pl.num_programs(0) - 1

    @pl.when(step == 0)
    def _():
        gq[...] = gq_in[...] if final else jnp.zeros_like(gq)
        sums[...] = sums_in[...] if final else jnp.zeros_like(sums)

    normalized = n_ref[0]
    first = (normalized * gb_ref[0:1, :] + gb_ref[2:3, :]).astype(BF16)
    grad = jnp.concatenate([pg[0] for pg in pg_refs], axis=1)
    first_grad = dot_nt(grad, w_ref[...])
    gq[...] += dot_tn(first, grad)
    e_ref[0] = (first_grad * gb_ref[0:1, :] + sg_ref[0]).astype(BF16)
    sums[0:1, :] += jnp.sum(first_grad * normalized, axis=0, keepdims=True)
    sums[1:2, :] += jnp.sum(first_grad, axis=0, keepdims=True)
    if final:

        @pl.when(step == last)
        def _():
            small[...] = norm_columns(sums)
            write_parts(info_ref, gq, small, part_refs)


def project_back(info, pgs, normalized, sg, weight, gb, pairs, so_far=(), after=()):
    feats, width = weight.shape
    final = bool(so_far)
    swapped = 0 if final else 1
    sums = (8, feats)
    shapes = [(2, feats // (2 * pairs), width + LANES)] * pairs if final else []
    two = (2, PIECE, feats)
    by_step = lambda i, info: (i, 0, 0)
    relative = pl.BlockSpec((1, PIECE, feats), lambda i, info: (2 * (info[1] ^ info[3] ^ swapped) + i, 0, 0))
    inputs = [info, *pgs, normalized, sg.reshape(PIECES, PIECE, feats), weight, gb, *so_far]
    totals = [pltpu.VMEM(weight.shape, F32), pltpu.VMEM(sums, F32)]
    results = [(two, BF16)] + ([(s, BF16) for s in shapes] if final else [(weight.shape, F32), (sums, F32)])
    return pl.pallas_call(
        fenced(partial(project_back_kernel, pairs, len(pgs), final), len(inputs), len(after)),
        grid_spec=pltpu.PrefetchScalarGridSpec(
            num_scalar_prefetch=1,
            grid=(2,),
            in_specs=[pl.BlockSpec((1, PIECE, pg.shape[2]), by_step) for pg in pgs]
            + [relative, relative]
            + [once(a.shape) for a in (weight, gb, *so_far)]
            + [ANYWHERE] * len(after),
            out_specs=[pl.BlockSpec((1, PIECE, feats), by_step)] + [once(s) for s, _ in results[1:]],
            scratch_shapes=totals + [pltpu.VMEM((feats, LANES), F32)] if final else [],
        ),
        out_shape=[jax.ShapeDtypeStruct(s, kind) for s, kind in results],
        compiler_params=params(),
        cost_estimate=cost(2 * L * feats * width, 6 * L * feats),
        name="project_back_" + ("b" if final else "a"),
    )(*inputs, *after)


def build_tables(segments):
    places = jnp.arange(L, dtype=jnp.int32)
    starts = jnp.zeros_like(segments)
    for value in range(DOCS):
        starts = starts + jnp.where(segments > value, jnp.sum((segments == value).astype(jnp.int32)), 0)
    position = (places - starts).astype(F32)
    lane = jnp.arange(LANES, dtype=jnp.int32)
    inner = lane % HD
    half = ROT // 2
    frequency = 10000.0 ** (-((inner % half).astype(F32) * 2.0 / ROT))
    angles = position[:, None] * frequency[None, :]
    turned = (inner < ROT)[None, :]
    sine = jnp.sin(angles)
    cosine = jnp.where(turned, jnp.cos(angles), 1.0)
    up = jnp.where(turned & (inner >= half)[None, :], sine, 0.0)
    down = jnp.where((inner < half)[None, :], -sine, 0.0)
    feature = lane - SEG_LANE
    is_doc = ((feature >= 0) & (feature < DOCS))[None, :]
    same = segments[:, None] == feature[None, :]
    one = ((lane >= LSE_LANE) & (lane < LSE_LANE + 3))[None, :]
    query_feature = jnp.where(is_doc & ~same, MASKED, 0.0)
    key_feature = jnp.where((is_doc & same) | one, 1.0, 0.0)
    features = jnp.concatenate([query_feature, key_feature], axis=1).astype(BF16)
    return jnp.concatenate([cosine, up, down], axis=1), features


class Wires:
    def __init__(self, mesh):
        self.pairs = mesh.shape["pair"]
        self.sizes = [mesh.shape[a] for a in AXES]

    def send(self, array, target):
        _, cores, halves, ms = self.sizes

        def index(k, c, h, m):
            return ((k * cores + c) * halves + h) * ms + m

        moves = []
        for k in range(self.pairs):
            for c in range(cores):
                for h in range(halves):
                    for m in range(ms):
                        there = target(k, c, h, m)
                        if there is not None:
                            moves.append((index(k, c, h, m), index(*there)))
        return lax.ppermute(array, AXES, moves)

    def core(self, array):
        return self.send(array, lambda k, c, h, m: (k, 1 - c, h, m))

    def near(self, array, native):
        return self.send(array, lambda k, c, h, m: (k, c, h, 1 - m) if (c == h) == native else None)

    def core_from(self, array, native):
        return self.send(array, lambda k, c, h, m: (k, 1 - c, h, m) if (c == h) == native else None)

    def near_all(self, array):
        return self.send(array, lambda k, c, h, m: (k, c, h, 1 - m))

    def across(self, array):
        return self.send(array, lambda k, c, h, m: (k, c, 1 - h, 1 - m))

    def half(self, array):
        return self.send(array, lambda k, c, h, m: (k, c, 1 - h, m))

    def regroup(self, array):
        return self.send(array, lambda k, c, h, m: (k, 1 - c, 1 - h, m) if c != h else None)

    def plane(self, array, bit):
        return self.send(array, lambda k, c, h, m: (k ^ bit, c, h, m))

    def gather_near(self, both):
        return [both] + [self.plane(both, j) for j in hops(self.pairs)[0][1:]]

    def gather_far(self, parts):
        near, far = hops(self.pairs)
        a_parts = {j: part[0] for j, part in zip(near, parts)}
        b_parts = {j: part[1] for j, part in zip(near, parts)}
        result = list(parts)
        for j in far:
            low, high = j & -j, 1 << (j.bit_length() - 1)
            a_parts[j] = self.plane(a_parts[j ^ low], low)
            b_parts[j] = self.plane(b_parts[j ^ high], high)
            result += [a_parts[j], b_parts[j]]
        return result

    def gather_direct(self, both):
        return [both] + [self.plane(both, j) for j in range(1, self.pairs)]

    def scatter_direct(self, parts):
        return [self.plane(part, j) for j, part in enumerate(parts) if j]


def on_device(mesh, inputs, qkv_weight, dense_weight, expand_weight, shrink_weight, norm_gains, norm_biases, cotangent, segments):
    wires = Wires(mesh)
    pairs = wires.pairs
    pair, core, half, near = (lax.axis_index(a) for a in AXES)
    native = core == half
    me = 2 * core + near
    info = jnp.stack([me, core, pair, half]).astype(jnp.int32)

    def since(value, *done):
        return lax.optimization_barrier((value, done))[0]

    def at(values):
        return lax.optimization_barrier(values)

    def swap_weights(block, swapped):
        own = jnp.where(native, block, swapped)
        return jnp.stack([own, wires.core(jnp.where(native, swapped, block))])

    def swap_grads(both):
        other = wires.core(both[1])
        small = (both[0][:, -LANES:].astype(F32) + other[:, -LANES:].astype(F32)).astype(BF16)
        mine, sent = jnp.where(native, both[0], other), jnp.where(native, other, both[0])
        return [jnp.concatenate([a[:, :-LANES], small], axis=1) for a in (mine, sent)]

    def core_sum(parts):
        return parts[0].astype(F32) + wires.core(parts[1]).astype(F32)

    def since(value, *done):
        return lax.optimization_barrier((value, done))[0]

    def since(value, *done):
        return lax.optimization_barrier((value, done))[0]

    small = jnp.concatenate([norm_gains, norm_biases], axis=0).T
    first_block = jnp.concatenate([qkv_weight, jnp.pad(small, ((0, 0), (0, LANES - 4)))], axis=1)
    first_swapped = wires.half(first_block)
    other_segments = wires.core(since(segments, first_block))
    x_swapped = wires.regroup(since(inputs, other_segments))
    x_near = wires.near(since(inputs, other_segments), True)
    first_both = swap_weights(first_block, first_swapped)
    first_parts = wires.gather_direct(first_both)
    tables = build_tables(jnp.where(native, since(segments, first_both), other_segments))
    first_parts = since(first_parts, tables)
    qkv_full, gb = assemble_first(info, first_parts, pairs, qkv_weight.shape[1])
    x_swapped, x_near, qkv_full, gb = at((x_swapped, x_near, qkv_full, gb))
    x_mine = jnp.where(native, inputs, x_swapped)
    x_far = wires.near(x_swapped, False)
    x_core = wires.core(x_mine)
    stacks = project(0, info, x_mine, x_core, qkv_full, gb, tables, ())

    stacks, x_near, x_far = at((stacks, x_near, x_far))
    second_a = jnp.concatenate([dense_weight, expand_weight], axis=1)
    x_beside = jnp.where(native, x_near, x_far)
    x_last = wires.core(x_beside)
    a_swapped = wires.half(since(second_a, x_beside))
    stacks = project(1, info, x_beside, x_last, qkv_full, gb, tables, stacks)
    stacks, a_swapped = at((stacks, a_swapped))
    normalized, queries, keys, values = stacks

    b_swapped = wires.half(since(shrink_weight, a_swapped))
    a_both = swap_weights(second_a, a_swapped)
    a_near = wires.gather_near(a_both)
    out_0, queries_0 = attend(info, queries, keys, values, 0, 2, after=(a_both,))
    out_0, a_near, b_swapped = at((out_0, a_near, b_swapped))
    b_both = swap_weights(shrink_weight, b_swapped)
    a_parts = wires.gather_far(a_near)
    b_near = wires.gather_near(b_both)
    g_swapped = wires.regroup(since(cotangent, b_swapped))
    g_near = wires.near(since(cotangent, b_swapped), True)
    out_1, queries_1 = attend(info, queries, keys, values, 1, 2, after=(out_0, b_both))
    out_1, a_parts, b_near = at((out_1, a_parts, b_near))
    b_parts = wires.gather_far(b_near)
    widths = (dense_weight.shape[1], expand_weight.shape[1], shrink_weight.shape[1])
    dense_full, expand_full = assemble_second(info, a_parts, pairs, widths[:2])
    dense_full, expand_full, b_parts = at((dense_full, expand_full, b_parts))
    (shrink_full,) = assemble_second(info, b_parts, pairs, widths[2:])
    shrink_full, g_swapped, g_near = at((shrink_full, g_swapped, g_near))
    g_far = wires.near(g_swapped, False)
    g_mine = jnp.where(native, cotangent, g_swapped)
    g_core = wires.core(g_mine)
    results = feed(normalized, (out_0, out_1), dense_full, expand_full, shrink_full, gb, after=(g_mine,))
    results, g_near, g_far, g_core = at((results, g_near, g_far, g_core))
    *branches, activated, slope = results
    g_beside = jnp.where(native, g_near, g_far)
    g_parts = [g_mine, g_beside, g_core, wires.core(g_beside)]

    branch = core_sum(branches)
    passed = branch[1].astype(BF16)
    branch_far = wires.near(passed, False)
    branch_near = wires.near(passed, True)
    results = feed_back(
        normalized, activated, slope, g_parts, (out_0, out_1), dense_full, expand_full, shrink_full, gb, after=(passed,)
    )
    results, branch_far, branch_near = at((results, branch_far, branch_near))
    second_e, *grads, feed_grads = results

    turns = tables[0]
    feed_both = lax.psum_scatter(feed_grads, "pair", scatter_dimension=0, tiled=True)
    branch_sent = (branch[0] + branch_far.astype(F32)).astype(BF16)
    branch_back = wires.regroup(branch_sent)
    pg_0, *rests_0 = attend_back(info, queries_0, grads[0], keys, values, turns, 0, after=(branch_sent,))
    pg_0, rests_0, branch_back = at((pg_0, rests_0, branch_back))
    pg_1, *rests_1 = attend_back(info, queries_1, grads[1], keys, values, turns, 1, after=(pg_0,))
    results = project_back(info, (pg_0, pg_1), normalized, second_e, qkv_full, gb, pairs)
    results = at(results)
    e_swapped, *so_far = results

    e_core = wires.core_from(e_swapped, True)
    e_swapped = e_swapped.astype(F32) + e_core.astype(F32)
    e_passed = e_swapped[1].astype(BF16)
    e_far = wires.near(e_passed, False)
    (pg_0,) = attend_back(info, queries_0, grads[0], keys, values, turns, 0, rests_0, after=(e_passed, *so_far))
    pg_0, e_far = at((pg_0, e_far))
    e_sent = (e_swapped[0] + e_far.astype(F32)).astype(BF16)
    e_back = wires.regroup(e_sent)
    (pg_1,) = attend_back(info, queries_1, grads[1], keys, values, turns, 1, rests_1, after=(pg_0, e_sent))
    pg_1, feed_both = at((pg_1, feed_both))
    feed_both = feed_both.reshape(2, qkv_weight.shape[0], -1)
    feed_both = jnp.where(core == 0, feed_both, feed_both[::-1])
    feed_mine, feed_sent = swap_grads(feed_both)
    feed_arrived = wires.half(feed_sent)
    results = project_back(
        info, (pg_0, pg_1), normalized, second_e, qkv_full, gb, pairs, so_far, after=(feed_sent,)
    )
    results, e_back = at((results, e_back))
    e_native, *qkv_grads = results
    e_core = wires.core_from(e_native, False)
    qkv_near = wires.scatter_direct(qkv_grads)
    e_sum = e_native.astype(F32) + e_core.astype(F32)
    e_passed = e_sum[1].astype(BF16)
    e_near = wires.near(e_passed, True)
    qkv_near, feed_arrived = since((qkv_near, feed_arrived), e_passed)
    rows_f32 = inputs.astype(F32)
    layer_out = jnp.where(native, branch[0] + branch_near.astype(F32), branch_back.astype(F32))
    layer_out = (rows_f32 + layer_out).astype(BF16)
    feed_total = feed_mine.astype(F32) + feed_arrived.astype(F32)
    qkv_both = sum(part.astype(F32) for part in (qkv_grads[0], *qkv_near)).astype(BF16)
    qkv_mine, qkv_sent = swap_grads(qkv_both)
    smalls = jnp.concatenate([qkv_mine[:, -LANES:], feed_mine[:, -LANES:]], axis=1)
    smalls = since(smalls, e_near)
    qkv_total = qkv_mine.astype(F32) + wires.half(since(qkv_sent, e_near)).astype(F32)
    arrived = wires.near_all(smalls).astype(F32) + wires.across(smalls).astype(F32)
    attention_norm_grad = (qkv_total[:, -LANES:] + arrived[:, :LANES])[:, :8].T[:2]
    feedforward_norm_grad = (feed_total[:, -LANES:] + arrived[:, LANES:])[:, :8].T[:2]
    e = jnp.where(native, e_sum[0] + e_near.astype(F32), e_back.astype(F32))

    centered = rows_f32 - jnp.mean(rows_f32, axis=-1, keepdims=True)
    inv_scale = lax.rsqrt(jnp.mean(centered * centered, axis=-1, keepdims=True) + EPSILON)
    normalized = centered * inv_scale
    input_grad = cotangent.astype(F32) + inv_scale * (
        e - jnp.mean(e, axis=-1, keepdims=True) - normalized * jnp.mean(e * normalized, axis=-1, keepdims=True)
    )
    return (
        layer_out,
        input_grad,
        qkv_total[:, :-LANES],
        feed_total[:, : widths[0]],
        feed_total[:, widths[0] : widths[0] + widths[1]],
        feed_total[:, widths[0] + widths[1] : -LANES],
        attention_norm_grad,
        feedforward_norm_grad,
    )


def solution(mesh):
    dp, tensor = mesh.shape["dp"], mesh.shape["tensor"]
    fine = Mesh(mesh.devices.reshape(dp // 2, 2, 2, tensor // 2), AXES)
    data, split = ("pair", "core"), ("half", "m")
    tokens, weight, norm = P(AXES, None), P(data, split), P(None, data)
    return jax.shard_map(
        partial(on_device, fine),
        mesh=fine,
        in_specs=(tokens, weight, weight, weight, weight, norm, norm, tokens, P(data)),
        out_specs=(tokens, tokens, weight, weight, weight, weight, norm, norm),
        check_vma=False,
    )
```

```python
from functools import partial

import jax
import jax.numpy as jnp
from jax import lax
from jax.experimental import pallas as pl
from jax.experimental.pallas import tpu as pltpu
from jax.sharding import Mesh
from jax.sharding import PartitionSpec as P

HD = 64
ROT = 16
L = 2048
LANES = 128
EPSILON = 1e-05
MASKED = -1e30
AXES = ("pair", "core", "half", "m")
PIECES = 4
PIECE = L // PIECES
SEG_LANE = 64
DOCS = 5
LSE_LANE = SEG_LANE + DOCS
DELTA_LANE = 64
MIB = 1024 * 1024
F32 = jnp.float32
BF16 = jnp.bfloat16


def dot_nn(left, right):
    return lax.dot_general(left, right, (((1,), (0,)), ((), ())), preferred_element_type=F32)


def dot_nt(left, right):
    return lax.dot_general(left, right, (((1,), (1,)), ((), ())), preferred_element_type=F32)


def dot_tn(left, right):
    return lax.dot_general(left, right, (((0,), (0,)), ((), ())), preferred_element_type=F32)


def lanes_of(shape):
    return lax.broadcasted_iota(jnp.int32, shape, len(shape) - 1)


def rows_of(shape):
    return lax.broadcasted_iota(jnp.int32, shape, len(shape) - 2)


def normalize(x):
    rows = x.astype(F32)
    centered = rows - jnp.mean(rows, axis=-1, keepdims=True)
    return centered * lax.rsqrt(jnp.mean(centered * centered, axis=-1, keepdims=True) + EPSILON)


def split3(column):
    high = column.astype(BF16).astype(F32)
    rest = column - high
    middle = rest.astype(BF16).astype(F32)
    return high, middle, rest - middle


def with_lanes(base, first, columns):
    lane = lanes_of(base.shape)
    for offset, column in enumerate(columns):
        base = jnp.where(lane == first + offset, column, base)
    return base


def params():
    return pltpu.CompilerParams(vmem_limit_bytes=60 * MIB)


def fenced(kernel, inputs, after):
    return lambda *refs: kernel(*refs[:inputs], *refs[inputs + after :])


ANYWHERE = pl.BlockSpec(memory_space=pl.ANY)


def whole(shape, **kw):
    return pl.BlockSpec(shape, lambda *_: (0,) * len(shape), **kw)


def once(shape):
    return whole(shape, pipeline_mode=pl.Buffered(1))


def cost(flops, nbytes, trans=0):
    return pl.CostEstimate(flops=int(flops) // 256, bytes_accessed=int(nbytes) // 256, transcendentals=int(trans) // 256)


def hops(pairs):
    near = [0] + [1 << b for b in range(pairs.bit_length() - 1)]
    far = sorted((j for j in range(pairs) if j not in near), key=lambda j: (j.bit_count(), j))
    return near, far


def block_places(info_ref, pairs, rows):
    near, far = hops(pairs)
    return pair_places(info_ref, near + far, rows)


def pair_places(info_ref, order, rows):
    core, pair = info_ref[1], info_ref[2]
    for j in order:
        base = (pair ^ j) * 2
        yield pl.multiple_of((base + core) * rows, rows), pl.multiple_of((base + 1 - core) * rows, rows)


def block_refs(refs, pairs):
    near, far = hops(pairs)
    refs = list(refs)
    for _ in near:
        both = refs.pop(0)
        yield both.at[0], both.at[1]
    for _ in far:
        yield refs.pop(0), refs.pop(0)


def block_shapes(pairs, rows, width):
    near, far = hops(pairs)
    return [(2, rows, width)] * len(near) + [(rows, width)] * (2 * len(far))


def assemble_first_kernel(pairs, rows, width, info_ref, *refs):
    weight_ref, gb_ref, small = refs[-3:]
    for offs, both in zip(pair_places(info_ref, range(pairs), rows), refs[:-3]):
        for off, part in zip(offs, (both.at[0], both.at[1])):
            weight_ref[pl.ds(off, rows), :] = part[:, :width]
            small[pl.ds(off, rows), :] = part[:, width:].astype(F32)
    gb_ref[...] = small[...].T[:8, :]


def assemble_first(info, parts, pairs, width):
    rows = parts[0].shape[1]
    feats = pairs * 2 * rows
    return pl.pallas_call(
        partial(assemble_first_kernel, pairs, rows, width),
        out_shape=(jax.ShapeDtypeStruct((feats, width), BF16), jax.ShapeDtypeStruct((8, feats), F32)),
        in_specs=[pl.BlockSpec(memory_space=pltpu.SMEM)] + [pl.BlockSpec(memory_space=pltpu.VMEM)] * len(parts),
        scratch_shapes=[pltpu.VMEM((feats, LANES), F32)],
        compiler_params=params(),
        cost_estimate=cost(0, 4 * feats * width),
        name="assemble_qkv",
    )(info, *parts)


def assemble_second_kernel(pairs, rows, widths, info_ref, *refs):
    outs = refs[-len(widths) :]
    for offs, parts in zip(block_places(info_ref, pairs, rows), block_refs(refs[: -len(widths)], pairs)):
        for off, part in zip(offs, parts):
            start = 0
            for out, width in zip(outs, widths):
                out[pl.ds(off, rows), :] = part[:, start : start + width]
                start += width


def assemble_second(info, parts, pairs, widths):
    rows = parts[0].shape[1]
    feats = pairs * 2 * rows
    return pl.pallas_call(
        partial(assemble_second_kernel, pairs, rows, widths),
        out_shape=tuple(jax.ShapeDtypeStruct((feats, w), BF16) for w in widths),
        in_specs=[pl.BlockSpec(memory_space=pltpu.SMEM)] + [pl.BlockSpec(memory_space=pltpu.VMEM)] * len(parts),
        compiler_params=params(),
        cost_estimate=cost(0, 4 * feats * sum(widths)),
        name="assemble_ffn",
    )(info, *parts)


def turn(values, cosine, sine_up, sine_down):
    return (
        values * cosine
        + pltpu.roll(values, ROT // 2, 1) * sine_up
        + pltpu.roll(values, LANES - ROT // 2, 1) * sine_down
    )


def project_kernel(heads, info_ref, xa_ref, xb_ref, w_ref, gb_ref, turn_ref, feature_ref, *refs):
    n_ref, q_ref, k_ref, v_ref = refs[-4:]
    first_piece = pl.program_id(0) < pl.num_programs(0) // 2
    normalized = normalize(jnp.where(first_piece, xa_ref[...], xb_ref[...]))
    n_ref[0] = normalized
    first = (normalized * gb_ref[0:1, :] + gb_ref[2:3, :]).astype(BF16)
    projected = dot_nn(first, w_ref[...])
    cosine, up, down = (turn_ref[:, n * LANES : (n + 1) * LANES] for n in range(3))
    query_feature, key_feature = (feature_ref[:, n * LANES : (n + 1) * LANES].astype(F32) for n in range(2))
    lane = lanes_of(cosine.shape)
    low = lane < HD
    value_feature = ((lane >= DELTA_LANE) & (lane < DELTA_LANE + 3)).astype(F32)

    def part(offset):
        tile = projected[:, offset // LANES * LANES : offset // LANES * LANES + LANES]
        return pltpu.roll(tile, HD, 1) if offset % LANES else tile

    for h in range(heads):
        sl = slice(h * LANES, (h + 1) * LANES)
        base = h * 3 * HD
        query = turn(part(base), cosine, up, down) * HD ** (-0.5)
        key = turn(part(base + HD), cosine, up, down)
        q_ref[0, :, sl] = jnp.where(low, query, query_feature).astype(BF16)
        k_ref[0, :, sl] = jnp.where(low, key, key_feature).astype(BF16)
        v_ref[0, :, sl] = jnp.where(low, part(base + 2 * HD), value_feature).astype(BF16)


def project(r, info, xa, xb, weight, gb, tables, stacks, after=(), block=256):
    feats, width = weight.shape
    heads = width // (3 * HD)
    steps = PIECE // block
    shapes = [(PIECES, PIECE, feats)] + [(PIECES, PIECE, heads * LANES)] * 3
    kinds = [F32, BF16, BF16, BF16]
    piece = lambda i: r + 2 * (i // steps)
    table = lambda n: pl.BlockSpec((block, n * LANES), lambda i, info: ((info[0] ^ piece(i)) * steps + i % steps, 0))
    inputs = [info, xa, xb, weight, gb, *tables]
    return pl.pallas_call(
        partial(project_kernel, heads),
        grid_spec=pltpu.PrefetchScalarGridSpec(
            num_scalar_prefetch=1,
            grid=(2 * steps,),
            in_specs=[
                pl.BlockSpec((block, feats), lambda i, info: (jnp.minimum(i, steps - 1), 0)),
                pl.BlockSpec((block, feats), lambda i, info: (jnp.maximum(i - steps, 0), 0)),
                once((feats, width)),
                once((8, feats)),
                table(3),
                table(2),
            ]
            + [ANYWHERE] * (len(stacks) + len(after)),
            out_specs=[pl.BlockSpec((1, block, s[2]), lambda i, info: (piece(i), i % steps, 0)) for s in shapes],
        ),
        out_shape=[jax.ShapeDtypeStruct(s, kind) for s, kind in zip(shapes, kinds)],
        input_output_aliases={len(inputs) + n: n for n in range(len(stacks))},
        compiler_params=params(),
        cost_estimate=cost(4 * PIECE * feats * width, 2 * (feats * width + 12 * PIECE * feats)),
        name=f"project_{r}",
    )(*inputs, *stacks, *after)


def attend_kernel(heads, info_ref, q_ref, k_ref, v_ref, o_ref, qb_ref):
    me = info_ref[0]
    causal = lanes_of((PIECE, PIECE)) <= rows_of((PIECE, PIECE))
    low = lanes_of((PIECE, LANES)) < HD
    at = [pl.multiple_of((me ^ p) * PIECE, PIECE) for p in range(PIECES)]
    for i in range(PIECES):
        rows = pl.ds(at[i], PIECE)
        outs = []
        for h in range(heads):
            sl = slice(h * LANES, (h + 1) * LANES)
            query = q_ref[rows, sl]
            scores = [dot_nt(query, k_ref[pl.ds(at[j], PIECE), sl]) for j in range(i + 1)]
            scores[-1] = jnp.where(causal, scores[-1], MASKED)
            top = jnp.max(scores[0], axis=-1, keepdims=True)
            for s in scores[1:]:
                top = jnp.maximum(top, jnp.max(s, axis=-1, keepdims=True))
            out = total = None
            for j, s in enumerate(scores):
                weight = jnp.exp(s - top)
                part = jnp.sum(weight, axis=-1, keepdims=True)
                term = dot_nn(weight.astype(BF16), v_ref[pl.ds(at[j], PIECE), sl])
                total = part if total is None else total + part
                out = term if out is None else out + term
            outs.append(out * (1.0 / total))
            log_total = split3(top + jnp.log(total))
            qb_ref[rows, sl] = with_lanes(query.astype(F32), LSE_LANE, [-c for c in log_total]).astype(BF16)
        for h in range(0, heads, 2):
            o_ref[rows, h * HD : h * HD + LANES] = jnp.where(low, outs[h], pltpu.roll(outs[h + 1], HD, 1))


def attend(info, queries, keys, values, group, heads, after=()):
    full = queries.shape[2]
    width = heads * LANES
    own = pl.BlockSpec((L, width), lambda i, info: (0, group))
    return pl.pallas_call(
        fenced(partial(attend_kernel, heads), 4, len(after)),
        grid_spec=pltpu.PrefetchScalarGridSpec(
            num_scalar_prefetch=1,
            grid=(1,),
            in_specs=[own] * 3 + [ANYWHERE] * len(after),
            out_specs=[whole((L, heads * HD)), whole((L, width))],
        ),
        out_shape=[jax.ShapeDtypeStruct((L, heads * HD), F32), jax.ShapeDtypeStruct((L, width), BF16)],
        compiler_params=params(),
        cost_estimate=cost(heads * L * L * LANES * 4, 5 * L * width, heads * L * L // 2),
        name=f"attention_forward_{group}",
    )(info, *(a.reshape(L, full) for a in (queries, keys, values)), *after)


def gelu_parts(h):
    bell = jnp.exp2(h * h * (-0.5 * 1.4426950408889634))
    t = pl.reciprocal(1.0 + (0.3275911 * 0.5**0.5) * jnp.abs(h))
    poly = t * (
        0.127414796 + t * (-0.142248368 + t * (0.7107068705 + t * (-0.7265760135 + t * 0.5307027145)))
    )
    tail = poly * bell
    return jnp.where(h < 0, tail, 1.0 - tail), bell * 0.3989422804014327


def norm_columns(sums_ref):
    wide = jnp.concatenate([sums_ref[...], jnp.zeros((LANES - 8, sums_ref.shape[1]), F32)], axis=0)
    return wide.T


def write_parts(info_ref, total, small, refs):
    width, rows = total.shape[1], refs[0].shape[1]
    for offs, both in zip(pair_places(info_ref, range(len(refs)), rows), refs):
        for n, off in enumerate(offs):
            both[n, :, :width] = total[pl.ds(off, rows), :].astype(BF16)
            both[n, :, width:] = small[pl.ds(off, rows), :].astype(BF16)


def feed_kernel(groups, parts, n_ref, *refs):
    o_refs, refs = refs[:groups], refs[groups:]
    wd_ref, we_ref, ws_ref, gb_ref, br01_ref, br23_ref, activated_ref, slope_ref, b_now = refs
    step = pl.program_id(0)
    rows = PIECE // parts
    for n in range(parts):
        sl = slice(n * rows, (n + 1) * rows)
        second = (n_ref[sl, :] * gb_ref[1:2, :] + gb_ref[3:4, :]).astype(BF16)
        hidden = dot_nn(second, we_ref[...])
        cdf, density = gelu_parts(hidden)
        activated = (hidden * cdf).astype(BF16)
        activated_ref[sl, :] = activated
        slope_ref[sl, :] = cdf + hidden * density
        attended = jnp.concatenate([o[sl, :] for o in o_refs], axis=1).astype(BF16)
        b_now[sl, :] = (dot_nt(attended, wd_ref[...]) + dot_nt(activated, ws_ref[...])).astype(BF16)

    @pl.when(step < 2)
    def _():
        br01_ref[0] = b_now[...]

    @pl.when(step >= 2)
    def _():
        br23_ref[0] = b_now[...]


def feed(normalized, outs, wd, we, ws, gb, after=(), parts=1):
    feats, hidden = we.shape
    two = (2, PIECE, feats)
    by_step = lambda i: (i, 0)
    inputs = [normalized.reshape(L, feats), *outs, wd, we, ws, gb]
    return pl.pallas_call(
        fenced(partial(feed_kernel, len(outs), parts), len(inputs), len(after)),
        grid=(PIECES,),
        in_specs=[pl.BlockSpec((PIECE, feats), by_step)]
        + [pl.BlockSpec((PIECE, o.shape[1]), by_step) for o in outs]
        + [once(w.shape) for w in (wd, we, ws, gb)]
        + [ANYWHERE] * len(after),
        out_specs=[
            pl.BlockSpec((1, PIECE, feats), lambda i: (jnp.minimum(i, 1), 0, 0)),
            pl.BlockSpec((1, PIECE, feats), lambda i: (jnp.maximum(i - 2, 0), 0, 0)),
            pl.BlockSpec((PIECE, hidden), by_step),
            pl.BlockSpec((PIECE, hidden), by_step),
        ],
        out_shape=[jax.ShapeDtypeStruct(two, BF16)] * 2
        + [jax.ShapeDtypeStruct((L, hidden), BF16), jax.ShapeDtypeStruct((L, hidden), F32)],
        scratch_shapes=[pltpu.VMEM((PIECE, feats), BF16)],
        compiler_params=params(),
        cost_estimate=cost(4 * L * feats * hidden, 16 * L * feats),
        name="feed_forward",
    )(*inputs, *after)


def feed_back_kernel(heads, group, n_ref, activated_ref, slope_ref, *refs):
    groups = heads // group
    g_refs, refs = refs[:PIECES], refs[PIECES:]
    o_refs, refs = refs[:groups], refs[groups:]
    (wd_ref, we_ref, ws_ref, gb_ref, sg_ref), refs = refs[:5], refs[5:]
    doa_refs, refs = refs[:groups], refs[groups:]
    grads_ref, g_now, gd, ge, gs, sums = refs
    step, last = pl.program_id(0), pl.num_programs(0) - 1

    @pl.when(step == 0)
    def _():
        for total in (gd, ge, gs, sums):
            total[...] = jnp.zeros_like(total)

    for r in range(PIECES):

        @pl.when(step == r)
        def _():
            g_now[...] = g_refs[r][...]

    g = g_now[...]
    hidden_grad = (dot_nn(g, ws_ref[...]) * slope_ref[...]).astype(BF16)
    normalized = n_ref[...]
    second = (normalized * gb_ref[1:2, :] + gb_ref[3:4, :]).astype(BF16)
    out = jnp.concatenate([o[...] for o in o_refs], axis=1)
    gs[...] += dot_tn(g, activated_ref[...])
    gd[...] += dot_tn(g, out.astype(BF16))
    ge[...] += dot_tn(second, hidden_grad)
    second_grad = dot_nt(hidden_grad, we_ref[...])
    sg_ref[...] = second_grad * gb_ref[1:2, :]
    sums[0:1, :] += jnp.sum(second_grad * normalized, axis=0, keepdims=True)
    sums[1:2, :] += jnp.sum(second_grad, axis=0, keepdims=True)
    attended_grad = dot_nn(g, wd_ref[...]).astype(BF16).astype(F32)
    product = attended_grad * out
    lane = lanes_of((PIECE, LANES))
    for h in range(heads):
        tile = slice(h // 2 * LANES, (h // 2 + 1) * LANES)
        mine = (lane < HD) if h % 2 == 0 else (lane >= HD)
        delta = split3(jnp.sum(jnp.where(mine, product[:, tile], 0.0), axis=-1, keepdims=True))
        grad = attended_grad[:, tile]
        if h % 2:
            grad = pltpu.roll(grad, HD, 1)
        grad = jnp.where(lane < HD, grad, 0.0)
        start = h % group * LANES
        doa_refs[h // group][:, start : start + LANES] = with_lanes(grad, DELTA_LANE, [-c for c in delta]).astype(BF16)

    @pl.when(step == last)
    def _():
        start = 0
        for total in (gd, ge, gs):
            grads_ref[:, start : start + total.shape[1]] = total[...].astype(BF16)
            start += total.shape[1]
        grads_ref[:, start:] = norm_columns(sums).astype(BF16)


def feed_back(normalized, activated, slope, g_parts, outs, wd, we, ws, gb, after=()):
    feats, hidden = we.shape
    heads = wd.shape[1] // HD
    group = heads // len(outs)
    width = wd.shape[1] + 2 * hidden + LANES
    by_step = lambda i: (i, 0)
    step = lambda w: pl.BlockSpec((PIECE, w), by_step)
    inputs = [normalized.reshape(L, feats), activated, slope, *g_parts, *outs, wd, we, ws, gb]
    return pl.pallas_call(
        fenced(partial(feed_back_kernel, heads, group), len(inputs), len(after)),
        grid=(PIECES,),
        in_specs=[step(feats), step(hidden), step(hidden)]
        + [once((PIECE, feats))] * PIECES
        + [step(group * HD)] * len(outs)
        + [once(w.shape) for w in (wd, we, ws, gb)]
        + [ANYWHERE] * len(after),
        out_specs=[step(feats)] + [step(group * LANES)] * len(outs) + [once((feats, width))],
        out_shape=[jax.ShapeDtypeStruct((L, feats), F32)]
        + [jax.ShapeDtypeStruct((L, group * LANES), BF16)] * len(outs)
        + [jax.ShapeDtypeStruct((feats, width), BF16)],
        scratch_shapes=[
            pltpu.VMEM((PIECE, feats), BF16),
            pltpu.VMEM(wd.shape, F32),
            pltpu.VMEM(we.shape, F32),
            pltpu.VMEM(ws.shape, F32),
            pltpu.VMEM((8, feats), F32),
        ],
        compiler_params=params(),
        cost_estimate=cost(8 * L * feats * hidden, 20 * L * feats),
        name="feed_back",
    )(*inputs, *after)


def block_back(query, grad, key, value, causal):
    scores = dot_nt(key, query)
    if causal is not None:
        scores = jnp.where(causal, scores, MASKED)
    probs = jnp.exp(scores)
    score_grad = (probs * dot_nt(value, grad)).astype(BF16)
    return dot_tn(score_grad, key), dot_nn(score_grad, query), dot_nn(probs.astype(BF16), grad)


def triangle_back(load, base, sums, h, causal):
    q0, g0, k0, v0 = load(base)
    q1, g1, k1, v1 = load(base + 1)
    low = block_back(q0, g0, k0, v0, causal)
    side = block_back(q1, g1, k0, v0, None)
    high = block_back(q1, g1, k1, v1, causal)
    dq, dk, dv = sums
    dq[h, base] += low[0]
    dq[h, base + 1] += side[0] + high[0]
    for d, n in ((dk, 1), (dv, 2)):
        d[h, base] += low[n] + side[n]
        d[h, base + 1] += high[n]


def finish_back(pg_ref, tables_ref, table_row, sums, base, near, heads):
    low = lanes_of((PIECE, LANES)) < HD
    dq, dk, dv = sums
    for n in range(2):
        rows = pl.ds(pl.multiple_of(table_row + n * PIECE, PIECE), PIECE)
        cosine = tables_ref[rows, :LANES]
        up, down = -tables_ref[rows, LANES : 2 * LANES], -tables_ref[rows, 2 * LANES :]
        for h in range(0, heads, 2):
            start = h // 2 * 3 * LANES
            q0, q1 = (turn(dq[h + x, base + n] * HD ** (-0.5), cosine, up, down) for x in (0, 1))
            k0, k1 = (turn(dk[h + x, base + n], cosine, up, down) for x in (0, 1))
            v0, v1 = dv[h, base + n], dv[h + 1, base + n]
            for tile, (left, right) in enumerate(((q0, k0), (v0, q1), (k1, v1))):
                pg_ref[near ^ n, :, start + tile * LANES : start + (tile + 1) * LANES] = jnp.where(
                    low, left, pltpu.roll(right, HD, 1)
                ).astype(BF16)


def attend_back_first_kernel(info_ref, q_ref, do_ref, k_ref, v_ref, tables_ref, pg_ref, *refs):
    rests, sums = refs[:3], refs[3:]
    dq, dk, dv = sums
    me, half = info_ref[0], info_ref[3]
    heads = q_ref.shape[1] // LANES
    causal = rows_of((PIECE, PIECE)) <= lanes_of((PIECE, PIECE))
    swapped, native = 2 * (1 - half), 2 * half
    zero = jnp.zeros((PIECE, LANES), F32)
    for h in range(heads):
        sl = slice(h * LANES, (h + 1) * LANES)

        def load(piece):
            rows = pl.ds(pl.multiple_of((me ^ piece) * PIECE, PIECE), PIECE)
            return q_ref[rows, sl], do_ref[rows, sl], k_ref[rows, sl], v_ref[rows, sl]

        pieces = [load(p) for p in range(PIECES)]
        terms = {
            (i, j): block_back(*pieces[i][:2], *pieces[j][2:], None) for j in (0, 1) for i in (2, 3)
        }
        for p in (0, 1):
            dq[h, p] = zero
            dq[h, p + 2] = terms[p + 2, 0][0] + terms[p + 2, 1][0]
            for d, n in ((dk, 1), (dv, 2)):
                d[h, p] = terms[2, p][n] + terms[3, p][n]
                d[h, p + 2] = zero
        triangle_back(load, swapped, sums, h, causal)
        for rest, d in zip(rests, sums):
            for n in range(2):
                rest[h, n] = d[h, native + n]
    finish_back(pg_ref, tables_ref, swapped * PIECE, sums, swapped, me % 2, heads)


def attend_back_second_kernel(info_ref, q_ref, do_ref, k_ref, v_ref, tables_ref, *refs):
    rests, pg_ref, sums = refs[:3], refs[3], refs[4:]
    near = info_ref[0] % 2
    heads = q_ref.shape[1] // LANES
    causal = rows_of((PIECE, PIECE)) <= lanes_of((PIECE, PIECE))
    for h in range(heads):
        sl = slice(h * LANES, (h + 1) * LANES)

        def load(piece):
            rows = pl.ds(pl.multiple_of((near ^ piece) * PIECE, PIECE), PIECE)
            return q_ref[rows, sl], do_ref[rows, sl], k_ref[rows, sl], v_ref[rows, sl]

        for rest, d in zip(rests, sums):
            for n in range(2):
                d[h, n] = rest[h, n]
        triangle_back(load, 0, sums, h, causal)
    finish_back(pg_ref, tables_ref, 0, sums, 0, near, heads)


def attend_back(info, queries, grads, keys, values, tables, group, rests=(), after=()):
    width, full = queries.shape[1], keys.shape[2]
    heads = width // LANES
    rest = (heads, 2, PIECE, LANES)
    pg = (2, PIECE, heads * 3 * HD)
    first = not rests
    rows = L if first else L // 2
    place = (lambda info: 0) if first else (lambda info: info[1] ^ info[3])
    own = pl.BlockSpec((rows, width), lambda s, info: (place(info), 0))
    shared = pl.BlockSpec((rows, width), lambda s, info: (place(info), group))
    table = pl.BlockSpec((rows, 3 * LANES), lambda s, info: (0 if first else info[3], 0))
    inputs = [info, queries, grads, keys.reshape(L, full), values.reshape(L, full), tables, *rests]
    blocks = 7 if first else 3
    return pl.pallas_call(
        fenced(attend_back_first_kernel if first else attend_back_second_kernel, len(inputs), len(after)),
        grid_spec=pltpu.PrefetchScalarGridSpec(
            num_scalar_prefetch=1,
            grid=(1,),
            in_specs=[own, own, shared, shared, table] + [whole(rest)] * len(rests) + [ANYWHERE] * len(after),
            out_specs=[whole(pg)] + [whole(rest)] * (3 if first else 0),
            scratch_shapes=[pltpu.VMEM((heads, PIECES if first else 2, PIECE, LANES), F32)] * 3,
        ),
        out_shape=[jax.ShapeDtypeStruct(pg, BF16)] + [jax.ShapeDtypeStruct(rest, F32)] * (3 if first else 0),
        compiler_params=params(),
        cost_estimate=cost(blocks * heads * PIECE * PIECE * LANES * 10, 12 * L * width, blocks * heads * PIECE * PIECE),
        name=f"attention_backward_{group}" + ("a" if first else "b"),
    )(*inputs, *after)


def project_back_kernel(pairs, groups, final, info_ref, *refs):
    pg_refs, refs = refs[:groups], refs[groups:]
    (n_ref, sg_ref, w_ref, gb_ref), refs = refs[:4], refs[4:]
    if final:
        (gq_in, sums_in, e_ref), refs = refs[:3], refs[3:]
        *part_refs, gq, sums, small = refs
    else:
        e_ref, gq, sums = refs
    step, last = pl.program_id(0), pl.num_programs(0) - 1

    @pl.when(step == 0)
    def _():
        gq[...] = gq_in[...] if final else jnp.zeros_like(gq)
        sums[...] = sums_in[...] if final else jnp.zeros_like(sums)

    normalized = n_ref[0]
    first = (normalized * gb_ref[0:1, :] + gb_ref[2:3, :]).astype(BF16)
    grad = jnp.concatenate([pg[0] for pg in pg_refs], axis=1)
    first_grad = dot_nt(grad, w_ref[...])
    gq[...] += dot_tn(first, grad)
    e_ref[0] = (first_grad * gb_ref[0:1, :] + sg_ref[0]).astype(BF16)
    sums[0:1, :] += jnp.sum(first_grad * normalized, axis=0, keepdims=True)
    sums[1:2, :] += jnp.sum(first_grad, axis=0, keepdims=True)
    if final:

        @pl.when(step == last)
        def _():
            small[...] = norm_columns(sums)
            write_parts(info_ref, gq, small, part_refs)


def project_back(info, pgs, normalized, sg, weight, gb, pairs, so_far=(), after=()):
    feats, width = weight.shape
    final = bool(so_far)
    swapped = 0 if final else 1
    sums = (8, feats)
    shapes = [(2, feats // (2 * pairs), width + LANES)] * pairs if final else []
    two = (2, PIECE, feats)
    by_step = lambda i, info: (i, 0, 0)
    relative = pl.BlockSpec((1, PIECE, feats), lambda i, info: (2 * (info[1] ^ info[3] ^ swapped) + i, 0, 0))
    inputs = [info, *pgs, normalized, sg.reshape(PIECES, PIECE, feats), weight, gb, *so_far]
    totals = [pltpu.VMEM(weight.shape, F32), pltpu.VMEM(sums, F32)]
    results = [(two, BF16)] + ([(s, BF16) for s in shapes] if final else [(weight.shape, F32), (sums, F32)])
    return pl.pallas_call(
        fenced(partial(project_back_kernel, pairs, len(pgs), final), len(inputs), len(after)),
        grid_spec=pltpu.PrefetchScalarGridSpec(
            num_scalar_prefetch=1,
            grid=(2,),
            in_specs=[pl.BlockSpec((1, PIECE, pg.shape[2]), by_step) for pg in pgs]
            + [relative, relative]
            + [once(a.shape) for a in (weight, gb, *so_far)]
            + [ANYWHERE] * len(after),
            out_specs=[pl.BlockSpec((1, PIECE, feats), by_step)] + [once(s) for s, _ in results[1:]],
            scratch_shapes=totals + [pltpu.VMEM((feats, LANES), F32)] if final else [],
        ),
        out_shape=[jax.ShapeDtypeStruct(s, kind) for s, kind in results],
        compiler_params=params(),
        cost_estimate=cost(2 * L * feats * width, 6 * L * feats),
        name="project_back_" + ("b" if final else "a"),
    )(*inputs, *after)


def build_tables(segments):
    places = jnp.arange(L, dtype=jnp.int32)
    starts = jnp.zeros_like(segments)
    for value in range(DOCS):
        starts = starts + jnp.where(segments > value, jnp.sum((segments == value).astype(jnp.int32)), 0)
    position = (places - starts).astype(F32)
    lane = jnp.arange(LANES, dtype=jnp.int32)
    inner = lane % HD
    half = ROT // 2
    frequency = 10000.0 ** (-((inner % half).astype(F32) * 2.0 / ROT))
    angles = position[:, None] * frequency[None, :]
    turned = (inner < ROT)[None, :]
    sine = jnp.sin(angles)
    cosine = jnp.where(turned, jnp.cos(angles), 1.0)
    up = jnp.where(turned & (inner >= half)[None, :], sine, 0.0)
    down = jnp.where((inner < half)[None, :], -sine, 0.0)
    feature = lane - SEG_LANE
    is_doc = ((feature >= 0) & (feature < DOCS))[None, :]
    same = segments[:, None] == feature[None, :]
    one = ((lane >= LSE_LANE) & (lane < LSE_LANE + 3))[None, :]
    query_feature = jnp.where(is_doc & ~same, MASKED, 0.0)
    key_feature = jnp.where((is_doc & same) | one, 1.0, 0.0)
    features = jnp.concatenate([query_feature, key_feature], axis=1).astype(BF16)
    return jnp.concatenate([cosine, up, down], axis=1), features


class Wires:
    def __init__(self, mesh):
        self.pairs = mesh.shape["pair"]
        self.sizes = [mesh.shape[a] for a in AXES]

    def send(self, array, target):
        _, cores, halves, ms = self.sizes

        def index(k, c, h, m):
            return ((k * cores + c) * halves + h) * ms + m

        moves = []
        for k in range(self.pairs):
            for c in range(cores):
                for h in range(halves):
                    for m in range(ms):
                        there = target(k, c, h, m)
                        if there is not None:
                            moves.append((index(k, c, h, m), index(*there)))
        return lax.ppermute(array, AXES, moves)

    def core(self, array):
        return self.send(array, lambda k, c, h, m: (k, 1 - c, h, m))

    def near(self, array, native):
        return self.send(array, lambda k, c, h, m: (k, c, h, 1 - m) if (c == h) == native else None)

    def core_from(self, array, native):
        return self.send(array, lambda k, c, h, m: (k, 1 - c, h, m) if (c == h) == native else None)

    def near_all(self, array):
        return self.send(array, lambda k, c, h, m: (k, c, h, 1 - m))

    def across(self, array):
        return self.send(array, lambda k, c, h, m: (k, c, 1 - h, 1 - m))

    def half(self, array):
        return self.send(array, lambda k, c, h, m: (k, c, 1 - h, m))

    def regroup(self, array):
        return self.send(array, lambda k, c, h, m: (k, 1 - c, 1 - h, m) if c != h else None)

    def plane(self, array, bit):
        return self.send(array, lambda k, c, h, m: (k ^ bit, c, h, m))

    def gather_near(self, both):
        return [both] + [self.plane(both, j) for j in hops(self.pairs)[0][1:]]

    def gather_far(self, parts):
        near, far = hops(self.pairs)
        a_parts = {j: part[0] for j, part in zip(near, parts)}
        b_parts = {j: part[1] for j, part in zip(near, parts)}
        result = list(parts)
        for j in far:
            low, high = j & -j, 1 << (j.bit_length() - 1)
            a_parts[j] = self.plane(a_parts[j ^ low], low)
            b_parts[j] = self.plane(b_parts[j ^ high], high)
            result += [a_parts[j], b_parts[j]]
        return result

    def gather_direct(self, both):
        return [both] + [self.plane(both, j) for j in range(1, self.pairs)]

    def scatter_direct(self, parts):
        return [self.plane(part, j) for j, part in enumerate(parts) if j]


def on_device(mesh, inputs, qkv_weight, dense_weight, expand_weight, shrink_weight, norm_gains, norm_biases, cotangent, segments):
    wires = Wires(mesh)
    pairs = wires.pairs
    pair, core, half, near = (lax.axis_index(a) for a in AXES)
    native = core == half
    me = 2 * core + near
    info = jnp.stack([me, core, pair, half]).astype(jnp.int32)

    def since(value, *done):
        return lax.optimization_barrier((value, done))[0]

    def at(values):
        return lax.optimization_barrier(values)

    def swap_weights(block, swapped):
        own = jnp.where(native, block, swapped)
        return jnp.stack([own, wires.core(jnp.where(native, swapped, block))])

    def swap_grads(both):
        other = wires.core(both[1])
        small = (both[0][:, -LANES:].astype(F32) + other[:, -LANES:].astype(F32)).astype(BF16)
        mine, sent = jnp.where(native, both[0], other), jnp.where(native, other, both[0])
        return [jnp.concatenate([a[:, :-LANES], small], axis=1) for a in (mine, sent)]

    def core_sum(parts):
        return parts[0].astype(F32) + wires.core(parts[1]).astype(F32)

    def since(value, *done):
        return lax.optimization_barrier((value, done))[0]

    def since(value, *done):
        return lax.optimization_barrier((value, done))[0]

    small = jnp.concatenate([norm_gains, norm_biases], axis=0).T
    first_block = jnp.concatenate([qkv_weight, jnp.pad(small, ((0, 0), (0, LANES - 4)))], axis=1)
    first_swapped = wires.half(first_block)
    other_segments = wires.core(since(segments, first_block))
    x_swapped = wires.regroup(since(inputs, other_segments))
    x_near = wires.near(since(inputs, other_segments), True)
    first_both = swap_weights(first_block, first_swapped)
    first_parts = wires.gather_direct(first_both)
    tables = build_tables(jnp.where(native, since(segments, first_both), other_segments))
    first_parts = since(first_parts, tables)
    qkv_full, gb = assemble_first(info, first_parts, pairs, qkv_weight.shape[1])
    x_swapped, x_near, qkv_full, gb = at((x_swapped, x_near, qkv_full, gb))
    x_mine = jnp.where(native, inputs, x_swapped)
    x_far = wires.near(x_swapped, False)
    x_core = wires.core(x_mine)
    stacks = project(0, info, x_mine, x_core, qkv_full, gb, tables, ())

    stacks, x_near, x_far = at((stacks, x_near, x_far))
    second_a = jnp.concatenate([dense_weight, expand_weight], axis=1)
    x_beside = jnp.where(native, x_near, x_far)
    x_last = wires.core(x_beside)
    a_swapped = wires.half(since(second_a, x_beside))
    stacks = project(1, info, x_beside, x_last, qkv_full, gb, tables, stacks)
    stacks, a_swapped = at((stacks, a_swapped))
    normalized, queries, keys, values = stacks

    b_swapped = wires.half(since(shrink_weight, a_swapped))
    a_both = swap_weights(second_a, a_swapped)
    a_near = wires.gather_near(a_both)
    out_0, queries_0 = attend(info, queries, keys, values, 0, 2, after=(a_both,))
    out_0, a_near, b_swapped = at((out_0, a_near, b_swapped))
    b_both = swap_weights(shrink_weight, b_swapped)
    a_parts = wires.gather_far(a_near)
    b_near = wires.gather_near(b_both)
    g_swapped = wires.regroup(since(cotangent, b_swapped))
    g_near = wires.near(since(cotangent, b_swapped), True)
    out_1, queries_1 = attend(info, queries, keys, values, 1, 2, after=(out_0, b_both))
    out_1, a_parts, b_near = at((out_1, a_parts, b_near))
    b_parts = wires.gather_far(b_near)
    widths = (dense_weight.shape[1], expand_weight.shape[1], shrink_weight.shape[1])
    dense_full, expand_full = assemble_second(info, a_parts, pairs, widths[:2])
    dense_full, expand_full, b_parts = at((dense_full, expand_full, b_parts))
    (shrink_full,) = assemble_second(info, b_parts, pairs, widths[2:])
    shrink_full, g_swapped, g_near = at((shrink_full, g_swapped, g_near))
    g_far = wires.near(g_swapped, False)
    g_mine = jnp.where(native, cotangent, g_swapped)
    g_core = wires.core(g_mine)
    results = feed(normalized, (out_0, out_1), dense_full, expand_full, shrink_full, gb, after=(g_mine,))
    results, g_near, g_far, g_core = at((results, g_near, g_far, g_core))
    branch_kept, branch_given, activated, slope = results
    branch_core = wires.core(branch_given)
    g_beside = jnp.where(native, g_near, g_far)
    g_parts = [g_mine, g_beside, g_core, wires.core(g_beside)]

    passed = (branch_kept[1].astype(F32) + branch_core[1].astype(F32)).astype(BF16)
    branch_far = wires.near(passed, False)
    branch_near = wires.near(passed, True)
    results = feed_back(
        normalized, activated, slope, g_parts, (out_0, out_1), dense_full, expand_full, shrink_full, gb, after=(passed,)
    )
    results, branch_far, branch_near, branch_kept, branch_core = at(
        (results, branch_far, branch_near, branch_kept, branch_core)
    )
    second_e, *grads, feed_grads = results

    turns = tables[0]
    feed_both = lax.psum_scatter(feed_grads, "pair", scatter_dimension=0, tiled=True)
    branch_sent = (
        branch_kept[0].astype(F32) + branch_core[0].astype(F32) + branch_far.astype(F32)
    ).astype(BF16)
    branch_back = wires.regroup(branch_sent)
    pg_0, *rests_0 = attend_back(info, queries_0, grads[0], keys, values, turns, 0, after=(branch_sent,))
    pg_0, rests_0 = at((pg_0, rests_0))
    pg_1, *rests_1 = attend_back(info, queries_1, grads[1], keys, values, turns, 1, after=(pg_0,))
    pg_1, rests_1, branch_back = at((pg_1, rests_1, branch_back))
    results = project_back(info, (pg_0, pg_1), normalized, second_e, qkv_full, gb, pairs)
    e_swapped, *so_far = at(results)

    e_core = wires.core_from(e_swapped, True)
    e_passed = (e_swapped[1].astype(F32) + e_core[1].astype(F32)).astype(BF16)
    e_far = wires.near(e_passed, False)
    (pg_0,) = attend_back(info, queries_0, grads[0], keys, values, turns, 0, rests_0, after=(e_passed, *so_far))
    pg_0, e_far, e_swapped, e_core, feed_both = at((pg_0, e_far, e_swapped, e_core, feed_both))
    feed_both = feed_both.reshape(2, qkv_weight.shape[0], -1)
    feed_both = jnp.where(core == 0, feed_both, feed_both[::-1])
    feed_mine, feed_sent = swap_grads(feed_both)
    feed_arrived = wires.half(feed_sent)
    (pg_1,) = attend_back(info, queries_1, grads[1], keys, values, turns, 1, rests_1, after=(pg_0, feed_sent))
    results = project_back(info, (pg_0, pg_1), normalized, second_e, qkv_full, gb, pairs, so_far)
    results, feed_arrived, e_far, e_swapped, e_core = at((results, feed_arrived, e_far, e_swapped, e_core))
    e_sent = (e_swapped[0].astype(F32) + e_core[0].astype(F32) + e_far.astype(F32)).astype(BF16)
    e_native, *qkv_grads = results
    e_core = wires.core_from(e_native, False)
    e_back = wires.regroup(e_sent)
    qkv_near = wires.scatter_direct(qkv_grads)
    e_passed = (e_native[1].astype(F32) + e_core[1].astype(F32)).astype(BF16)
    e_near = wires.near(e_passed, True)
    qkv_near, e_back = since((qkv_near, e_back), e_passed)
    qkv_both = sum(part.astype(F32) for part in (qkv_grads[0], *qkv_near)).astype(BF16)
    qkv_mine, qkv_sent = swap_grads(since(qkv_both, e_back))
    smalls = jnp.concatenate([qkv_mine[:, -LANES:], feed_mine[:, -LANES:]], axis=1)
    qkv_sent, smalls = since((qkv_sent, smalls), e_near)
    small_near, small_across = wires.near_all(smalls), wires.across(smalls)
    qkv_arrived = wires.half(qkv_sent)
    rows_f32 = inputs.astype(F32)
    branch = branch_kept[0].astype(F32) + branch_core[0].astype(F32) + branch_near.astype(F32)
    layer_out = (rows_f32 + jnp.where(native, branch, branch_back.astype(F32))).astype(BF16)
    feed_total = feed_mine.astype(F32) + feed_arrived.astype(F32)
    qkv_total = qkv_mine.astype(F32) + qkv_arrived.astype(F32)
    arrived = small_near.astype(F32) + small_across.astype(F32)
    attention_norm_grad = (qkv_total[:, -LANES:] + arrived[:, :LANES])[:, :8].T[:2]
    feedforward_norm_grad = (feed_total[:, -LANES:] + arrived[:, LANES:])[:, :8].T[:2]
    e = e_native[0].astype(F32) + e_core[0].astype(F32) + e_near.astype(F32)
    e = jnp.where(native, e, e_back.astype(F32))

    centered = rows_f32 - jnp.mean(rows_f32, axis=-1, keepdims=True)
    inv_scale = lax.rsqrt(jnp.mean(centered * centered, axis=-1, keepdims=True) + EPSILON)
    normalized = centered * inv_scale
    input_grad = cotangent.astype(F32) + inv_scale * (
        e - jnp.mean(e, axis=-1, keepdims=True) - normalized * jnp.mean(e * normalized, axis=-1, keepdims=True)
    )
    return (
        layer_out,
        input_grad,
        qkv_total[:, :-LANES],
        feed_total[:, : widths[0]],
        feed_total[:, widths[0] : widths[0] + widths[1]],
        feed_total[:, widths[0] + widths[1] : -LANES],
        attention_norm_grad,
        feedforward_norm_grad,
    )


def solution(mesh):
    dp, tensor = mesh.shape["dp"], mesh.shape["tensor"]
    fine = Mesh(mesh.devices.reshape(dp // 2, 2, 2, tensor // 2), AXES)
    data, split = ("pair", "core"), ("half", "m")
    tokens, weight, norm = P(AXES, None), P(data, split), P(None, data)
    return jax.shard_map(
        partial(on_device, fine),
        mesh=fine,
        in_specs=(tokens, weight, weight, weight, weight, norm, norm, tokens, P(data)),
        out_specs=(tokens, tokens, weight, weight, weight, weight, norm, norm),
        check_vma=False,
    )
```

```python
from functools import partial

import jax
import jax.numpy as jnp
from jax import lax
from jax.experimental import pallas as pl
from jax.experimental.pallas import tpu as pltpu
from jax.sharding import Mesh
from jax.sharding import PartitionSpec as P

HD = 64
ROT = 16
L = 2048
LANES = 128
EPSILON = 1e-05
MASKED = -1e30
AXES = ("pair", "core", "half", "m")
PIECES = 4
PIECE = L // PIECES
SEG_LANE = 64
DOCS = 5
LSE_LANE = SEG_LANE + DOCS
DELTA_LANE = 64
MIB = 1024 * 1024
F32 = jnp.float32
BF16 = jnp.bfloat16


def dot_nn(left, right):
    return lax.dot_general(left, right, (((1,), (0,)), ((), ())), preferred_element_type=F32)


def dot_nt(left, right):
    return lax.dot_general(left, right, (((1,), (1,)), ((), ())), preferred_element_type=F32)


def dot_tn(left, right):
    return lax.dot_general(left, right, (((0,), (0,)), ((), ())), preferred_element_type=F32)


def lanes_of(shape):
    return lax.broadcasted_iota(jnp.int32, shape, len(shape) - 1)


def rows_of(shape):
    return lax.broadcasted_iota(jnp.int32, shape, len(shape) - 2)


def normalize(x):
    rows = x.astype(F32)
    centered = rows - jnp.mean(rows, axis=-1, keepdims=True)
    return centered * lax.rsqrt(jnp.mean(centered * centered, axis=-1, keepdims=True) + EPSILON)


def split3(column):
    high = column.astype(BF16).astype(F32)
    rest = column - high
    middle = rest.astype(BF16).astype(F32)
    return high, middle, rest - middle


def with_lanes(base, first, columns):
    lane = lanes_of(base.shape)
    for offset, column in enumerate(columns):
        base = jnp.where(lane == first + offset, column, base)
    return base


def params(limit=60):
    return pltpu.CompilerParams(vmem_limit_bytes=limit * MIB)


def fenced(kernel, inputs, after):
    return lambda *refs: kernel(*refs[:inputs], *refs[inputs + after :])


ANYWHERE = pl.BlockSpec(memory_space=pl.ANY)


def whole(shape, **kw):
    return pl.BlockSpec(shape, lambda *_: (0,) * len(shape), **kw)


def once(shape):
    return whole(shape, pipeline_mode=pl.Buffered(1))


def cost(flops, nbytes, trans=0):
    return pl.CostEstimate(flops=int(flops) // 256, bytes_accessed=int(nbytes) // 256, transcendentals=int(trans) // 256)


def hops(pairs):
    near = [0] + [1 << b for b in range(pairs.bit_length() - 1)]
    far = sorted((j for j in range(pairs) if j not in near), key=lambda j: (j.bit_count(), j))
    return near, far


def block_places(info_ref, pairs, rows):
    near, far = hops(pairs)
    return pair_places(info_ref, near + far, rows)


def pair_places(info_ref, order, rows):
    core, pair = info_ref[1], info_ref[2]
    for j in order:
        base = (pair ^ j) * 2
        yield pl.multiple_of((base + core) * rows, rows), pl.multiple_of((base + 1 - core) * rows, rows)


def block_refs(refs, pairs):
    near, far = hops(pairs)
    refs = list(refs)
    for _ in near:
        both = refs.pop(0)
        yield both.at[0], both.at[1]
    for _ in far:
        yield refs.pop(0), refs.pop(0)


def block_shapes(pairs, rows, width):
    near, far = hops(pairs)
    return [(2, rows, width)] * len(near) + [(rows, width)] * (2 * len(far))


def assemble_first_kernel(pairs, rows, width, info_ref, *refs):
    weight_ref, gb_ref, small = refs[-3:]
    for offs, both in zip(pair_places(info_ref, range(pairs), rows), refs[:-3]):
        for off, part in zip(offs, (both.at[0], both.at[1])):
            weight_ref[pl.ds(off, rows), :] = part[:, :width]
            small[pl.ds(off, rows), :] = part[:, width:].astype(F32)
    gb_ref[...] = small[...].T[:8, :]


def assemble_first(info, parts, pairs, width):
    rows = parts[0].shape[1]
    feats = pairs * 2 * rows
    return pl.pallas_call(
        partial(assemble_first_kernel, pairs, rows, width),
        out_shape=(jax.ShapeDtypeStruct((feats, width), BF16), jax.ShapeDtypeStruct((8, feats), F32)),
        in_specs=[pl.BlockSpec(memory_space=pltpu.SMEM)] + [pl.BlockSpec(memory_space=pltpu.VMEM)] * len(parts),
        scratch_shapes=[pltpu.VMEM((feats, LANES), F32)],
        compiler_params=params(24),
        cost_estimate=cost(0, 4 * feats * width),
        name="assemble_qkv",
    )(info, *parts)


def assemble_second_kernel(pairs, rows, widths, info_ref, *refs):
    outs = refs[-len(widths) :]
    for offs, parts in zip(block_places(info_ref, pairs, rows), block_refs(refs[: -len(widths)], pairs)):
        for off, part in zip(offs, parts):
            start = 0
            for out, width in zip(outs, widths):
                out[pl.ds(off, rows), :] = part[:, start : start + width]
                start += width


def assemble_second(info, parts, pairs, widths):
    rows = parts[0].shape[1]
    feats = pairs * 2 * rows
    return pl.pallas_call(
        partial(assemble_second_kernel, pairs, rows, widths),
        out_shape=tuple(jax.ShapeDtypeStruct((feats, w), BF16) for w in widths),
        in_specs=[pl.BlockSpec(memory_space=pltpu.SMEM)] + [pl.BlockSpec(memory_space=pltpu.VMEM)] * len(parts),
        compiler_params=params(24),
        cost_estimate=cost(0, 4 * feats * sum(widths)),
        name="assemble_ffn",
    )(info, *parts)


def turn(values, cosine, sine_up, sine_down):
    return (
        values * cosine
        + pltpu.roll(values, ROT // 2, 1) * sine_up
        + pltpu.roll(values, LANES - ROT // 2, 1) * sine_down
    )


def project_kernel(heads, info_ref, xa_ref, xb_ref, w_ref, gb_ref, turn_ref, feature_ref, *refs):
    n_ref, q_ref, k_ref, v_ref = refs[-4:]
    first_piece = pl.program_id(0) < pl.num_programs(0) // 2
    normalized = normalize(jnp.where(first_piece, xa_ref[...], xb_ref[...]))
    n_ref[0] = normalized
    first = (normalized * gb_ref[0:1, :] + gb_ref[2:3, :]).astype(BF16)
    projected = dot_nn(first, w_ref[...])
    cosine, up, down = (turn_ref[:, n * LANES : (n + 1) * LANES] for n in range(3))
    query_feature, key_feature = (feature_ref[:, n * LANES : (n + 1) * LANES].astype(F32) for n in range(2))
    lane = lanes_of(cosine.shape)
    low = lane < HD
    value_feature = ((lane >= DELTA_LANE) & (lane < DELTA_LANE + 3)).astype(F32)

    def part(offset):
        tile = projected[:, offset // LANES * LANES : offset // LANES * LANES + LANES]
        return pltpu.roll(tile, HD, 1) if offset % LANES else tile

    for h in range(heads):
        sl = slice(h * LANES, (h + 1) * LANES)
        base = h * 3 * HD
        query = turn(part(base), cosine, up, down) * HD ** (-0.5)
        key = turn(part(base + HD), cosine, up, down)
        q_ref[0, :, sl] = jnp.where(low, query, query_feature).astype(BF16)
        k_ref[0, :, sl] = jnp.where(low, key, key_feature).astype(BF16)
        v_ref[0, :, sl] = jnp.where(low, part(base + 2 * HD), value_feature).astype(BF16)


def project(r, info, xa, xb, weight, gb, tables, stacks, after=(), block=512):
    feats, width = weight.shape
    heads = width // (3 * HD)
    steps = PIECE // block
    shapes = [(PIECES, PIECE, feats)] + [(PIECES, PIECE, heads * LANES)] * 3
    kinds = [F32, BF16, BF16, BF16]
    piece = lambda i: r + 2 * (i // steps)
    table = lambda n: pl.BlockSpec((block, n * LANES), lambda i, info: ((info[0] ^ piece(i)) * steps + i % steps, 0))
    inputs = [info, xa, xb, weight, gb, *tables]
    return pl.pallas_call(
        partial(project_kernel, heads),
        grid_spec=pltpu.PrefetchScalarGridSpec(
            num_scalar_prefetch=1,
            grid=(2 * steps,),
            in_specs=[
                pl.BlockSpec((block, feats), lambda i, info: (jnp.minimum(i, steps - 1), 0)),
                pl.BlockSpec((block, feats), lambda i, info: (jnp.maximum(i - steps, 0), 0)),
                once((feats, width)),
                once((8, feats)),
                table(3),
                table(2),
            ]
            + [ANYWHERE] * (len(stacks) + len(after)),
            out_specs=[pl.BlockSpec((1, block, s[2]), lambda i, info: (piece(i), i % steps, 0)) for s in shapes],
        ),
        out_shape=[jax.ShapeDtypeStruct(s, kind) for s, kind in zip(shapes, kinds)],
        input_output_aliases={len(inputs) + n: n for n in range(len(stacks))},
        compiler_params=params(36),
        cost_estimate=cost(4 * PIECE * feats * width, 2 * (feats * width + 12 * PIECE * feats)),
        name=f"project_{r}",
    )(*inputs, *stacks, *after)


def attend_kernel(heads, info_ref, q_ref, k_ref, v_ref, o_ref, qb_ref):
    me = info_ref[0]
    causal = lanes_of((PIECE, PIECE)) <= rows_of((PIECE, PIECE))
    low = lanes_of((PIECE, LANES)) < HD
    at = [pl.multiple_of((me ^ p) * PIECE, PIECE) for p in range(PIECES)]
    for i in range(PIECES):
        rows = pl.ds(at[i], PIECE)
        outs = []
        for h in range(heads):
            sl = slice(h * LANES, (h + 1) * LANES)
            query = q_ref[rows, sl]
            scores = [dot_nt(query, k_ref[pl.ds(at[j], PIECE), sl]) for j in range(i + 1)]
            scores[-1] = jnp.where(causal, scores[-1], MASKED)
            top = jnp.max(scores[0], axis=-1, keepdims=True)
            for s in scores[1:]:
                top = jnp.maximum(top, jnp.max(s, axis=-1, keepdims=True))
            out = total = None
            for j, s in enumerate(scores):
                weight = jnp.exp(s - top)
                part = jnp.sum(weight, axis=-1, keepdims=True)
                term = dot_nn(weight.astype(BF16), v_ref[pl.ds(at[j], PIECE), sl])
                total = part if total is None else total + part
                out = term if out is None else out + term
            outs.append(out * (1.0 / total))
            log_total = split3(top + jnp.log(total))
            qb_ref[rows, sl] = with_lanes(query.astype(F32), LSE_LANE, [-c for c in log_total]).astype(BF16)
        for h in range(0, heads, 2):
            o_ref[rows, h * HD : h * HD + LANES] = jnp.where(low, outs[h], pltpu.roll(outs[h + 1], HD, 1))


def attend(info, queries, keys, values, group, heads, after=()):
    full = queries.shape[2]
    width = heads * LANES
    own = pl.BlockSpec((L, width), lambda i, info: (0, group))
    return pl.pallas_call(
        fenced(partial(attend_kernel, heads), 4, len(after)),
        grid_spec=pltpu.PrefetchScalarGridSpec(
            num_scalar_prefetch=1,
            grid=(1,),
            in_specs=[own] * 3 + [ANYWHERE] * len(after),
            out_specs=[whole((L, heads * HD)), whole((L, width))],
        ),
        out_shape=[jax.ShapeDtypeStruct((L, heads * HD), F32), jax.ShapeDtypeStruct((L, width), BF16)],
        compiler_params=params(44),
        cost_estimate=cost(heads * L * L * LANES * 4, 5 * L * width, heads * L * L // 2),
        name=f"attention_forward_{group}",
    )(info, *(a.reshape(L, full) for a in (queries, keys, values)), *after)


def gelu_parts(h):
    bell = jnp.exp2(h * h * (-0.5 * 1.4426950408889634))
    t = pl.reciprocal(1.0 + (0.3275911 * 0.5**0.5) * jnp.abs(h))
    poly = t * (
        0.127414796 + t * (-0.142248368 + t * (0.7107068705 + t * (-0.7265760135 + t * 0.5307027145)))
    )
    tail = poly * bell
    return jnp.where(h < 0, tail, 1.0 - tail), bell * 0.3989422804014327


def norm_columns(sums_ref):
    wide = jnp.concatenate([sums_ref[...], jnp.zeros((LANES - 8, sums_ref.shape[1]), F32)], axis=0)
    return wide.T


def write_parts(info_ref, total, small, refs):
    width, rows = total.shape[1], refs[0].shape[1]
    for offs, both in zip(pair_places(info_ref, range(len(refs)), rows), refs):
        for n, off in enumerate(offs):
            both[n, :, :width] = total[pl.ds(off, rows), :].astype(BF16)
            both[n, :, width:] = small[pl.ds(off, rows), :].astype(BF16)


def feed_kernel(groups, parts, n_ref, *refs):
    o_refs, refs = refs[:groups], refs[groups:]
    (wd_ref, we_ref, ws_ref, gb_ref), refs = refs[:4], refs[4:]
    br_refs, (activated_ref, slope_ref, b_now) = refs[:PIECES], refs[PIECES:]
    step = pl.program_id(0)
    rows = PIECE // parts
    for n in range(parts):
        sl = slice(n * rows, (n + 1) * rows)
        second = (n_ref[sl, :] * gb_ref[1:2, :] + gb_ref[3:4, :]).astype(BF16)
        hidden = dot_nn(second, we_ref[...])
        cdf, density = gelu_parts(hidden)
        activated = (hidden * cdf).astype(BF16)
        activated_ref[sl, :] = activated
        slope_ref[sl, :] = cdf + hidden * density
        attended = jnp.concatenate([o[sl, :] for o in o_refs], axis=1).astype(BF16)
        b_now[sl, :] = (dot_nt(attended, wd_ref[...]) + dot_nt(activated, ws_ref[...])).astype(BF16)

    for r in range(PIECES):

        @pl.when(step == r)
        def _():
            br_refs[r][...] = b_now[...]


def feed(normalized, outs, wd, we, ws, gb, after=(), parts=1):
    feats, hidden = we.shape
    by_step = lambda i: (i, 0)
    inputs = [normalized.reshape(L, feats), *outs, wd, we, ws, gb]
    return pl.pallas_call(
        fenced(partial(feed_kernel, len(outs), parts), len(inputs), len(after)),
        grid=(PIECES,),
        in_specs=[pl.BlockSpec((PIECE, feats), by_step)]
        + [pl.BlockSpec((PIECE, o.shape[1]), by_step) for o in outs]
        + [once(w.shape) for w in (wd, we, ws, gb)]
        + [ANYWHERE] * len(after),
        out_specs=[
            *[once((PIECE, feats))] * PIECES,
            pl.BlockSpec((PIECE, hidden), by_step),
            pl.BlockSpec((PIECE, hidden), by_step),
        ],
        out_shape=[jax.ShapeDtypeStruct((PIECE, feats), BF16)] * PIECES
        + [jax.ShapeDtypeStruct((L, hidden), BF16), jax.ShapeDtypeStruct((L, hidden), F32)],
        scratch_shapes=[pltpu.VMEM((PIECE, feats), BF16)],
        compiler_params=params(44),
        cost_estimate=cost(4 * L * feats * hidden, 16 * L * feats),
        name="feed_forward",
    )(*inputs, *after)


def feed_back_kernel(heads, group, n_ref, activated_ref, slope_ref, *refs):
    groups = heads // group
    g_refs, refs = refs[:PIECES], refs[PIECES:]
    o_refs, refs = refs[:groups], refs[groups:]
    (wd_ref, we_ref, ws_ref, gb_ref, sg_ref), refs = refs[:5], refs[5:]
    doa_refs, refs = refs[:groups], refs[groups:]
    grads_ref, g_now, gd, ge, gs, sums = refs
    step, last = pl.program_id(0), pl.num_programs(0) - 1

    @pl.when(step == 0)
    def _():
        for total in (gd, ge, gs, sums):
            total[...] = jnp.zeros_like(total)

    for r in range(PIECES):

        @pl.when(step == r)
        def _():
            g_now[...] = g_refs[r][...]

    g = g_now[...]
    hidden_grad = (dot_nn(g, ws_ref[...]) * slope_ref[...]).astype(BF16)
    normalized = n_ref[...]
    second = (normalized * gb_ref[1:2, :] + gb_ref[3:4, :]).astype(BF16)
    out = jnp.concatenate([o[...] for o in o_refs], axis=1)
    gs[...] += dot_tn(g, activated_ref[...])
    gd[...] += dot_tn(g, out.astype(BF16))
    ge[...] += dot_tn(second, hidden_grad)
    second_grad = dot_nt(hidden_grad, we_ref[...])
    sg_ref[...] = second_grad * gb_ref[1:2, :]
    sums[0:1, :] += jnp.sum(second_grad * normalized, axis=0, keepdims=True)
    sums[1:2, :] += jnp.sum(second_grad, axis=0, keepdims=True)
    attended_grad = dot_nn(g, wd_ref[...]).astype(BF16).astype(F32)
    product = attended_grad * out
    lane = lanes_of((PIECE, LANES))
    for h in range(heads):
        tile = slice(h // 2 * LANES, (h // 2 + 1) * LANES)
        mine = (lane < HD) if h % 2 == 0 else (lane >= HD)
        delta = split3(jnp.sum(jnp.where(mine, product[:, tile], 0.0), axis=-1, keepdims=True))
        grad = attended_grad[:, tile]
        if h % 2:
            grad = pltpu.roll(grad, HD, 1)
        grad = jnp.where(lane < HD, grad, 0.0)
        start = h % group * LANES
        doa_refs[h // group][:, start : start + LANES] = with_lanes(grad, DELTA_LANE, [-c for c in delta]).astype(BF16)

    @pl.when(step == last)
    def _():
        start = 0
        for total in (gd, ge, gs):
            grads_ref[:, start : start + total.shape[1]] = total[...].astype(BF16)
            start += total.shape[1]
        grads_ref[:, start:] = norm_columns(sums).astype(BF16)


def feed_back(normalized, activated, slope, g_parts, outs, wd, we, ws, gb, after=()):
    feats, hidden = we.shape
    heads = wd.shape[1] // HD
    group = heads // len(outs)
    width = wd.shape[1] + 2 * hidden + LANES
    by_step = lambda i: (i, 0)
    step = lambda w: pl.BlockSpec((PIECE, w), by_step)
    inputs = [normalized.reshape(L, feats), activated, slope, *g_parts, *outs, wd, we, ws, gb]
    return pl.pallas_call(
        fenced(partial(feed_back_kernel, heads, group), len(inputs), len(after)),
        grid=(PIECES,),
        in_specs=[step(feats), step(hidden), step(hidden)]
        + [once((PIECE, feats))] * PIECES
        + [step(group * HD)] * len(outs)
        + [once(w.shape) for w in (wd, we, ws, gb)]
        + [ANYWHERE] * len(after),
        out_specs=[step(feats)] + [step(group * LANES)] * len(outs) + [once((feats, width))],
        out_shape=[jax.ShapeDtypeStruct((L, feats), F32)]
        + [jax.ShapeDtypeStruct((L, group * LANES), BF16)] * len(outs)
        + [jax.ShapeDtypeStruct((feats, width), BF16)],
        scratch_shapes=[
            pltpu.VMEM((PIECE, feats), BF16),
            pltpu.VMEM(wd.shape, F32),
            pltpu.VMEM(we.shape, F32),
            pltpu.VMEM(ws.shape, F32),
            pltpu.VMEM((8, feats), F32),
        ],
        compiler_params=params(),
        cost_estimate=cost(8 * L * feats * hidden, 20 * L * feats),
        name="feed_back",
    )(*inputs, *after)


def block_back(query, grad, key, value, causal):
    scores = dot_nt(key, query)
    if causal is not None:
        scores = jnp.where(causal, scores, MASKED)
    probs = jnp.exp(scores)
    score_grad = (probs * dot_nt(value, grad)).astype(BF16)
    return dot_tn(score_grad, key), dot_nn(score_grad, query), dot_nn(probs.astype(BF16), grad)


def triangle_back(load, base, sums, h, causal):
    q0, g0, k0, v0 = load(base)
    q1, g1, k1, v1 = load(base + 1)
    low = block_back(q0, g0, k0, v0, causal)
    side = block_back(q1, g1, k0, v0, None)
    high = block_back(q1, g1, k1, v1, causal)
    dq, dk, dv = sums
    dq[h, base] += low[0]
    dq[h, base + 1] += side[0] + high[0]
    for d, n in ((dk, 1), (dv, 2)):
        d[h, base] += low[n] + side[n]
        d[h, base + 1] += high[n]


def finish_back(pg_ref, tables_ref, table_row, sums, base, near, heads):
    low = lanes_of((PIECE, LANES)) < HD
    dq, dk, dv = sums
    for n in range(2):
        rows = pl.ds(pl.multiple_of(table_row + n * PIECE, PIECE), PIECE)
        cosine = tables_ref[rows, :LANES]
        up, down = -tables_ref[rows, LANES : 2 * LANES], -tables_ref[rows, 2 * LANES :]
        for h in range(0, heads, 2):
            start = h // 2 * 3 * LANES
            q0, q1 = (turn(dq[h + x, base + n] * HD ** (-0.5), cosine, up, down) for x in (0, 1))
            k0, k1 = (turn(dk[h + x, base + n], cosine, up, down) for x in (0, 1))
            v0, v1 = dv[h, base + n], dv[h + 1, base + n]
            for tile, (left, right) in enumerate(((q0, k0), (v0, q1), (k1, v1))):
                pg_ref[near ^ n, :, start + tile * LANES : start + (tile + 1) * LANES] = jnp.where(
                    low, left, pltpu.roll(right, HD, 1)
                ).astype(BF16)


def attend_back_first_kernel(info_ref, q_ref, do_ref, k_ref, v_ref, tables_ref, pg_ref, *refs):
    rests, sums = refs[:3], refs[3:]
    dq, dk, dv = sums
    me, half = info_ref[0], info_ref[3]
    heads = q_ref.shape[1] // LANES
    causal = rows_of((PIECE, PIECE)) <= lanes_of((PIECE, PIECE))
    swapped, native = 2 * (1 - half), 2 * half
    zero = jnp.zeros((PIECE, LANES), F32)
    for h in range(heads):
        sl = slice(h * LANES, (h + 1) * LANES)

        def load(piece):
            rows = pl.ds(pl.multiple_of((me ^ piece) * PIECE, PIECE), PIECE)
            return q_ref[rows, sl], do_ref[rows, sl], k_ref[rows, sl], v_ref[rows, sl]

        pieces = [load(p) for p in range(PIECES)]
        terms = {
            (i, j): block_back(*pieces[i][:2], *pieces[j][2:], None) for j in (0, 1) for i in (2, 3)
        }
        for p in (0, 1):
            dq[h, p] = zero
            dq[h, p + 2] = terms[p + 2, 0][0] + terms[p + 2, 1][0]
            for d, n in ((dk, 1), (dv, 2)):
                d[h, p] = terms[2, p][n] + terms[3, p][n]
                d[h, p + 2] = zero
        triangle_back(load, swapped, sums, h, causal)
        for rest, d in zip(rests, sums):
            for n in range(2):
                rest[h, n] = d[h, native + n]
    finish_back(pg_ref, tables_ref, 0, sums, swapped, me % 2, heads)


def attend_back_second_kernel(info_ref, q_ref, do_ref, k_ref, v_ref, tables_ref, *refs):
    rests, pg_ref, sums = refs[:3], refs[3], refs[4:]
    near = info_ref[0] % 2
    heads = q_ref.shape[1] // LANES
    causal = rows_of((PIECE, PIECE)) <= lanes_of((PIECE, PIECE))
    for h in range(heads):
        sl = slice(h * LANES, (h + 1) * LANES)

        def load(piece):
            rows = pl.ds(pl.multiple_of((near ^ piece) * PIECE, PIECE), PIECE)
            return q_ref[rows, sl], do_ref[rows, sl], k_ref[rows, sl], v_ref[rows, sl]

        for rest, d in zip(rests, sums):
            for n in range(2):
                d[h, n] = rest[h, n]
        triangle_back(load, 0, sums, h, causal)
    finish_back(pg_ref, tables_ref, 0, sums, 0, near, heads)


def attend_back(info, queries, grads, keys, values, tables, group, rests=(), after=()):
    width, full = queries.shape[1], keys.shape[2]
    heads = width // LANES
    rest = (heads, 2, PIECE, LANES)
    pg = (2, PIECE, heads * 3 * HD)
    first = not rests
    rows = L if first else L // 2
    place = (lambda info: 0) if first else (lambda info: info[1] ^ info[3])
    own = pl.BlockSpec((rows, width), lambda s, info: (place(info), 0))
    shared = pl.BlockSpec((rows, width), lambda s, info: (place(info), group))
    table = pl.BlockSpec((L // 2, 3 * LANES), lambda s, info: (1 - info[3] if first else info[3], 0))
    inputs = [info, queries, grads, keys.reshape(L, full), values.reshape(L, full), tables, *rests]
    blocks = 7 if first else 3
    return pl.pallas_call(
        fenced(attend_back_first_kernel if first else attend_back_second_kernel, len(inputs), len(after)),
        grid_spec=pltpu.PrefetchScalarGridSpec(
            num_scalar_prefetch=1,
            grid=(1,),
            in_specs=[own, own, shared, shared, table] + [whole(rest)] * len(rests) + [ANYWHERE] * len(after),
            out_specs=[whole(pg)] + [whole(rest)] * (3 if first else 0),
            scratch_shapes=[pltpu.VMEM((heads, PIECES if first else 2, PIECE, LANES), F32)] * 3,
        ),
        out_shape=[jax.ShapeDtypeStruct(pg, BF16)] + [jax.ShapeDtypeStruct(rest, F32)] * (3 if first else 0),
        compiler_params=params(44),
        cost_estimate=cost(blocks * heads * PIECE * PIECE * LANES * 10, 12 * L * width, blocks * heads * PIECE * PIECE),
        name=f"attention_backward_{group}" + ("a" if first else "b"),
    )(*inputs, *after)


def project_back_kernel(pairs, groups, final, info_ref, *refs):
    pg_refs, refs = refs[:groups], refs[groups:]
    (n_ref, sg_ref, w_ref, gb_ref), refs = refs[:4], refs[4:]
    if final:
        (gq_in, sums_in, *e_refs), refs = refs[:4], refs[4:]
        *part_refs, gq, sums, small, e_now = refs
    else:
        *e_refs, gq, sums, e_now = refs
    step, last = pl.program_id(0), pl.num_programs(0) - 1

    @pl.when(step == 0)
    def _():
        gq[...] = gq_in[...] if final else jnp.zeros_like(gq)
        sums[...] = sums_in[...] if final else jnp.zeros_like(sums)

    normalized = n_ref[0]
    first = (normalized * gb_ref[0:1, :] + gb_ref[2:3, :]).astype(BF16)
    grad = jnp.concatenate([pg[0] for pg in pg_refs], axis=1)
    first_grad = dot_nt(grad, w_ref[...])
    gq[...] += dot_tn(first, grad)
    e_now[...] = (first_grad * gb_ref[0:1, :] + sg_ref[0]).astype(BF16)
    block = e_now.shape[0]
    per = PIECE // block
    place = pl.ds(pl.multiple_of(step % per * block, block), block)
    for n in range(2):

        @pl.when(step // per == n)
        def _():
            e_refs[n][place, :] = e_now[...]

    sums[0:1, :] += jnp.sum(first_grad * normalized, axis=0, keepdims=True)
    sums[1:2, :] += jnp.sum(first_grad, axis=0, keepdims=True)
    if final:

        @pl.when(step == last)
        def _():
            small[...] = norm_columns(sums)
            write_parts(info_ref, gq, small, part_refs)


def project_back(info, pgs, normalized, sg, weight, gb, pairs, so_far=(), after=(), block=PIECE):
    feats, width = weight.shape
    final = bool(so_far)
    swapped = 0 if final else 1
    sums = (8, feats)
    shapes = [(2, feats // (2 * pairs), width + LANES)] * pairs if final else []
    piece = (PIECE, feats)
    per = PIECE // block
    by_step = lambda i, info: (i // per, i % per, 0)
    relative = pl.BlockSpec(
        (1, block, feats), lambda i, info: (2 * (info[1] ^ info[3] ^ swapped) + i // per, i % per, 0)
    )
    inputs = [info, *pgs, normalized, sg.reshape(PIECES, PIECE, feats), weight, gb, *so_far]
    totals = [pltpu.VMEM(weight.shape, F32), pltpu.VMEM(sums, F32)]
    results = [(piece, BF16)] * 2 + ([(s, BF16) for s in shapes] if final else [(weight.shape, F32), (sums, F32)])
    return pl.pallas_call(
        fenced(partial(project_back_kernel, pairs, len(pgs), final), len(inputs), len(after)),
        grid_spec=pltpu.PrefetchScalarGridSpec(
            num_scalar_prefetch=1,
            grid=(2 * per,),
            in_specs=[pl.BlockSpec((1, block, pg.shape[2]), by_step) for pg in pgs]
            + [relative, relative]
            + [once(a.shape) for a in (weight, gb, *so_far)]
            + [ANYWHERE] * len(after),
            out_specs=[once(s) for s, _ in results],
            scratch_shapes=(totals + [pltpu.VMEM((feats, LANES), F32)] if final else [])
            + [pltpu.VMEM((block, feats), BF16)],
        ),
        out_shape=[jax.ShapeDtypeStruct(s, kind) for s, kind in results],
        compiler_params=params(44),
        cost_estimate=cost(2 * L * feats * width, 6 * L * feats),
        name="project_back_" + ("b" if final else "a"),
    )(*inputs, *after)


def build_tables(segments):
    places = jnp.arange(L, dtype=jnp.int32)
    starts = jnp.zeros_like(segments)
    for value in range(DOCS):
        starts = starts + jnp.where(segments > value, jnp.sum((segments == value).astype(jnp.int32)), 0)
    position = (places - starts).astype(F32)
    lane = jnp.arange(LANES, dtype=jnp.int32)
    inner = lane % HD
    half = ROT // 2
    frequency = 10000.0 ** (-((inner % half).astype(F32) * 2.0 / ROT))
    angles = position[:, None] * frequency[None, :]
    turned = (inner < ROT)[None, :]
    sine = jnp.sin(angles)
    cosine = jnp.where(turned, jnp.cos(angles), 1.0)
    up = jnp.where(turned & (inner >= half)[None, :], sine, 0.0)
    down = jnp.where((inner < half)[None, :], -sine, 0.0)
    feature = lane - SEG_LANE
    is_doc = ((feature >= 0) & (feature < DOCS))[None, :]
    same = segments[:, None] == feature[None, :]
    one = ((lane >= LSE_LANE) & (lane < LSE_LANE + 3))[None, :]
    query_feature = jnp.where(is_doc & ~same, MASKED, 0.0)
    key_feature = jnp.where((is_doc & same) | one, 1.0, 0.0)
    features = jnp.concatenate([query_feature, key_feature], axis=1).astype(BF16)
    return jnp.concatenate([cosine, up, down], axis=1), features


class Wires:
    def __init__(self, mesh):
        self.pairs = mesh.shape["pair"]
        self.sizes = [mesh.shape[a] for a in AXES]

    def send(self, array, target):
        _, cores, halves, ms = self.sizes

        def index(k, c, h, m):
            return ((k * cores + c) * halves + h) * ms + m

        moves = []
        for k in range(self.pairs):
            for c in range(cores):
                for h in range(halves):
                    for m in range(ms):
                        there = target(k, c, h, m)
                        if there is not None:
                            moves.append((index(k, c, h, m), index(*there)))
        return lax.ppermute(array, AXES, moves)

    def core(self, array):
        return self.send(array, lambda k, c, h, m: (k, 1 - c, h, m))

    def near(self, array, native):
        return self.send(array, lambda k, c, h, m: (k, c, h, 1 - m) if (c == h) == native else None)

    def core_from(self, array, native):
        return self.send(array, lambda k, c, h, m: (k, 1 - c, h, m) if (c == h) == native else None)

    def near_all(self, array):
        return self.send(array, lambda k, c, h, m: (k, c, h, 1 - m))

    def across(self, array):
        return self.send(array, lambda k, c, h, m: (k, c, 1 - h, 1 - m))

    def half(self, array):
        return self.send(array, lambda k, c, h, m: (k, c, 1 - h, m))

    def regroup(self, array):
        return self.send(array, lambda k, c, h, m: (k, 1 - c, 1 - h, m) if c != h else None)

    def plane(self, array, bit):
        return self.send(array, lambda k, c, h, m: (k ^ bit, c, h, m))

    def gather_near(self, both):
        return [both] + [self.plane(both, j) for j in hops(self.pairs)[0][1:]]

    def gather_far(self, parts):
        near, far = hops(self.pairs)
        a_parts = {j: part[0] for j, part in zip(near, parts)}
        b_parts = {j: part[1] for j, part in zip(near, parts)}
        result = list(parts)
        for j in far:
            low, high = j & -j, 1 << (j.bit_length() - 1)
            a_parts[j] = self.plane(a_parts[j ^ low], low)
            b_parts[j] = self.plane(b_parts[j ^ high], high)
            result += [a_parts[j], b_parts[j]]
        return result

    def gather_direct(self, both):
        return [both] + [self.plane(both, j) for j in range(1, self.pairs)]

    def scatter_direct(self, parts):
        return [self.plane(part, j) for j, part in enumerate(parts) if j]


def on_device(mesh, inputs, qkv_weight, dense_weight, expand_weight, shrink_weight, norm_gains, norm_biases, cotangent, segments):
    wires = Wires(mesh)
    pairs = wires.pairs
    pair, core, half, near = (lax.axis_index(a) for a in AXES)
    native = core == half
    me = 2 * core + near
    info = jnp.stack([me, core, pair, half]).astype(jnp.int32)

    def since(value, *done):
        return lax.optimization_barrier((value, done))[0]

    def at(values):
        return lax.optimization_barrier(values)

    def swap_weights(block, swapped):
        own = jnp.where(native, block, swapped)
        return jnp.stack([own, wires.core(jnp.where(native, swapped, block))])

    def swap_grads(both):
        other = wires.core(both[1])
        small = (both[0][:, -LANES:].astype(F32) + other[:, -LANES:].astype(F32)).astype(BF16)
        mine, sent = jnp.where(native, both[0], other), jnp.where(native, other, both[0])
        return [jnp.concatenate([a[:, :-LANES], small], axis=1) for a in (mine, sent)]

    def core_sum(parts):
        return parts[0].astype(F32) + wires.core(parts[1]).astype(F32)

    def since(value, *done):
        return lax.optimization_barrier((value, done))[0]

    def since(value, *done):
        return lax.optimization_barrier((value, done))[0]

    small = jnp.concatenate([norm_gains, norm_biases], axis=0).T
    first_block = jnp.concatenate([qkv_weight, jnp.pad(small, ((0, 0), (0, LANES - 4)))], axis=1)
    first_swapped = wires.half(first_block)
    other_segments = wires.core(since(segments, first_block))
    x_swapped = wires.regroup(since(inputs, other_segments))
    x_near = wires.near(since(inputs, other_segments), True)
    first_both = swap_weights(first_block, first_swapped)
    first_parts = wires.gather_direct(first_both)
    tables = build_tables(jnp.where(native, since(segments, first_both), other_segments))
    first_parts = since(first_parts, tables)
    qkv_full, gb = assemble_first(info, first_parts, pairs, qkv_weight.shape[1])
    x_swapped, x_near, qkv_full, gb = at((x_swapped, x_near, qkv_full, gb))
    x_mine = jnp.where(native, inputs, x_swapped)
    x_far = wires.near(x_swapped, False)
    x_core = wires.core(x_mine)
    stacks = project(0, info, x_mine, x_core, qkv_full, gb, tables, ())

    stacks, x_near, x_far = at((stacks, x_near, x_far))
    second_a = jnp.concatenate([dense_weight, expand_weight], axis=1)
    x_beside = jnp.where(native, x_near, x_far)
    x_last = wires.core(x_beside)
    a_swapped = wires.half(since(second_a, x_beside))
    stacks = project(1, info, x_beside, x_last, qkv_full, gb, tables, stacks)
    stacks, a_swapped = at((stacks, a_swapped))
    normalized, queries, keys, values = stacks

    b_swapped = wires.half(since(shrink_weight, a_swapped))
    a_both = swap_weights(second_a, a_swapped)
    a_near = wires.gather_near(a_both)
    out_0, queries_0 = attend(info, queries, keys, values, 0, 2, after=(a_both,))
    out_0, a_near, b_swapped = at((out_0, a_near, b_swapped))
    b_both = swap_weights(shrink_weight, b_swapped)
    a_parts = wires.gather_far(a_near)
    b_near = wires.gather_near(b_both)
    g_swapped = wires.regroup(since(cotangent, b_swapped))
    g_near = wires.near(since(cotangent, b_swapped), True)
    out_1, queries_1 = attend(info, queries, keys, values, 1, 2, after=(out_0, b_both))
    out_1, a_parts, b_near = at((out_1, a_parts, b_near))
    b_parts = wires.gather_far(b_near)
    widths = (dense_weight.shape[1], expand_weight.shape[1], shrink_weight.shape[1])
    dense_full, expand_full = assemble_second(info, a_parts, pairs, widths[:2])
    dense_full, expand_full, b_parts = at((dense_full, expand_full, b_parts))
    (shrink_full,) = assemble_second(info, b_parts, pairs, widths[2:])
    shrink_full, g_swapped, g_near = at((shrink_full, g_swapped, g_near))
    g_far = wires.near(g_swapped, False)
    g_mine = jnp.where(native, cotangent, g_swapped)
    g_core = wires.core(g_mine)
    results = feed(normalized, (out_0, out_1), dense_full, expand_full, shrink_full, gb, after=(g_mine,))
    results, g_near, g_far, g_core = at((results, g_near, g_far, g_core))
    *branches, activated, slope = results
    passed_core = wires.core(branches[3])
    g_beside = jnp.where(native, g_near, g_far)
    g_parts = [g_mine, g_beside, g_core, wires.core(g_beside)]

    passed = (branches[1].astype(F32) + passed_core.astype(F32)).astype(BF16)
    branch_kept, branch_core = branches[0], wires.core(since(branches[2], passed_core))
    branch_far = wires.near(passed, False)
    branch_near = wires.near(passed, True)
    results = feed_back(
        normalized, activated, slope, g_parts, (out_0, out_1), dense_full, expand_full, shrink_full, gb, after=(passed,)
    )
    results, branch_far, branch_near, branch_kept, branch_core = at(
        (results, branch_far, branch_near, branch_kept, branch_core)
    )
    second_e, *grads, feed_grads = results

    turns = tables[0]
    feed_both = lax.psum_scatter(feed_grads, "pair", scatter_dimension=0, tiled=True)
    branch_sent = (
        branch_kept.astype(F32) + branch_core.astype(F32) + branch_far.astype(F32)
    ).astype(BF16)
    branch_back = wires.regroup(branch_sent)
    pg_0, *rests_0 = attend_back(info, queries_0, grads[0], keys, values, turns, 0, after=(branch_sent,))
    pg_0, rests_0 = at((pg_0, rests_0))
    pg_1, *rests_1 = attend_back(info, queries_1, grads[1], keys, values, turns, 1, after=(pg_0,))
    pg_1, rests_1, branch_back = at((pg_1, rests_1, branch_back))
    results = project_back(info, (pg_0, pg_1), normalized, second_e, qkv_full, gb, pairs)
    e_swapped, e_given, *so_far = at(results)

    passed_core = wires.core_from(e_given, True)
    e_passed = (e_given.astype(F32) + passed_core.astype(F32)).astype(BF16)
    e_core = wires.core_from(since(e_swapped, passed_core), True)
    e_far = wires.near(e_passed, False)
    (pg_0,) = attend_back(info, queries_0, grads[0], keys, values, turns, 0, rests_0, after=(e_passed, *so_far))
    pg_0, e_far, e_swapped, e_core, feed_both = at((pg_0, e_far, e_swapped, e_core, feed_both))
    feed_both = feed_both.reshape(2, qkv_weight.shape[0], -1)
    feed_both = jnp.where(core == 0, feed_both, feed_both[::-1])
    feed_mine, feed_sent = swap_grads(feed_both)
    feed_arrived = wires.half(feed_sent)
    (pg_1,) = attend_back(info, queries_1, grads[1], keys, values, turns, 1, rests_1, after=(pg_0, feed_sent))
    results = project_back(info, (pg_0, pg_1), normalized, second_e, qkv_full, gb, pairs, so_far)
    results, feed_arrived, e_far, e_swapped, e_core = at((results, feed_arrived, e_far, e_swapped, e_core))
    e_sent = (e_swapped.astype(F32) + e_core.astype(F32) + e_far.astype(F32)).astype(BF16)
    e_native, e_given, *qkv_grads = results
    passed_core = wires.core_from(e_given, False)
    e_back = wires.regroup(e_sent)
    qkv_near = wires.scatter_direct(qkv_grads)
    e_passed = (e_given.astype(F32) + passed_core.astype(F32)).astype(BF16)
    e_near = wires.near(e_passed, True)
    e_core = wires.core_from(since(e_native, passed_core), False)
    qkv_near, e_back = since((qkv_near, e_back), e_passed)
    qkv_both = sum(part.astype(F32) for part in (qkv_grads[0], *qkv_near)).astype(BF16)
    qkv_mine, qkv_sent = swap_grads(since(qkv_both, e_back))
    smalls = jnp.concatenate([qkv_mine[:, -LANES:], feed_mine[:, -LANES:]], axis=1)
    qkv_sent, smalls = since((qkv_sent, smalls), e_near)
    small_near, small_across = wires.near_all(smalls), wires.across(smalls)
    qkv_arrived = wires.half(qkv_sent)
    rows_f32 = inputs.astype(F32)
    branch = branch_kept.astype(F32) + branch_core.astype(F32) + branch_near.astype(F32)
    layer_out = (rows_f32 + jnp.where(native, branch, branch_back.astype(F32))).astype(BF16)
    feed_total = feed_mine.astype(F32) + feed_arrived.astype(F32)
    qkv_total = qkv_mine.astype(F32) + qkv_arrived.astype(F32)
    arrived = small_near.astype(F32) + small_across.astype(F32)
    attention_norm_grad = (qkv_total[:, -LANES:] + arrived[:, :LANES])[:, :8].T[:2]
    feedforward_norm_grad = (feed_total[:, -LANES:] + arrived[:, LANES:])[:, :8].T[:2]
    e = e_native.astype(F32) + e_core.astype(F32) + e_near.astype(F32)
    e = jnp.where(native, e, e_back.astype(F32))

    centered = rows_f32 - jnp.mean(rows_f32, axis=-1, keepdims=True)
    inv_scale = lax.rsqrt(jnp.mean(centered * centered, axis=-1, keepdims=True) + EPSILON)
    normalized = centered * inv_scale
    input_grad = cotangent.astype(F32) + inv_scale * (
        e - jnp.mean(e, axis=-1, keepdims=True) - normalized * jnp.mean(e * normalized, axis=-1, keepdims=True)
    )
    return (
        layer_out,
        input_grad,
        qkv_total[:, :-LANES],
        feed_total[:, : widths[0]],
        feed_total[:, widths[0] : widths[0] + widths[1]],
        feed_total[:, widths[0] + widths[1] : -LANES],
        attention_norm_grad,
        feedforward_norm_grad,
    )


def solution(mesh):
    dp, tensor = mesh.shape["dp"], mesh.shape["tensor"]
    fine = Mesh(mesh.devices.reshape(dp // 2, 2, 2, tensor // 2), AXES)
    data, split = ("pair", "core"), ("half", "m")
    tokens, weight, norm = P(AXES, None), P(data, split), P(None, data)
    return jax.shard_map(
        partial(on_device, fine),
        mesh=fine,
        in_specs=(tokens, weight, weight, weight, weight, norm, norm, tokens, P(data)),
        out_specs=(tokens, tokens, weight, weight, weight, weight, norm, norm),
        check_vma=False,
    )
```

```python
from functools import partial

import jax
import jax.numpy as jnp
from jax import lax
from jax.experimental import pallas as pl
from jax.experimental.pallas import tpu as pltpu
from jax.sharding import Mesh
from jax.sharding import PartitionSpec as P

HD = 64
ROT = 16
L = 2048
LANES = 128
EPSILON = 1e-05
MASKED = -1e30
AXES = ("pair", "core", "half", "m")
PIECES = 4
PIECE = L // PIECES
SEG_LANE = 64
DOCS = 5
LSE_LANE = SEG_LANE + DOCS
DELTA_LANE = 64
MIB = 1024 * 1024
F32 = jnp.float32
BF16 = jnp.bfloat16


def dot_nn(left, right):
    return lax.dot_general(left, right, (((1,), (0,)), ((), ())), preferred_element_type=F32)


def dot_nt(left, right):
    return lax.dot_general(left, right, (((1,), (1,)), ((), ())), preferred_element_type=F32)


def dot_tn(left, right):
    return lax.dot_general(left, right, (((0,), (0,)), ((), ())), preferred_element_type=F32)


def lanes_of(shape):
    return lax.broadcasted_iota(jnp.int32, shape, len(shape) - 1)


def rows_of(shape):
    return lax.broadcasted_iota(jnp.int32, shape, len(shape) - 2)


def normalize(x):
    rows = x.astype(F32)
    centered = rows - jnp.mean(rows, axis=-1, keepdims=True)
    return centered * lax.rsqrt(jnp.mean(centered * centered, axis=-1, keepdims=True) + EPSILON)


def split3(column):
    high = column.astype(BF16).astype(F32)
    rest = column - high
    middle = rest.astype(BF16).astype(F32)
    return high, middle, rest - middle


def with_lanes(base, first, columns):
    lane = lanes_of(base.shape)
    for offset, column in enumerate(columns):
        base = jnp.where(lane == first + offset, column, base)
    return base


def params(limit=60):
    return pltpu.CompilerParams(vmem_limit_bytes=limit * MIB)


def fenced(kernel, inputs, after):
    return lambda *refs: kernel(*refs[:inputs], *refs[inputs + after :])


ANYWHERE = pl.BlockSpec(memory_space=pl.ANY)


def whole(shape, **kw):
    return pl.BlockSpec(shape, lambda *_: (0,) * len(shape), **kw)


def once(shape):
    return whole(shape, pipeline_mode=pl.Buffered(1))


def cost(flops, nbytes, trans=0):
    return pl.CostEstimate(flops=int(flops) // 256, bytes_accessed=int(nbytes) // 256, transcendentals=int(trans) // 256)


def hops(pairs):
    near = [0] + [1 << b for b in range(pairs.bit_length() - 1)]
    far = sorted((j for j in range(pairs) if j not in near), key=lambda j: (j.bit_count(), j))
    return near, far


def block_places(info_ref, pairs, rows):
    near, far = hops(pairs)
    return pair_places(info_ref, near + far, rows)


def pair_places(info_ref, order, rows):
    core, pair = info_ref[1], info_ref[2]
    for j in order:
        base = (pair ^ j) * 2
        yield pl.multiple_of((base + core) * rows, rows), pl.multiple_of((base + 1 - core) * rows, rows)


def block_refs(refs, pairs):
    near, far = hops(pairs)
    refs = list(refs)
    for _ in near:
        both = refs.pop(0)
        yield both.at[0], both.at[1]
    for _ in far:
        yield refs.pop(0), refs.pop(0)


def block_shapes(pairs, rows, width):
    near, far = hops(pairs)
    return [(2, rows, width)] * len(near) + [(rows, width)] * (2 * len(far))


def assemble_first_kernel(pairs, rows, width, info_ref, *refs):
    weight_ref, gb_ref, small = refs[-3:]
    for offs, both in zip(pair_places(info_ref, range(pairs), rows), refs[:-3]):
        for off, part in zip(offs, (both.at[0], both.at[1])):
            weight_ref[pl.ds(off, rows), :] = part[:, :width]
            small[pl.ds(off, rows), :] = part[:, width:].astype(F32)
    gb_ref[...] = small[...].T[:8, :]


def assemble_first(info, parts, pairs, width):
    rows = parts[0].shape[1]
    feats = pairs * 2 * rows
    return pl.pallas_call(
        partial(assemble_first_kernel, pairs, rows, width),
        out_shape=(jax.ShapeDtypeStruct((feats, width), BF16), jax.ShapeDtypeStruct((8, feats), F32)),
        in_specs=[pl.BlockSpec(memory_space=pltpu.SMEM)] + [pl.BlockSpec(memory_space=pltpu.VMEM)] * len(parts),
        scratch_shapes=[pltpu.VMEM((feats, LANES), F32)],
        compiler_params=params(24),
        cost_estimate=cost(0, 4 * feats * width),
        name="assemble_qkv",
    )(info, *parts)


def assemble_second_kernel(pairs, rows, widths, info_ref, *refs):
    outs = refs[-len(widths) :]
    for offs, parts in zip(block_places(info_ref, pairs, rows), block_refs(refs[: -len(widths)], pairs)):
        for off, part in zip(offs, parts):
            start = 0
            for out, width in zip(outs, widths):
                out[pl.ds(off, rows), :] = part[:, start : start + width]
                start += width


def assemble_second(info, parts, pairs, widths):
    rows = parts[0].shape[1]
    feats = pairs * 2 * rows
    return pl.pallas_call(
        partial(assemble_second_kernel, pairs, rows, widths),
        out_shape=tuple(jax.ShapeDtypeStruct((feats, w), BF16) for w in widths),
        in_specs=[pl.BlockSpec(memory_space=pltpu.SMEM)] + [pl.BlockSpec(memory_space=pltpu.VMEM)] * len(parts),
        compiler_params=params(24),
        cost_estimate=cost(0, 4 * feats * sum(widths)),
        name="assemble_ffn",
    )(info, *parts)


def turn(values, cosine, sine_up, sine_down):
    return (
        values * cosine
        + pltpu.roll(values, ROT // 2, 1) * sine_up
        + pltpu.roll(values, LANES - ROT // 2, 1) * sine_down
    )


def project_kernel(heads, info_ref, xa_ref, xb_ref, w_ref, gb_ref, turn_ref, feature_ref, *refs):
    n_ref, q_ref, k_ref, v_ref = refs[-4:]
    first_piece = pl.program_id(0) < pl.num_programs(0) // 2
    normalized = normalize(jnp.where(first_piece, xa_ref[...], xb_ref[...]))
    n_ref[0] = normalized
    first = (normalized * gb_ref[0:1, :] + gb_ref[2:3, :]).astype(BF16)
    projected = dot_nn(first, w_ref[...])
    cosine, up, down = (turn_ref[:, n * LANES : (n + 1) * LANES] for n in range(3))
    query_feature, key_feature = (feature_ref[:, n * LANES : (n + 1) * LANES].astype(F32) for n in range(2))
    lane = lanes_of(cosine.shape)
    low = lane < HD
    value_feature = ((lane >= DELTA_LANE) & (lane < DELTA_LANE + 3)).astype(F32)

    def part(offset):
        tile = projected[:, offset // LANES * LANES : offset // LANES * LANES + LANES]
        return pltpu.roll(tile, HD, 1) if offset % LANES else tile

    for h in range(heads):
        sl = slice(h * LANES, (h + 1) * LANES)
        base = h * 3 * HD
        query = turn(part(base), cosine, up, down) * HD ** (-0.5)
        key = turn(part(base + HD), cosine, up, down)
        q_ref[0, :, sl] = jnp.where(low, query, query_feature).astype(BF16)
        k_ref[0, :, sl] = jnp.where(low, key, key_feature).astype(BF16)
        v_ref[0, :, sl] = jnp.where(low, part(base + 2 * HD), value_feature).astype(BF16)


def project(r, info, xa, xb, weight, gb, tables, stacks, after=(), block=512):
    feats, width = weight.shape
    heads = width // (3 * HD)
    steps = PIECE // block
    shapes = [(PIECES, PIECE, feats)] + [(PIECES, PIECE, heads * LANES)] * 3
    kinds = [F32, BF16, BF16, BF16]
    piece = lambda i: r + 2 * (i // steps)
    table = lambda n: pl.BlockSpec((block, n * LANES), lambda i, info: ((info[0] ^ piece(i)) * steps + i % steps, 0))
    inputs = [info, xa, xb, weight, gb, *tables]
    return pl.pallas_call(
        partial(project_kernel, heads),
        grid_spec=pltpu.PrefetchScalarGridSpec(
            num_scalar_prefetch=1,
            grid=(2 * steps,),
            in_specs=[
                pl.BlockSpec((block, feats), lambda i, info: (jnp.minimum(i, steps - 1), 0)),
                pl.BlockSpec((block, feats), lambda i, info: (jnp.maximum(i - steps, 0), 0)),
                once((feats, width)),
                once((8, feats)),
                table(3),
                table(2),
            ]
            + [ANYWHERE] * (len(stacks) + len(after)),
            out_specs=[pl.BlockSpec((1, block, s[2]), lambda i, info: (piece(i), i % steps, 0)) for s in shapes],
        ),
        out_shape=[jax.ShapeDtypeStruct(s, kind) for s, kind in zip(shapes, kinds)],
        input_output_aliases={len(inputs) + n: n for n in range(len(stacks))},
        compiler_params=params(36),
        cost_estimate=cost(4 * PIECE * feats * width, 2 * (feats * width + 12 * PIECE * feats)),
        name=f"project_{r}",
    )(*inputs, *stacks, *after)


def attend_kernel(heads, info_ref, q_ref, k_ref, v_ref, o_ref, qb_ref):
    me = info_ref[0]
    causal = lanes_of((PIECE, PIECE)) <= rows_of((PIECE, PIECE))
    low = lanes_of((PIECE, LANES)) < HD
    at = [pl.multiple_of((me ^ p) * PIECE, PIECE) for p in range(PIECES)]
    for i in range(PIECES):
        rows = pl.ds(at[i], PIECE)
        outs = []
        for h in range(heads):
            sl = slice(h * LANES, (h + 1) * LANES)
            query = q_ref[rows, sl]
            scores = [dot_nt(query, k_ref[pl.ds(at[j], PIECE), sl]) for j in range(i + 1)]
            scores[-1] = jnp.where(causal, scores[-1], MASKED)
            top = jnp.max(scores[0], axis=-1, keepdims=True)
            for s in scores[1:]:
                top = jnp.maximum(top, jnp.max(s, axis=-1, keepdims=True))
            out = total = None
            for j, s in enumerate(scores):
                weight = jnp.exp(s - top)
                part = jnp.sum(weight, axis=-1, keepdims=True)
                term = dot_nn(weight.astype(BF16), v_ref[pl.ds(at[j], PIECE), sl])
                total = part if total is None else total + part
                out = term if out is None else out + term
            outs.append(out * (1.0 / total))
            log_total = split3(top + jnp.log(total))
            qb_ref[rows, sl] = with_lanes(query.astype(F32), LSE_LANE, [-c for c in log_total]).astype(BF16)
        for h in range(0, heads, 2):
            o_ref[rows, h * HD : h * HD + LANES] = jnp.where(low, outs[h], pltpu.roll(outs[h + 1], HD, 1))


def attend(info, queries, keys, values, group, heads, after=()):
    full = queries.shape[2]
    width = heads * LANES
    own = pl.BlockSpec((L, width), lambda i, info: (0, group))
    return pl.pallas_call(
        fenced(partial(attend_kernel, heads), 4, len(after)),
        grid_spec=pltpu.PrefetchScalarGridSpec(
            num_scalar_prefetch=1,
            grid=(1,),
            in_specs=[own] * 3 + [ANYWHERE] * len(after),
            out_specs=[whole((L, heads * HD)), whole((L, width))],
        ),
        out_shape=[jax.ShapeDtypeStruct((L, heads * HD), F32), jax.ShapeDtypeStruct((L, width), BF16)],
        compiler_params=params(44),
        cost_estimate=cost(heads * L * L * LANES * 4, 5 * L * width, heads * L * L // 2),
        name=f"attention_forward_{group}",
    )(info, *(a.reshape(L, full) for a in (queries, keys, values)), *after)


def gelu_parts(h):
    bell = jnp.exp2(h * h * (-0.5 * 1.4426950408889634))
    t = pl.reciprocal(1.0 + (0.3275911 * 0.5**0.5) * jnp.abs(h))
    poly = t * (
        0.127414796 + t * (-0.142248368 + t * (0.7107068705 + t * (-0.7265760135 + t * 0.5307027145)))
    )
    tail = poly * bell
    return jnp.where(h < 0, tail, 1.0 - tail), bell * 0.3989422804014327


def norm_columns(sums_ref):
    wide = jnp.concatenate([sums_ref[...], jnp.zeros((LANES - 8, sums_ref.shape[1]), F32)], axis=0)
    return wide.T


def write_parts(info_ref, total, small, refs):
    width, rows = total.shape[1], refs[0].shape[1]
    for offs, both in zip(pair_places(info_ref, range(len(refs)), rows), refs):
        for n, off in enumerate(offs):
            both[n, :, :width] = total[pl.ds(off, rows), :].astype(BF16)
            both[n, :, width:] = small[pl.ds(off, rows), :].astype(BF16)


def feed_kernel(groups, parts, n_ref, *refs):
    o_refs, refs = refs[:groups], refs[groups:]
    (wd_ref, we_ref, ws_ref, gb_ref), refs = refs[:4], refs[4:]
    br_refs, (activated_ref, slope_ref, b_now) = refs[:PIECES], refs[PIECES:]
    step = pl.program_id(0)
    rows = PIECE // parts
    for n in range(parts):
        sl = slice(n * rows, (n + 1) * rows)
        second = (n_ref[sl, :] * gb_ref[1:2, :] + gb_ref[3:4, :]).astype(BF16)
        hidden = dot_nn(second, we_ref[...])
        cdf, density = gelu_parts(hidden)
        activated = (hidden * cdf).astype(BF16)
        activated_ref[sl, :] = activated
        slope_ref[sl, :] = cdf + hidden * density
        attended = jnp.concatenate([o[sl, :] for o in o_refs], axis=1).astype(BF16)
        b_now[sl, :] = (dot_nt(attended, wd_ref[...]) + dot_nt(activated, ws_ref[...])).astype(BF16)

    for r in range(PIECES):

        @pl.when(step == r)
        def _():
            br_refs[r][...] = b_now[...]


def feed(normalized, outs, wd, we, ws, gb, after=(), parts=1):
    feats, hidden = we.shape
    by_step = lambda i: (i, 0)
    inputs = [normalized.reshape(L, feats), *outs, wd, we, ws, gb]
    return pl.pallas_call(
        fenced(partial(feed_kernel, len(outs), parts), len(inputs), len(after)),
        grid=(PIECES,),
        in_specs=[pl.BlockSpec((PIECE, feats), by_step)]
        + [pl.BlockSpec((PIECE, o.shape[1]), by_step) for o in outs]
        + [once(w.shape) for w in (wd, we, ws, gb)]
        + [ANYWHERE] * len(after),
        out_specs=[
            *[once((PIECE, feats))] * PIECES,
            pl.BlockSpec((PIECE, hidden), by_step),
            pl.BlockSpec((PIECE, hidden), by_step),
        ],
        out_shape=[jax.ShapeDtypeStruct((PIECE, feats), BF16)] * PIECES
        + [jax.ShapeDtypeStruct((L, hidden), BF16), jax.ShapeDtypeStruct((L, hidden), F32)],
        scratch_shapes=[pltpu.VMEM((PIECE, feats), BF16)],
        compiler_params=params(44),
        cost_estimate=cost(4 * L * feats * hidden, 16 * L * feats),
        name="feed_forward",
    )(*inputs, *after)


def feed_back_kernel(heads, group, n_ref, activated_ref, slope_ref, *refs):
    groups = heads // group
    g_refs, refs = refs[:PIECES], refs[PIECES:]
    o_refs, refs = refs[:groups], refs[groups:]
    (wd_ref, we_ref, ws_ref, gb_ref, sg_ref), refs = refs[:5], refs[5:]
    doa_refs, refs = refs[:groups], refs[groups:]
    grads_ref, g_now, gd, ge, gs, sums = refs
    step, last = pl.program_id(0), pl.num_programs(0) - 1

    @pl.when(step == 0)
    def _():
        for total in (gd, ge, gs, sums):
            total[...] = jnp.zeros_like(total)

    for r in range(PIECES):

        @pl.when(step == r)
        def _():
            g_now[...] = g_refs[r][...]

    g = g_now[...]
    hidden_grad = (dot_nn(g, ws_ref[...]) * slope_ref[...]).astype(BF16)
    normalized = n_ref[...]
    second = (normalized * gb_ref[1:2, :] + gb_ref[3:4, :]).astype(BF16)
    out = jnp.concatenate([o[...] for o in o_refs], axis=1)
    gs[...] += dot_tn(g, activated_ref[...])
    gd[...] += dot_tn(g, out.astype(BF16))
    ge[...] += dot_tn(second, hidden_grad)
    second_grad = dot_nt(hidden_grad, we_ref[...])
    sg_ref[...] = second_grad * gb_ref[1:2, :]
    sums[0:1, :] += jnp.sum(second_grad * normalized, axis=0, keepdims=True)
    sums[1:2, :] += jnp.sum(second_grad, axis=0, keepdims=True)
    attended_grad = dot_nn(g, wd_ref[...]).astype(BF16).astype(F32)
    product = attended_grad * out
    lane = lanes_of((PIECE, LANES))
    for h in range(heads):
        tile = slice(h // 2 * LANES, (h // 2 + 1) * LANES)
        mine = (lane < HD) if h % 2 == 0 else (lane >= HD)
        delta = split3(jnp.sum(jnp.where(mine, product[:, tile], 0.0), axis=-1, keepdims=True))
        grad = attended_grad[:, tile]
        if h % 2:
            grad = pltpu.roll(grad, HD, 1)
        grad = jnp.where(lane < HD, grad, 0.0)
        start = h % group * LANES
        doa_refs[h // group][:, start : start + LANES] = with_lanes(grad, DELTA_LANE, [-c for c in delta]).astype(BF16)

    @pl.when(step == last)
    def _():
        start = 0
        for total in (gd, ge, gs):
            grads_ref[:, start : start + total.shape[1]] = total[...].astype(BF16)
            start += total.shape[1]
        grads_ref[:, start:] = norm_columns(sums).astype(BF16)


def feed_back(normalized, activated, slope, g_parts, outs, wd, we, ws, gb, after=()):
    feats, hidden = we.shape
    heads = wd.shape[1] // HD
    group = heads // len(outs)
    width = wd.shape[1] + 2 * hidden + LANES
    by_step = lambda i: (i, 0)
    step = lambda w: pl.BlockSpec((PIECE, w), by_step)
    inputs = [normalized.reshape(L, feats), activated, slope, *g_parts, *outs, wd, we, ws, gb]
    return pl.pallas_call(
        fenced(partial(feed_back_kernel, heads, group), len(inputs), len(after)),
        grid=(PIECES,),
        in_specs=[step(feats), step(hidden), step(hidden)]
        + [once((PIECE, feats))] * PIECES
        + [step(group * HD)] * len(outs)
        + [once(w.shape) for w in (wd, we, ws, gb)]
        + [ANYWHERE] * len(after),
        out_specs=[step(feats)] + [step(group * LANES)] * len(outs) + [once((feats, width))],
        out_shape=[jax.ShapeDtypeStruct((L, feats), F32)]
        + [jax.ShapeDtypeStruct((L, group * LANES), BF16)] * len(outs)
        + [jax.ShapeDtypeStruct((feats, width), BF16)],
        scratch_shapes=[
            pltpu.VMEM((PIECE, feats), BF16),
            pltpu.VMEM(wd.shape, F32),
            pltpu.VMEM(we.shape, F32),
            pltpu.VMEM(ws.shape, F32),
            pltpu.VMEM((8, feats), F32),
        ],
        compiler_params=params(),
        cost_estimate=cost(8 * L * feats * hidden, 20 * L * feats),
        name="feed_back",
    )(*inputs, *after)


def block_back(query, grad, key, value, causal):
    scores = dot_nt(key, query)
    if causal is not None:
        scores = jnp.where(causal, scores, MASKED)
    probs = jnp.exp(scores)
    score_grad = (probs * dot_nt(value, grad)).astype(BF16)
    return dot_tn(score_grad, key), dot_nn(score_grad, query), dot_nn(probs.astype(BF16), grad)


def triangle_back(load, base, sums, h, causal):
    q0, g0, k0, v0 = load(base)
    q1, g1, k1, v1 = load(base + 1)
    low = block_back(q0, g0, k0, v0, causal)
    side = block_back(q1, g1, k0, v0, None)
    high = block_back(q1, g1, k1, v1, causal)
    dq, dk, dv = sums
    dq[h, base] += low[0]
    dq[h, base + 1] += side[0] + high[0]
    for d, n in ((dk, 1), (dv, 2)):
        d[h, base] += low[n] + side[n]
        d[h, base + 1] += high[n]


def finish_back(pg_ref, tables_ref, table_row, sums, base, near, heads):
    low = lanes_of((PIECE, LANES)) < HD
    dq, dk, dv = sums
    for n in range(2):
        rows = pl.ds(pl.multiple_of(table_row + n * PIECE, PIECE), PIECE)
        cosine = tables_ref[rows, :LANES]
        up, down = -tables_ref[rows, LANES : 2 * LANES], -tables_ref[rows, 2 * LANES :]
        for h in range(0, heads, 2):
            start = h // 2 * 3 * LANES
            q0, q1 = (turn(dq[h + x, base + n] * HD ** (-0.5), cosine, up, down) for x in (0, 1))
            k0, k1 = (turn(dk[h + x, base + n], cosine, up, down) for x in (0, 1))
            v0, v1 = dv[h, base + n], dv[h + 1, base + n]
            for tile, (left, right) in enumerate(((q0, k0), (v0, q1), (k1, v1))):
                pg_ref[near ^ n, :, start + tile * LANES : start + (tile + 1) * LANES] = jnp.where(
                    low, left, pltpu.roll(right, HD, 1)
                ).astype(BF16)


def attend_back_first_kernel(info_ref, q_ref, do_ref, k_ref, v_ref, tables_ref, pg_ref, *refs):
    rests, sums = refs[:3], refs[3:]
    dq, dk, dv = sums
    me, half = info_ref[0], info_ref[3]
    heads = q_ref.shape[1] // LANES
    causal = rows_of((PIECE, PIECE)) <= lanes_of((PIECE, PIECE))
    swapped, native = 2 * (1 - half), 2 * half
    zero = jnp.zeros((PIECE, LANES), F32)
    for h in range(heads):
        sl = slice(h * LANES, (h + 1) * LANES)

        def load(piece):
            rows = pl.ds(pl.multiple_of((me ^ piece) * PIECE, PIECE), PIECE)
            return q_ref[rows, sl], do_ref[rows, sl], k_ref[rows, sl], v_ref[rows, sl]

        pieces = [load(p) for p in range(PIECES)]
        terms = {
            (i, j): block_back(*pieces[i][:2], *pieces[j][2:], None) for j in (0, 1) for i in (2, 3)
        }
        for p in (0, 1):
            dq[h, p] = zero
            dq[h, p + 2] = terms[p + 2, 0][0] + terms[p + 2, 1][0]
            for d, n in ((dk, 1), (dv, 2)):
                d[h, p] = terms[2, p][n] + terms[3, p][n]
                d[h, p + 2] = zero
        triangle_back(load, swapped, sums, h, causal)
        for rest, d in zip(rests, sums):
            for n in range(2):
                rest[h, n] = d[h, native + n]
    finish_back(pg_ref, tables_ref, 0, sums, swapped, me % 2, heads)


def attend_back_second_kernel(info_ref, q_ref, do_ref, k_ref, v_ref, tables_ref, *refs):
    rests, pg_ref, sums = refs[:3], refs[3], refs[4:]
    near = info_ref[0] % 2
    heads = q_ref.shape[1] // LANES
    causal = rows_of((PIECE, PIECE)) <= lanes_of((PIECE, PIECE))
    for h in range(heads):
        sl = slice(h * LANES, (h + 1) * LANES)

        def load(piece):
            rows = pl.ds(pl.multiple_of((near ^ piece) * PIECE, PIECE), PIECE)
            return q_ref[rows, sl], do_ref[rows, sl], k_ref[rows, sl], v_ref[rows, sl]

        for rest, d in zip(rests, sums):
            for n in range(2):
                d[h, n] = rest[h, n]
        triangle_back(load, 0, sums, h, causal)
    finish_back(pg_ref, tables_ref, 0, sums, 0, near, heads)


def attend_back(info, queries, grads, keys, values, tables, group, rests=(), after=()):
    width, full = queries.shape[1], keys.shape[2]
    heads = width // LANES
    rest = (heads, 2, PIECE, LANES)
    pg = (2, PIECE, heads * 3 * HD)
    first = not rests
    rows = L if first else L // 2
    place = (lambda info: 0) if first else (lambda info: info[1] ^ info[3])
    own = pl.BlockSpec((rows, width), lambda s, info: (place(info), 0))
    shared = pl.BlockSpec((rows, width), lambda s, info: (place(info), group))
    table = pl.BlockSpec((L // 2, 3 * LANES), lambda s, info: (1 - info[3] if first else info[3], 0))
    inputs = [info, queries, grads, keys.reshape(L, full), values.reshape(L, full), tables, *rests]
    blocks = 7 if first else 3
    return pl.pallas_call(
        fenced(attend_back_first_kernel if first else attend_back_second_kernel, len(inputs), len(after)),
        grid_spec=pltpu.PrefetchScalarGridSpec(
            num_scalar_prefetch=1,
            grid=(1,),
            in_specs=[own, own, shared, shared, table] + [whole(rest)] * len(rests) + [ANYWHERE] * len(after),
            out_specs=[whole(pg)] + [whole(rest)] * (3 if first else 0),
            scratch_shapes=[pltpu.VMEM((heads, PIECES if first else 2, PIECE, LANES), F32)] * 3,
        ),
        out_shape=[jax.ShapeDtypeStruct(pg, BF16)] + [jax.ShapeDtypeStruct(rest, F32)] * (3 if first else 0),
        compiler_params=params(44),
        cost_estimate=cost(blocks * heads * PIECE * PIECE * LANES * 10, 12 * L * width, blocks * heads * PIECE * PIECE),
        name=f"attention_backward_{group}" + ("a" if first else "b"),
    )(*inputs, *after)


def project_back_kernel(pairs, groups, final, info_ref, *refs):
    pg_refs, refs = refs[:groups], refs[groups:]
    (n_ref, sg_ref, w_ref, gb_ref), refs = refs[:4], refs[4:]
    if final:
        (gq_in, sums_in, *e_refs), refs = refs[:4], refs[4:]
        *part_refs, gq, sums, small, e_now = refs
    else:
        *e_refs, gq, sums, e_now = refs
    step, last = pl.program_id(0), pl.num_programs(0) - 1

    @pl.when(step == 0)
    def _():
        gq[...] = gq_in[...] if final else jnp.zeros_like(gq)
        sums[...] = sums_in[...] if final else jnp.zeros_like(sums)

    normalized = n_ref[0]
    first = (normalized * gb_ref[0:1, :] + gb_ref[2:3, :]).astype(BF16)
    grad = jnp.concatenate([pg[0] for pg in pg_refs], axis=1)
    first_grad = dot_nt(grad, w_ref[...])
    gq[...] += dot_tn(first, grad)
    e_now[...] = (first_grad * gb_ref[0:1, :] + sg_ref[0]).astype(BF16)
    block = e_now.shape[0]
    per = PIECE // block
    place = pl.ds(pl.multiple_of(step % per * block, block), block)
    for n in range(2):

        @pl.when(step // per == n)
        def _():
            e_refs[n][place, :] = e_now[...]

    sums[0:1, :] += jnp.sum(first_grad * normalized, axis=0, keepdims=True)
    sums[1:2, :] += jnp.sum(first_grad, axis=0, keepdims=True)
    if final:

        @pl.when(step == last)
        def _():
            small[...] = norm_columns(sums)
            write_parts(info_ref, gq, small, part_refs)


def project_back(info, pgs, normalized, sg, weight, gb, pairs, so_far=(), after=(), block=PIECE):
    feats, width = weight.shape
    final = bool(so_far)
    swapped = 0 if final else 1
    sums = (8, feats)
    shapes = [(2, feats // (2 * pairs), width + LANES)] * pairs if final else []
    piece = (PIECE, feats)
    per = PIECE // block
    by_step = lambda i, info: (i // per, i % per, 0)
    relative = pl.BlockSpec(
        (1, block, feats), lambda i, info: (2 * (info[1] ^ info[3] ^ swapped) + i // per, i % per, 0)
    )
    inputs = [info, *pgs, normalized, sg.reshape(PIECES, PIECE, feats), weight, gb, *so_far]
    totals = [pltpu.VMEM(weight.shape, F32), pltpu.VMEM(sums, F32)]
    results = [(piece, BF16)] * 2 + ([(s, BF16) for s in shapes] if final else [(weight.shape, F32), (sums, F32)])
    return pl.pallas_call(
        fenced(partial(project_back_kernel, pairs, len(pgs), final), len(inputs), len(after)),
        grid_spec=pltpu.PrefetchScalarGridSpec(
            num_scalar_prefetch=1,
            grid=(2 * per,),
            in_specs=[pl.BlockSpec((1, block, pg.shape[2]), by_step) for pg in pgs]
            + [relative, relative]
            + [once(a.shape) for a in (weight, gb, *so_far)]
            + [ANYWHERE] * len(after),
            out_specs=[once(s) for s, _ in results],
            scratch_shapes=(totals + [pltpu.VMEM((feats, LANES), F32)] if final else [])
            + [pltpu.VMEM((block, feats), BF16)],
        ),
        out_shape=[jax.ShapeDtypeStruct(s, kind) for s, kind in results],
        compiler_params=params(44),
        cost_estimate=cost(2 * L * feats * width, 6 * L * feats),
        name="project_back_" + ("b" if final else "a"),
    )(*inputs, *after)


def build_tables(segments):
    places = jnp.arange(L, dtype=jnp.int32)
    starts = jnp.zeros_like(segments)
    for value in range(DOCS):
        starts = starts + jnp.where(segments > value, jnp.sum((segments == value).astype(jnp.int32)), 0)
    position = (places - starts).astype(F32)
    lane = jnp.arange(LANES, dtype=jnp.int32)
    inner = lane % HD
    half = ROT // 2
    frequency = 10000.0 ** (-((inner % half).astype(F32) * 2.0 / ROT))
    angles = position[:, None] * frequency[None, :]
    turned = (inner < ROT)[None, :]
    sine = jnp.sin(angles)
    cosine = jnp.where(turned, jnp.cos(angles), 1.0)
    up = jnp.where(turned & (inner >= half)[None, :], sine, 0.0)
    down = jnp.where((inner < half)[None, :], -sine, 0.0)
    feature = lane - SEG_LANE
    is_doc = ((feature >= 0) & (feature < DOCS))[None, :]
    same = segments[:, None] == feature[None, :]
    one = ((lane >= LSE_LANE) & (lane < LSE_LANE + 3))[None, :]
    query_feature = jnp.where(is_doc & ~same, MASKED, 0.0)
    key_feature = jnp.where((is_doc & same) | one, 1.0, 0.0)
    features = jnp.concatenate([query_feature, key_feature], axis=1).astype(BF16)
    return jnp.concatenate([cosine, up, down], axis=1), features


class Wires:
    def __init__(self, mesh):
        self.pairs = mesh.shape["pair"]
        self.sizes = [mesh.shape[a] for a in AXES]

    def send(self, array, target):
        _, cores, halves, ms = self.sizes

        def index(k, c, h, m):
            return ((k * cores + c) * halves + h) * ms + m

        moves = []
        for k in range(self.pairs):
            for c in range(cores):
                for h in range(halves):
                    for m in range(ms):
                        there = target(k, c, h, m)
                        if there is not None:
                            moves.append((index(k, c, h, m), index(*there)))
        return lax.ppermute(array, AXES, moves)

    def core(self, array):
        return self.send(array, lambda k, c, h, m: (k, 1 - c, h, m))

    def near(self, array, native):
        return self.send(array, lambda k, c, h, m: (k, c, h, 1 - m) if (c == h) == native else None)

    def core_from(self, array, native):
        return self.send(array, lambda k, c, h, m: (k, 1 - c, h, m) if (c == h) == native else None)

    def near_all(self, array):
        return self.send(array, lambda k, c, h, m: (k, c, h, 1 - m))

    def across(self, array):
        return self.send(array, lambda k, c, h, m: (k, c, 1 - h, 1 - m))

    def half(self, array):
        return self.send(array, lambda k, c, h, m: (k, c, 1 - h, m))

    def regroup(self, array):
        return self.send(array, lambda k, c, h, m: (k, 1 - c, 1 - h, m) if c != h else None)

    def plane(self, array, bit):
        return self.send(array, lambda k, c, h, m: (k ^ bit, c, h, m))

    def gather_near(self, both):
        return [both] + [self.plane(both, j) for j in hops(self.pairs)[0][1:]]

    def gather_far(self, parts):
        near, far = hops(self.pairs)
        a_parts = {j: part[0] for j, part in zip(near, parts)}
        b_parts = {j: part[1] for j, part in zip(near, parts)}
        result = list(parts)
        for j in far:
            low, high = j & -j, 1 << (j.bit_length() - 1)
            a_parts[j] = self.plane(a_parts[j ^ low], low)
            b_parts[j] = self.plane(b_parts[j ^ high], high)
            result += [a_parts[j], b_parts[j]]
        return result

    def gather_direct(self, both):
        return [both] + [self.plane(both, j) for j in range(1, self.pairs)]

    def scatter_direct(self, parts):
        return [self.plane(part, j) for j, part in enumerate(parts) if j]


def on_device(mesh, inputs, qkv_weight, dense_weight, expand_weight, shrink_weight, norm_gains, norm_biases, cotangent, segments):
    wires = Wires(mesh)
    pairs = wires.pairs
    pair, core, half, near = (lax.axis_index(a) for a in AXES)
    native = core == half
    me = 2 * core + near
    info = jnp.stack([me, core, pair, half]).astype(jnp.int32)

    def since(value, *done):
        return lax.optimization_barrier((value, done))[0]

    def at(values):
        return lax.optimization_barrier(values)

    def swap_weights(block, swapped):
        own = jnp.where(native, block, swapped)
        return jnp.stack([own, wires.core(jnp.where(native, swapped, block))])

    def swap_grads(both):
        other = wires.core(both[1])
        small = (both[0][:, -LANES:].astype(F32) + other[:, -LANES:].astype(F32)).astype(BF16)
        mine, sent = jnp.where(native, both[0], other), jnp.where(native, other, both[0])
        return [jnp.concatenate([a[:, :-LANES], small], axis=1) for a in (mine, sent)]

    def core_sum(parts):
        return parts[0].astype(F32) + wires.core(parts[1]).astype(F32)

    def since(value, *done):
        return lax.optimization_barrier((value, done))[0]

    def since(value, *done):
        return lax.optimization_barrier((value, done))[0]

    small = jnp.concatenate([norm_gains, norm_biases], axis=0).T
    first_block = jnp.concatenate([qkv_weight, jnp.pad(small, ((0, 0), (0, LANES - 4)))], axis=1)
    first_swapped = wires.half(first_block)
    other_segments = wires.core(since(segments, first_block))
    x_swapped = wires.regroup(since(inputs, other_segments))
    x_near = wires.near(since(inputs, other_segments), True)
    first_both = swap_weights(first_block, first_swapped)
    first_parts = wires.gather_direct(first_both)
    tables = build_tables(jnp.where(native, since(segments, first_both), other_segments))
    x_swapped, x_near, first_parts = since((x_swapped, x_near, first_parts), tables)
    x_mine = jnp.where(native, inputs, x_swapped)
    x_far = wires.near(x_swapped, False)
    qkv_full, gb = assemble_first(info, since(first_parts, x_mine), pairs, qkv_weight.shape[1])
    x_core = wires.core(x_mine)
    stacks = project(0, info, x_mine, x_core, qkv_full, gb, tables, ())

    stacks, x_near, x_far = at((stacks, x_near, x_far))
    second_a = jnp.concatenate([dense_weight, expand_weight], axis=1)
    x_beside = jnp.where(native, x_near, x_far)
    x_last = wires.core(x_beside)
    a_swapped = wires.half(since(second_a, x_beside))
    stacks = project(1, info, x_beside, x_last, qkv_full, gb, tables, stacks)
    stacks, a_swapped = at((stacks, a_swapped))
    normalized, queries, keys, values = stacks

    b_swapped = wires.half(since(shrink_weight, a_swapped))
    a_both = swap_weights(second_a, a_swapped)
    a_near = wires.gather_near(a_both)
    out_0, queries_0 = attend(info, queries, keys, values, 0, 2, after=(a_both,))
    out_0, a_near, b_swapped = at((out_0, a_near, b_swapped))
    b_both = swap_weights(shrink_weight, b_swapped)
    a_parts = wires.gather_far(a_near)
    b_near = wires.gather_near(b_both)
    g_swapped = wires.regroup(since(cotangent, b_swapped))
    g_near = wires.near(since(cotangent, b_swapped), True)
    out_1, queries_1 = attend(info, queries, keys, values, 1, 2, after=(out_0, b_both))
    out_1, a_parts, b_near = at((out_1, a_parts, b_near))
    b_parts = wires.gather_far(b_near)
    widths = (dense_weight.shape[1], expand_weight.shape[1], shrink_weight.shape[1])
    dense_full, expand_full = assemble_second(info, a_parts, pairs, widths[:2])
    dense_full, expand_full, b_parts = at((dense_full, expand_full, b_parts))
    (shrink_full,) = assemble_second(info, b_parts, pairs, widths[2:])
    shrink_full, g_swapped, g_near = at((shrink_full, g_swapped, g_near))
    g_far = wires.near(g_swapped, False)
    g_mine = jnp.where(native, cotangent, g_swapped)
    g_core = wires.core(g_mine)
    results = feed(normalized, (out_0, out_1), dense_full, expand_full, shrink_full, gb, after=(g_mine,))
    results, g_near, g_far, g_core = at((results, g_near, g_far, g_core))
    *branches, activated, slope = results
    passed_core = wires.core(branches[3])
    g_beside = jnp.where(native, g_near, g_far)
    g_parts = [g_mine, g_beside, g_core, wires.core(g_beside)]

    passed = (branches[1].astype(F32) + passed_core.astype(F32)).astype(BF16)
    branch_kept, branch_core = branches[0], wires.core(since(branches[2], passed_core))
    branch_far = wires.near(passed, False)
    branch_near = wires.near(passed, True)
    results = feed_back(
        normalized, activated, slope, g_parts, (out_0, out_1), dense_full, expand_full, shrink_full, gb, after=(passed,)
    )
    results, branch_far, branch_near, branch_kept, branch_core = at(
        (results, branch_far, branch_near, branch_kept, branch_core)
    )
    second_e, *grads, feed_grads = results

    turns = tables[0]
    feed_both = lax.psum_scatter(feed_grads, "pair", scatter_dimension=0, tiled=True)
    branch_sent = (
        branch_kept.astype(F32) + branch_core.astype(F32) + branch_far.astype(F32)
    ).astype(BF16)
    branch_back = wires.regroup(branch_sent)
    pg_0, *rests_0 = attend_back(info, queries_0, grads[0], keys, values, turns, 0, after=(branch_sent,))
    pg_0, rests_0 = at((pg_0, rests_0))
    pg_1, *rests_1 = attend_back(info, queries_1, grads[1], keys, values, turns, 1, after=(pg_0,))
    pg_1, rests_1, branch_back = at((pg_1, rests_1, branch_back))
    results = project_back(info, (pg_0, pg_1), normalized, second_e, qkv_full, gb, pairs)
    e_swapped, e_given, *so_far = at(results)

    passed_core = wires.core_from(e_given, True)
    e_passed = (e_given.astype(F32) + passed_core.astype(F32)).astype(BF16)
    e_core = wires.core_from(since(e_swapped, passed_core), True)
    e_far = wires.near(e_passed, False)
    (pg_0,) = attend_back(info, queries_0, grads[0], keys, values, turns, 0, rests_0, after=(e_passed, *so_far))
    pg_0, e_far, e_swapped, e_core, feed_both = at((pg_0, e_far, e_swapped, e_core, feed_both))
    feed_both = feed_both.reshape(2, qkv_weight.shape[0], -1)
    feed_both = jnp.where(core == 0, feed_both, feed_both[::-1])
    feed_mine, feed_sent = swap_grads(feed_both)
    feed_arrived = wires.half(feed_sent)
    (pg_1,) = attend_back(info, queries_1, grads[1], keys, values, turns, 1, rests_1, after=(pg_0, feed_sent))
    results = project_back(info, (pg_0, pg_1), normalized, second_e, qkv_full, gb, pairs, so_far)
    results, feed_arrived, e_far, e_swapped, e_core = at((results, feed_arrived, e_far, e_swapped, e_core))
    e_sent = (e_swapped.astype(F32) + e_core.astype(F32) + e_far.astype(F32)).astype(BF16)
    e_native, e_given, *qkv_grads = results
    passed_core = wires.core_from(e_given, False)
    e_back = wires.regroup(e_sent)
    qkv_near = wires.scatter_direct(qkv_grads)
    e_passed = (e_given.astype(F32) + passed_core.astype(F32)).astype(BF16)
    e_near = wires.near(e_passed, True)
    e_core = wires.core_from(since(e_native, passed_core), False)
    qkv_near, e_back = since((qkv_near, e_back), e_passed)
    qkv_both = sum(part.astype(F32) for part in (qkv_grads[0], *qkv_near)).astype(BF16)
    qkv_mine, qkv_sent = swap_grads(since(qkv_both, e_back))
    smalls = jnp.concatenate([qkv_mine[:, -LANES:], feed_mine[:, -LANES:]], axis=1)
    qkv_sent, smalls = since((qkv_sent, smalls), e_near)
    small_near, small_across = wires.near_all(smalls), wires.across(smalls)
    qkv_arrived = wires.half(qkv_sent)
    rows_f32 = inputs.astype(F32)
    branch = branch_kept.astype(F32) + branch_core.astype(F32) + branch_near.astype(F32)
    layer_out = (rows_f32 + jnp.where(native, branch, branch_back.astype(F32))).astype(BF16)
    feed_total = feed_mine.astype(F32) + feed_arrived.astype(F32)
    qkv_total = qkv_mine.astype(F32) + qkv_arrived.astype(F32)
    arrived = small_near.astype(F32) + small_across.astype(F32)
    attention_norm_grad = (qkv_total[:, -LANES:] + arrived[:, :LANES])[:, :8].T[:2]
    feedforward_norm_grad = (feed_total[:, -LANES:] + arrived[:, LANES:])[:, :8].T[:2]
    e = e_native.astype(F32) + e_core.astype(F32) + e_near.astype(F32)
    e = jnp.where(native, e, e_back.astype(F32))

    centered = rows_f32 - jnp.mean(rows_f32, axis=-1, keepdims=True)
    inv_scale = lax.rsqrt(jnp.mean(centered * centered, axis=-1, keepdims=True) + EPSILON)
    normalized = centered * inv_scale
    input_grad = cotangent.astype(F32) + inv_scale * (
        e - jnp.mean(e, axis=-1, keepdims=True) - normalized * jnp.mean(e * normalized, axis=-1, keepdims=True)
    )
    return (
        layer_out,
        input_grad,
        qkv_total[:, :-LANES],
        feed_total[:, : widths[0]],
        feed_total[:, widths[0] : widths[0] + widths[1]],
        feed_total[:, widths[0] + widths[1] : -LANES],
        attention_norm_grad,
        feedforward_norm_grad,
    )


def solution(mesh):
    dp, tensor = mesh.shape["dp"], mesh.shape["tensor"]
    fine = Mesh(mesh.devices.reshape(dp // 2, 2, 2, tensor // 2), AXES)
    data, split = ("pair", "core"), ("half", "m")
    tokens, weight, norm = P(AXES, None), P(data, split), P(None, data)
    return jax.shard_map(
        partial(on_device, fine),
        mesh=fine,
        in_specs=(tokens, weight, weight, weight, weight, norm, norm, tokens, P(data)),
        out_specs=(tokens, tokens, weight, weight, weight, weight, norm, norm),
        check_vma=False,
    )
```
